128 devices in a mesh: pipe: 8 (over z_lo, x), dp: 16 (over y, z_hi, core).
Axes of the slice: x: 4, y: 4, z: 4 (z_hi: 2, z_lo: 2; z = z_hi * 2 + z_lo), core: 2. Of those that a mesh axis runs over, the one named last changes fastest.
Arguments:
- section_inputs: bfloat16 [8, 3, 2048, 3072], P('pipe', None, 'dp'), may hold values from -6 to 6
- weights: bfloat16 [8, 3072, 3072], P('pipe'), may hold values from -0.109375 to 0.109375
- norm_gains: float32 [8, 3072], P('pipe'), may hold values from 0.1 to 1.9
- upstream: bfloat16 [3, 2048, 3072], P(None, 'dp'), may hold values from -4 to 4
- edge_list: int32 [3, 16, 384, 2], P(None, 'dp'), may hold values from 0 to 127
- time_steps: int32 [3, 16], P(None, 'dp'), may hold values from 0 to 999
Outputs:
- section_grads: bfloat16 [8, 3, 2048, 3072], P('pipe', None, 'dp')
- weight_grads: bfloat16 [8, 3072, 3072], P('pipe', 'dp')
The draws below stay inside these ranges and needn't reach their ends.
Inputs may be any that keep to these rules, and one draw needn't show every extreme that they name: `edge_list`: every entry is a node number of the micro-batch's graph on that replica, from 0 to 127.
All inputs are finite; a program needn't handle non-finite values.
Results may differ from the reference program's by a relative error of at most 0.022.
Values may be sent and summed in bfloat16 or wider, within the bound.
No kernel may reach another device: no remote copies, remote signals or barrier semaphores. Data moves between devices by JAX's collectives and lax.ppermute only.
A program may use at most 192 MiB of HBM per device.

```python
import math
import jax
import jax.numpy as jnp
from jax import lax

D = 3072
TOK = 128
MB = 3
TSTEPS = 1000
EDGES = 384
SECTIONS = 8
REPLICAS = 16
TOKENS = 2048


def plant(entries, rng, low, largest):
    place = [jax.random.randint(jax.random.fold_in(rng, axis), (), 0, length) for axis, length in enumerate(entries.shape)]
    widest = entries.shape.index(max(entries.shape))
    beside = place[:widest] + [(place[widest] + 1) % entries.shape[widest]] + place[widest + 1:]
    return entries.at[tuple(place)].set(low).at[tuple(beside)].set(largest)


def spiked(result, rng, source, target, parts, factor):
    def block_of(position):
        return (jnp.arange(result.shape[position]) // (result.shape[position] // parts)).reshape((-1,) + (1,) * (result.ndim - 1 - position))

    near = jax.random.permutation(rng, parts)[block_of(target)]
    second = (block_of(target) + parts // 2) % parts
    return jnp.where((block_of(source) == near) | (block_of(source) == second), factor * result, result)


def block_levels(stream_key, dims, pieces, least, high):
    def one(dim, blocks):
        draws = jax.random.uniform(jax.random.fold_in(jax.random.fold_in(stream_key, 6), dim), (blocks,), jnp.float32, least / len(pieces), high / len(pieces))
        return jnp.repeat(jnp.exp(draws), dims[dim] // blocks).reshape((-1,) + (1,) * (len(dims) - dim - 1))

    level = one(*pieces[0])
    for cut in pieces[1:]:
        level = level * one(*cut)
    return level


def normal_values(key, shape, scale, limit, shards=(), kind=jnp.bfloat16):
    array = jax.random.normal(key, shape, jnp.float32) * scale
    if len(shards) > 0:
        array = block_levels(key, shape, shards, -0.22, 0.18) * array
    return jnp.clip(array, min=-limit, max=limit).astype(kind)


def heavy_noise(stream_key, extent, deviation, limit, pieces, heavy, kind=jnp.bfloat16):
    values = deviation * jax.random.normal(stream_key, extent, jnp.float32)
    if pieces:
        values = values * block_levels(stream_key, extent, pieces, -0.22, 0.18)
    return jnp.clip(spiked(values, jax.random.fold_in(stream_key, 3), *heavy), -limit, limit).astype(kind)


def setup_inputs(seed: int = 0) -> dict:
    splits = jax.random.split(jax.random.key(seed), 7)
    return {
        "section_inputs": heavy_noise(splits[0], (SECTIONS, MB, TOKENS, D), 1.0, 6.0, ((0, 8), (2, 16)), (2, 3, 16, 2.0)),
        "weights": normal_values(splits[1], (SECTIONS, D, D), D ** -0.5, 0.109375, ((0, 8),)),
        "norm_gains": jnp.clip(1.0 + 0.18 * jax.random.normal(splits[2], (SECTIONS, D), jnp.float32), 0.1, 1.9),
        "upstream": normal_values(splits[3], (MB, TOKENS, D), 0.5, 4.0, ((1, 16),)),
        "edge_list": plant(jax.random.randint(splits[4], (MB, REPLICAS, EDGES, 2), 0, TOK), jax.random.fold_in(splits[4], 1), 0, TOK - 1).astype(jnp.int32),
        "time_steps": plant(jax.random.randint(splits[5], (MB, REPLICAS), 0, TSTEPS), jax.random.fold_in(splits[5], 1), 0, TSTEPS - 1).astype(jnp.int32),
    }


def diffusion(edge_list, node_count):
    node_ids = jnp.arange(node_count, dtype=jnp.int32)
    source = (edge_list[:, 0:1] == node_ids[None, :]).astype(jnp.float32)
    target = (edge_list[:, 1:2] == node_ids[None, :]).astype(jnp.float32)
    adjacency = lax.dot_general(source, target, (((0,), (0,)), ((), ())), precision=lax.Precision.HIGHEST)
    adjacency = adjacency + adjacency.T + jnp.eye(node_count, dtype=jnp.float32)
    degree = lax.optimization_barrier(jnp.sum(adjacency, axis=-1, keepdims=True))
    return (adjacency / degree).astype(jnp.bfloat16)

def timestep_gate(time_steps, width):
    frequency = jnp.exp(-math.log(10000.0) * jnp.arange(width).astype(jnp.float32) / width)
    return 1.0 + 0.5 * jnp.sin(time_steps.astype(jnp.float32)[..., None] * frequency)

def recompute(hidden, mixing, norm_gain, weight):
    wide = hidden.astype(jnp.float32)
    inv_rms = lax.rsqrt(lax.optimization_barrier(jnp.mean(wide * wide, axis=-1, keepdims=True)) + 1e-06)
    normed = (wide * inv_rms * norm_gain).astype(jnp.bfloat16)
    mixed = jnp.dot(mixing, normed, preferred_element_type=jnp.float32).astype(jnp.bfloat16)
    pre_act = jnp.dot(mixed, weight, preferred_element_type=jnp.float32)
    return (mixed, pre_act, inv_rms)

def backprop(hidden, grad_out, mixing, norm_gain, weight, gate_row, pre_act, inv_rms):
    logistic = jax.nn.sigmoid(pre_act)
    slope = logistic * (1.0 + pre_act * (1.0 - logistic))
    grad_act = (grad_out.astype(jnp.float32) * gate_row * slope).astype(jnp.bfloat16)
    grad_mix = lax.dot_general(grad_act, weight, (((1,), (1,)), ((), ())), preferred_element_type=jnp.float32).astype(jnp.bfloat16)
    grad_norm = lax.dot_general(mixing, grad_mix, (((0,), (0,)), ((), ())), preferred_element_type=jnp.float32)
    wide = hidden.astype(jnp.float32)
    scaled = grad_norm * norm_gain
    inner = lax.optimization_barrier(jnp.mean(scaled * wide, axis=-1, keepdims=True))
    grad_in = grad_out.astype(jnp.float32) + inv_rms * scaled - wide * inv_rms * inv_rms * inv_rms * inner
    return (grad_in.astype(jnp.bfloat16), grad_act)

def reference(section_inputs, weights, norm_gains, upstream, edge_list, time_steps):
    flat_edges = edge_list.reshape(MB * REPLICAS, EDGES, 2)
    mixing_all = lax.map(lambda edges_one: diffusion(edges_one, TOK), flat_edges)
    gates_all = timestep_gate(time_steps.reshape(MB * REPLICAS), D)
    grad_out = upstream.reshape(MB * REPLICAS, TOK, D)
    section_list = []
    weight_list = []
    for section_idx in reversed(range(SECTIONS)):
        weight = weights[section_idx]
        norm_gain = norm_gains[section_idx]
        hidden_all = section_inputs[section_idx].reshape(MB * REPLICAS, TOK, D)

        def single(items):
            hidden, grad_one, mixing, gate_row = items
            mixed, pre_act, inv_rms = recompute(hidden, mixing, norm_gain, weight)
            grad_in, grad_act = backprop(hidden, grad_one, mixing, norm_gain, weight, gate_row, pre_act, inv_rms)
            return (grad_in, mixed, grad_act)
        grad_in, mixed, grad_act = lax.map(single, (hidden_all, grad_out, mixing_all, gates_all))
        mixed_rep = jnp.transpose(mixed.reshape(MB, REPLICAS, TOK, D), (1, 0, 2, 3)).reshape(REPLICAS, MB * TOK, D)
        act_rep = jnp.transpose(grad_act.reshape(MB, REPLICAS, TOK, D), (1, 0, 2, 3)).reshape(REPLICAS, MB * TOK, D)

        def add_replica(totals, pair):
            partial_value = lax.dot_general(pair[0], pair[1], (((0,), (0,)), ((), ())), preferred_element_type=jnp.float32)
            rounded = lax.optimization_barrier(partial_value.astype(jnp.bfloat16))
            return (totals + rounded.astype(jnp.float32), None)
        totals, unused = lax.scan(add_replica, jnp.zeros((D, D), jnp.float32), (mixed_rep, act_rep))
        section_list.insert(0, grad_in.reshape(MB, TOKENS, D))
        weight_list.insert(0, totals.astype(jnp.bfloat16))
        grad_out = grad_in
    return (jnp.stack(section_list), jnp.stack(weight_list))
```

```python
import functools
import math

import jax
import jax.numpy as jnp
from jax import lax
from jax.experimental import pallas as pl
from jax.experimental.pallas import tpu as pltpu
from jax.sharding import PartitionSpec as P

VMEM_LIMIT = 36 * 1024 * 1024
NT = (((1,), (1,)), ((), ()))


def timestep_gate(time_steps, width):
    frequency = jnp.exp(-math.log(10000.0) * jnp.arange(width).astype(jnp.float32) / width)
    return 1.0 + 0.5 * jnp.sin(time_steps.astype(jnp.float32)[..., None] * frequency)


def recompute_kernel(hidden_ref, edge_ref, gate_ref, gain_ref, w_ref,
                     mixed_ref, slope_ref, mixt_ref, inv_ref, grads_ref, act_ref, mixed_s):
    del grads_ref, act_ref
    micros, nodes, width = hidden_ref.shape

    @pl.when(pl.program_id(0) == 0)
    def _():
        edges = edge_ref.shape[2]
        ids = lax.broadcasted_iota(jnp.int32, (nodes, edges), 0)
        rows = lax.broadcasted_iota(jnp.int32, (nodes, nodes), 0)
        cols = lax.broadcasted_iota(jnp.int32, (nodes, nodes), 1)
        eye = jnp.where(rows == cols, 1.0, 0.0)
        for k in range(micros):
            src = jnp.where(edge_ref[k, 0:1, :] == ids, 1.0, 0.0).astype(jnp.bfloat16)
            tgt = jnp.where(edge_ref[k, 1:2, :] == ids, 1.0, 0.0).astype(jnp.bfloat16)
            adj = lax.dot_general(src, tgt, NT, preferred_element_type=jnp.float32)
            adj = adj + lax.dot_general(tgt, src, NT, preferred_element_type=jnp.float32) + eye
            mix = adj / jnp.sum(adj, axis=-1, keepdims=True)
            mixt_ref[k] = mix.T.astype(jnp.bfloat16)
            wide = hidden_ref[k].astype(jnp.float32)
            inv = lax.rsqrt(jnp.mean(wide * wide, axis=-1, keepdims=True) + 1e-06)
            inv_ref[k] = jnp.broadcast_to(inv, (nodes, 128))
            normed = (wide * inv * gain_ref[...]).astype(jnp.bfloat16)
            mixed = jnp.dot(mix.astype(jnp.bfloat16), normed, preferred_element_type=jnp.float32)
            mixed = mixed.astype(jnp.bfloat16)
            mixed_s[pl.ds(k * nodes, nodes), :] = mixed
            mixed_ref[k] = mixed

    u = jnp.dot(mixed_s[...], w_ref[...], preferred_element_type=jnp.float32)
    logistic = jax.nn.sigmoid(u)
    slope = logistic * (1.0 + u * (1.0 - logistic))
    for k in range(micros):
        slope_ref[k] = slope[k * nodes:(k + 1) * nodes, :] * gate_ref[pl.ds(k, 1), :]


def recompute(hidden, edges_t, gates, gain, weight):
    micros, nodes, width = hidden.shape
    block = 512
    whole3 = lambda j: (0, 0, 0)
    return pl.pallas_call(
        recompute_kernel,
        grid=(width // block,),
        in_specs=[
            pl.BlockSpec((micros, nodes, width), whole3),
            pl.BlockSpec(edges_t.shape, whole3),
            pl.BlockSpec((micros, block), lambda j: (0, j)),
            pl.BlockSpec((1, width), lambda j: (0, 0)),
            pl.BlockSpec((width, block), lambda j: (0, j)),
        ],
        out_specs=[
            pl.BlockSpec((micros, nodes, width), whole3),
            pl.BlockSpec((micros, nodes, block), lambda j: (0, 0, j)),
            pl.BlockSpec((micros, nodes, nodes), whole3),
            pl.BlockSpec((micros, nodes, 128), whole3),
            pl.BlockSpec(memory_space=pl.ANY),
            pl.BlockSpec(memory_space=pl.ANY),
        ],
        out_shape=[
            jax.ShapeDtypeStruct((micros, nodes, width), jnp.bfloat16),
            jax.ShapeDtypeStruct((micros, nodes, width), jnp.float32),
            jax.ShapeDtypeStruct((micros, nodes, nodes), jnp.bfloat16),
            jax.ShapeDtypeStruct((micros, nodes, 128), jnp.float32),
            jax.ShapeDtypeStruct((micros, nodes, width), jnp.bfloat16),
            jax.ShapeDtypeStruct((micros, nodes, width), jnp.bfloat16),
        ],
        scratch_shapes=[pltpu.VMEM((micros * nodes, width), jnp.bfloat16)],
        compiler_params=pltpu.CompilerParams(vmem_limit_bytes=VMEM_LIMIT),
        cost_estimate=pl.CostEstimate(
            flops=2 * micros * nodes * width * width,
            bytes_accessed=2 * width * width + 10 * micros * nodes * width,
            transcendentals=micros * nodes * width),
        name="recompute",
    )(hidden, edges_t, gates, gain, weight)


def tick_kernel(sc_ref, recv_ref, up_ref, slope_ref, mixt_ref, hidden_ref, inv_ref, gain_ref,
                w_ref, grads_in, act_in, out_ref, grads_ref, act_ref,
                g_s, act_s, a_s, z_s, inner_s, sems):
    del grads_in, act_in
    j = pl.program_id(0)
    steps = pl.num_programs(0)
    block = w_ref.shape[0]
    width = w_ref.shape[1]
    active = sc_ref[0] == 1
    slot = sc_ref[1]
    last = sc_ref[2] == 1

    @pl.when(jnp.logical_and(active, j == 0))
    def _():
        @pl.when(last)
        def _():
            pltpu.make_async_copy(up_ref.at[slot], g_s, sems.at[0]).start()

        @pl.when(jnp.logical_not(last))
        def _():
            pltpu.make_async_copy(recv_ref.at[0], g_s, sems.at[0]).start()

        pltpu.make_async_copy(recv_ref.at[0], g_s, sems.at[0]).wait()
        act = (g_s[...].astype(jnp.float32) * slope_ref[0]).astype(jnp.bfloat16)
        act_s[...] = act
        pltpu.make_async_copy(act_s, act_ref.at[slot], sems.at[1]).start()
        a_s[...] = jnp.dot(mixt_ref[0], act, preferred_element_type=jnp.float32).astype(jnp.bfloat16)
        inner_s[...] = jnp.zeros_like(inner_s)

    @pl.when(active)
    def _():
        at = pl.ds(pl.multiple_of(j * block, block), block)
        z = lax.dot_general(a_s[...], w_ref[...], NT, preferred_element_type=jnp.float32)
        z = z * gain_ref[:, at]
        z_s[:, at] = z
        part = jnp.sum(z * hidden_ref[0, :, at].astype(jnp.float32), axis=-1, keepdims=True)
        inner_s[...] += jnp.broadcast_to(part, inner_s.shape)

    @pl.when(jnp.logical_and(active, j == steps - 1))
    def _():
        inv = inv_ref[0, :, 0:1]
        scale = inv * inv * inv * (inner_s[:, 0:1] * (1.0 / width))
        grad = (g_s[...].astype(jnp.float32) + inv * z_s[...]
                - hidden_ref[0].astype(jnp.float32) * scale)
        out_ref[0] = grad.astype(jnp.bfloat16)
        copy = pltpu.make_async_copy(out_ref.at[0], grads_ref.at[slot], sems.at[2])
        copy.start()
        pltpu.make_async_copy(act_s, act_ref.at[slot], sems.at[1]).wait()
        copy.wait()


def tick(scalars, received, upstream, slope, mixt, hidden, inv, gain, weight, grads, act):
    micros, nodes, width = hidden.shape
    block = 512
    at_slot = lambda j, sc: (sc[1], 0, 0)
    return pl.pallas_call(
        tick_kernel,
        grid_spec=pltpu.PrefetchScalarGridSpec(
            num_scalar_prefetch=1,
            grid=(width // block,),
            in_specs=[
                pl.BlockSpec(memory_space=pl.ANY),
                pl.BlockSpec(memory_space=pl.ANY),
                pl.BlockSpec((1, nodes, width), at_slot),
                pl.BlockSpec((1, nodes, nodes), at_slot),
                pl.BlockSpec((1, nodes, width), at_slot),
                pl.BlockSpec((1, nodes, 128), at_slot),
                pl.BlockSpec((1, width), lambda j, sc: (0, 0)),
                pl.BlockSpec((block, width), lambda j, sc: (j * sc[0], 0)),
                pl.BlockSpec(memory_space=pl.ANY),
                pl.BlockSpec(memory_space=pl.ANY),
            ],
            out_specs=[
                pl.BlockSpec((1, nodes, width), lambda j, sc: (0, 0, 0)),
                pl.BlockSpec(memory_space=pl.ANY),
                pl.BlockSpec(memory_space=pl.ANY),
            ],
            scratch_shapes=[
                pltpu.VMEM((nodes, width), jnp.bfloat16),
                pltpu.VMEM((nodes, width), jnp.bfloat16),
                pltpu.VMEM((nodes, width), jnp.bfloat16),
                pltpu.VMEM((nodes, width), jnp.float32),
                pltpu.VMEM((nodes, 128), jnp.float32),
                pltpu.SemaphoreType.DMA((3,)),
            ],
        ),
        out_shape=[
            jax.ShapeDtypeStruct((1, nodes, width), jnp.bfloat16),
            jax.ShapeDtypeStruct(grads.shape, grads.dtype),
            jax.ShapeDtypeStruct(act.shape, act.dtype),
        ],
        input_output_aliases={9: 1, 10: 2},
        compiler_params=pltpu.CompilerParams(vmem_limit_bytes=VMEM_LIMIT),
        cost_estimate=pl.CostEstimate(
            flops=2 * nodes * width * width,
            bytes_accessed=2 * width * width + 12 * nodes * width,
            transcendentals=0),
        name="tick",
    )(scalars, received, upstream, slope, mixt, hidden, inv, gain, weight, grads, act)


def local(section_inputs, weights, norm_gains, upstream, edge_list, time_steps):
    section = lax.axis_index("pipe")
    sections = lax.axis_size("pipe")
    micros = section_inputs.shape[1]
    width = section_inputs.shape[3]
    hidden = section_inputs[0]
    weight = weights[0]
    gates = timestep_gate(time_steps[:, 0], width)
    edges_t = jnp.swapaxes(edge_list[:, 0], 1, 2)
    mixed, slope, mixt, inv, grads, act = recompute(hidden, edges_t, gates, norm_gains, weight)

    received = upstream
    is_last = (section == sections - 1).astype(jnp.int32)
    ticks = sections + micros - 1
    for t in range(ticks):
        micro = t - (sections - 1 - section)
        active = jnp.logical_and(micro >= 0, micro < micros).astype(jnp.int32)
        scalars = jnp.stack([active, jnp.clip(micro, 0, micros - 1), is_last])
        sent, grads, act = tick(scalars, received, upstream, slope, mixt, hidden, inv,
                                norm_gains, weight, grads, act)
        if t < ticks - 1:
            pairs = [(s, s - 1) for s in range(1, sections)
                     if 0 <= t - (sections - 1 - s) < micros]
            received = lax.ppermute(sent, "pipe", pairs)

    partial = lax.dot_general(mixed.reshape(-1, width), act.reshape(-1, width),
                              (((0,), (0,)), ((), ())), preferred_element_type=jnp.float32)
    rows = lax.psum_scatter(partial.astype(jnp.bfloat16), "dp", scatter_dimension=0, tiled=True)
    return (grads[None], rows[None])


def solution(mesh):
    in_specs = (
        P("pipe", None, "dp", None),
        P("pipe", None, None),
        P("pipe", None),
        P(None, "dp", None),
        P(None, "dp", None, None),
        P(None, "dp"),
    )
    out_specs = (P("pipe", None, "dp", None), P("pipe", "dp", None))
    return jax.shard_map(local, mesh=mesh, in_specs=in_specs, out_specs=out_specs, check_vma=False)
```

```python
import functools
import math

import jax
import jax.numpy as jnp
from jax import lax
from jax.experimental import pallas as pl
from jax.experimental.pallas import tpu as pltpu
from jax.sharding import PartitionSpec as P

NT = (((1,), (1,)), ((), ()))
BLOCK = 512
IN_VMEM = pl.BlockSpec(memory_space=pltpu.VMEM)
ANYWHERE = pl.BlockSpec(memory_space=pl.ANY)


def timestep_gate(time_steps, width):
    frequency = jnp.exp(-math.log(10000.0) * jnp.arange(width).astype(jnp.float32) / width)
    return 1.0 + 0.5 * jnp.sin(time_steps.astype(jnp.float32)[..., None] * frequency)


def in_hbm(x):
    return pltpu.with_memory_space_constraint(x, pltpu.HBM)


def held(x):
    return pltpu.with_memory_space_constraint(x, pltpu.VMEM)


def recompute_kernel(pos_ref, hidden_ref, edge_ref, gate_ref, gain_ref, w_ref,
                     own_own, own_far, far_own, far_far,
                     slope_ref, mixt_ref, inv_ref, wt_ref, grads_ref, act_ref,
                     mixed_s, turned_s, w_s, sems):
    del grads_ref, act_ref
    micros, nodes, width = hidden_ref.shape
    blocks = width // BLOCK
    rows16 = width // 16

    def fetch(j, slot):
        at = pl.ds(pl.multiple_of(j * BLOCK, BLOCK), BLOCK)
        return pltpu.make_async_copy(w_ref.at[:, at], w_s.at[slot], sems.at[slot])

    fetch(0, 0).start()
    edges = edge_ref.shape[2]
    ids = lax.broadcasted_iota(jnp.int32, (nodes, edges), 0)
    rows = lax.broadcasted_iota(jnp.int32, (nodes, nodes), 0)
    cols = lax.broadcasted_iota(jnp.int32, (nodes, nodes), 1)
    eye = jnp.where(rows == cols, 1.0, 0.0)
    for k in range(micros):
        src = jnp.where(edge_ref[k, 0:1, :] == ids, 1.0, 0.0).astype(jnp.bfloat16)
        tgt = jnp.where(edge_ref[k, 1:2, :] == ids, 1.0, 0.0).astype(jnp.bfloat16)
        adj = lax.dot_general(src, tgt, NT, preferred_element_type=jnp.float32)
        adj = adj + lax.dot_general(tgt, src, NT, preferred_element_type=jnp.float32) + eye
        mix = adj / jnp.sum(adj, axis=-1, keepdims=True)
        mixt_ref[k] = mix.T.astype(jnp.bfloat16)
        wide = hidden_ref[k].astype(jnp.float32)
        inv = lax.rsqrt(jnp.mean(wide * wide, axis=-1, keepdims=True) + 1e-06)
        inv_ref[k] = jnp.broadcast_to(inv, (nodes, 128))
        normed = (wide * inv * gain_ref[...]).astype(jnp.bfloat16)
        mixed = jnp.dot(mix.astype(jnp.bfloat16), normed, preferred_element_type=jnp.float32)
        mixed = mixed.astype(jnp.bfloat16)
        mixed_s[k * nodes:(k + 1) * nodes, :] = mixed
        turned = mixed.T
        for q in range(16):
            place = q // 4
            turned_s[q % 4, place * rows16:(place + 1) * rows16, k * nodes:(k + 1) * nodes] = (
                turned[q * rows16:(q + 1) * rows16, :])

    z, core = pos_ref[2], pos_ref[3]
    copies = []
    for n, ref in enumerate((own_own, own_far, far_own, far_far)):
        place = lax.rem(z + n % 2, 2) * 2 + lax.rem(core + n // 2, 2)
        copies.append(pltpu.make_async_copy(turned_s.at[place], ref, sems.at[2 + n]))
        copies[n].start()

    @pl.loop(0, blocks)
    def _(j):
        slot = lax.rem(j, 2)

        @pl.when(j + 1 < blocks)
        def _():
            fetch(j + 1, 1 - slot).start()

        fetch(j, slot).wait()
        at = pl.ds(pl.multiple_of(j * BLOCK, BLOCK), BLOCK)
        u = jnp.dot(mixed_s[...], w_s[slot], preferred_element_type=jnp.float32)
        wt_ref[at, :] = w_s[slot].T
        logistic = jax.nn.sigmoid(u)
        slope = logistic * (1.0 + u * (1.0 - logistic))
        for k in range(micros):
            gated = slope[k * nodes:(k + 1) * nodes, :] * gate_ref[k:k + 1, at]
            slope_ref[k, :, at] = gated.astype(jnp.bfloat16)

    for copy in copies:
        copy.wait()


def recompute(position, hidden, edges_t, gates, gain, weight):
    micros, nodes, width = hidden.shape
    piece = pltpu.HBM((width // 4, micros * nodes), jnp.bfloat16)
    return pl.pallas_call(
        recompute_kernel,
        in_specs=[pl.BlockSpec(memory_space=pltpu.SMEM)] + [IN_VMEM] * 4 + [ANYWHERE],
        out_specs=[ANYWHERE] * 4 + [IN_VMEM] * 4 + [ANYWHERE] * 2,
        out_shape=[
            piece, piece, piece, piece,
            pltpu.VMEM((micros, nodes, width), jnp.bfloat16),
            pltpu.VMEM((micros, nodes, nodes), jnp.bfloat16),
            pltpu.VMEM((micros, nodes, 128), jnp.float32),
            pltpu.VMEM((width, width), jnp.bfloat16),
            pltpu.HBM((micros, nodes, width), jnp.bfloat16),
            pltpu.HBM((micros, 4, nodes, width // 4), jnp.bfloat16),
        ],
        scratch_shapes=[
            pltpu.VMEM((micros * nodes, width), jnp.bfloat16),
            pltpu.VMEM((4, width // 4, micros * nodes), jnp.bfloat16),
            pltpu.VMEM((2, width, BLOCK), jnp.bfloat16),
            pltpu.SemaphoreType.DMA((6,)),
        ],
        compiler_params=pltpu.CompilerParams(vmem_limit_bytes=20 * 1024 * 1024),
        cost_estimate=pl.CostEstimate(
            flops=2 * micros * nodes * width * width,
            bytes_accessed=2 * width * width + 10 * micros * nodes * width,
            transcendentals=micros * nodes * width),
        name="recompute",
    )(position, held(hidden), held(edges_t), held(gates), held(gain), in_hbm(weight))


def put_columns(ref, act, y):
    part = ref.shape[2]
    for q in range(4):
        ref[lax.rem(q + 4 - y, 4)] = act[:, q * part:(q + 1) * part]


def tick_kernel(t, sections, sec_ref, *refs):
    if t < 3:
        up_ref, *refs = refs
    if t > 0:
        recv_ref, *refs = refs
    (slope_ref, mixt_ref, hidden_ref, inv_ref, gain_ref, wt_ref, grads_in, act_in,
     out_ref, grads_ref, act_ref, g_s, a_s, z_s, inner_s, h_s, act_s, sems) = refs
    del grads_in, act_in
    micros, nodes, width = hidden_ref.shape
    section = sec_ref[0]
    slot = t - (sections - 1 - section)
    last = section == sections - 1

    @pl.when(jnp.logical_and(slot >= 0, slot < micros))
    def _():
        fetch = pltpu.make_async_copy(hidden_ref.at[slot], h_s, sems.at[0])
        fetch.start()
        if t < micros:
            @pl.when(last)
            def _():
                copy = pltpu.make_async_copy(up_ref.at[t], out_ref.at[0], sems.at[1])
                copy.start()
                copy.wait()
                g_s[...] = out_ref[0].astype(jnp.float32)

            if t > 0:
                @pl.when(jnp.logical_not(last))
                def _():
                    g_s[...] = recv_ref[0].astype(jnp.float32)
        else:
            g_s[...] = recv_ref[0].astype(jnp.float32)
        act = (g_s[...] * slope_ref[slot].astype(jnp.float32)).astype(jnp.bfloat16)
        put_columns(act_s, act, sec_ref[1])
        keep_act = pltpu.make_async_copy(act_s, act_ref.at[slot], sems.at[2])
        keep_act.start()
        a_s[...] = jnp.dot(mixt_ref[slot], act, preferred_element_type=jnp.float32).astype(jnp.bfloat16)
        inner_s[...] = jnp.zeros_like(inner_s)
        fetch.wait()

        @pl.loop(0, width // BLOCK)
        def _(j):
            at = pl.ds(pl.multiple_of(j * BLOCK, BLOCK), BLOCK)
            z = jnp.dot(a_s[...], wt_ref[:, at], preferred_element_type=jnp.float32)
            z = z * gain_ref[:, at]
            z_s[:, at] = z
            part = jnp.sum(z * h_s[:, at].astype(jnp.float32), axis=-1, keepdims=True)
            inner_s[...] += jnp.broadcast_to(part, inner_s.shape)

        inv = inv_ref[slot, :, 0:1]
        scale = inv * inv * inv * (inner_s[:, 0:1] * (1.0 / width))
        grad = g_s[...] + inv * z_s[...] - h_s[...].astype(jnp.float32) * scale
        out_ref[0] = grad.astype(jnp.bfloat16)
        keep_grad = pltpu.make_async_copy(out_ref.at[0], grads_ref.at[slot], sems.at[3])
        keep_grad.start()
        keep_act.wait()
        keep_grad.wait()


def tick(t, sections, section, received, upstream, slope, mixt, hidden, inv, gain, wt, grads, act):
    micros, nodes, width = hidden.shape
    extra = [in_hbm(upstream)] if t < 3 else []
    taken = [held(received)] if t > 0 else []
    base = 7 + len(extra) + len(taken)
    return pl.pallas_call(
        functools.partial(tick_kernel, t, sections),
        in_specs=[pl.BlockSpec(memory_space=pltpu.SMEM)] + [ANYWHERE] * len(extra)
        + [IN_VMEM] * (2 + len(taken)) + [ANYWHERE] + [IN_VMEM] * 3 + [ANYWHERE] * 2,
        out_specs=[IN_VMEM, ANYWHERE, ANYWHERE],
        scratch_shapes=[
            pltpu.VMEM((nodes, width), jnp.float32),
            pltpu.VMEM((nodes, width), jnp.bfloat16),
            pltpu.VMEM((nodes, width), jnp.float32),
            pltpu.VMEM((nodes, 128), jnp.float32),
            pltpu.VMEM((nodes, width), jnp.bfloat16),
            pltpu.VMEM(act.shape[1:], jnp.bfloat16),
            pltpu.SemaphoreType.DMA((4,)),
        ],
        out_shape=[
            pltpu.VMEM((1, nodes, width), jnp.bfloat16),
            pltpu.HBM(grads.shape, grads.dtype),
            pltpu.HBM(act.shape, act.dtype),
        ],
        input_output_aliases={base: 1, base + 1: 2},
        compiler_params=pltpu.CompilerParams(vmem_limit_bytes=14 * 1024 * 1024),
        cost_estimate=pl.CostEstimate(
            flops=2 * nodes * width * width,
            bytes_accessed=2 * width * width + 12 * nodes * width,
            transcendentals=0),
        name="tick",
    )(section, *extra, *taken, held(slope), held(mixt), in_hbm(hidden), held(inv),
      held(gain), held(wt), in_hbm(grads), in_hbm(act))


def last_act_kernel(pos_ref, recv_ref, slope_ref, act_ref, *refs):
    outs, (act_s, sems) = refs[:4], refs[4:]
    micros = act_ref.shape[0]

    @pl.when(pos_ref[0] == 0)
    def _():
        act = recv_ref[0].astype(jnp.float32) * slope_ref[micros - 1].astype(jnp.float32)
        put_columns(act_s, act.astype(jnp.bfloat16), pos_ref[1])

    @pl.when(pos_ref[0] != 0)
    def _():
        copy = pltpu.make_async_copy(act_ref.at[micros - 1], act_s, sems.at[0])
        copy.start()
        copy.wait()

    for d in range(4):
        outs[d][...] = act_s[d]


def last_act(position, received, slope, act):
    micros, nodes, width = slope.shape
    return pl.pallas_call(
        last_act_kernel,
        in_specs=[pl.BlockSpec(memory_space=pltpu.SMEM), IN_VMEM, IN_VMEM, ANYWHERE],
        out_specs=[IN_VMEM] * 4,
        out_shape=[pltpu.VMEM((nodes, width // 4), jnp.bfloat16)] * 4,
        scratch_shapes=[pltpu.VMEM(act.shape[1:], jnp.bfloat16), pltpu.SemaphoreType.DMA((1,))],
        compiler_params=pltpu.CompilerParams(vmem_limit_bytes=14 * 1024 * 1024),
        cost_estimate=pl.CostEstimate(flops=nodes * width, bytes_accessed=8 * nodes * width,
                                      transcendentals=0),
        name="last_act",
    )(position, held(received), held(slope), in_hbm(act))


def head_acts_kernel(act_ref, *refs):
    outs, sems = refs[:4], refs[4]
    nodes = act_ref.shape[2]
    copies = []
    for d in range(4):
        for k in range(act_ref.shape[0] - 1):
            to = outs[d].at[pl.ds(k * nodes, nodes), :]
            copies.append(pltpu.make_async_copy(act_ref.at[k, d], to, sems.at[d, k]))
            copies[-1].start()
    for copy in copies:
        copy.wait()


def head_acts(act):
    micros, parts, nodes, part = act.shape
    return pl.pallas_call(
        head_acts_kernel,
        in_specs=[ANYWHERE],
        out_specs=[ANYWHERE] * 4,
        out_shape=[pltpu.HBM(((micros - 1) * nodes, part), jnp.bfloat16)] * 4,
        scratch_shapes=[pltpu.SemaphoreType.DMA((4, micros - 1))],
        compiler_params=pltpu.CompilerParams(vmem_limit_bytes=14 * 1024 * 1024),
        cost_estimate=pl.CostEstimate(flops=0, bytes_accessed=16 * micros * nodes * part,
                                      transcendentals=0),
        name="head_acts",
    )(in_hbm(act))


def gradient_kernel(first, start, y_ref, *refs):
    count = 16
    turned, acts, rest = refs[:count], refs[count:2 * count], refs[2 * count:]
    left_s, right_s, total_s, sems = rest[-4:]
    tokens = left_s.shape[2]

    def copies(p):
        at = pl.ds(start, tokens)
        return (pltpu.make_async_copy(turned[p].at[:, at], left_s.at[p % 2], sems.at[0, p % 2]),
                pltpu.make_async_copy(acts[p], right_s.at[p % 2], sems.at[1, p % 2]))

    for copy in copies(0):
        copy.start()
    for p in range(count):
        if p + 1 < count:
            for copy in copies(p + 1):
                copy.start()
        for copy in copies(p):
            copy.wait()
        product = jnp.dot(left_s[p % 2], right_s[p % 2], preferred_element_type=jnp.float32)
        if p > 0:
            total_s[...] += product
        elif first:
            total_s[...] = product
        else:
            total_s[...] = rest[0][...] + product
    if first:
        rest[0][...] = total_s[...]
    else:
        rows = rest[1].shape[0]
        for d in range(4):
            q = lax.rem(y_ref[1] + d, 4)
            part = total_s[pl.ds(pl.multiple_of(q * rows, rows), rows), :]
            rest[1 + d][...] = part.astype(jnp.bfloat16)


def gradient(position, turned, acts, start, total):
    rows = turned[0].shape[0]
    tokens, part = acts[0].shape
    first = total is None
    kept = [] if first else [held(total)]
    if first:
        out_shape = [pltpu.VMEM((rows, part), jnp.float32)]
    else:
        out_shape = [pltpu.VMEM((rows // 4, part), jnp.bfloat16)] * 4
    return pl.pallas_call(
        functools.partial(gradient_kernel, first, start),
        in_specs=[pl.BlockSpec(memory_space=pltpu.SMEM)] + [ANYWHERE] * 32 + [IN_VMEM] * len(kept),
        out_specs=[IN_VMEM] * len(out_shape),
        out_shape=out_shape,
        scratch_shapes=[
            pltpu.VMEM((2, rows, tokens), jnp.bfloat16),
            pltpu.VMEM((2, tokens, part), jnp.bfloat16),
            pltpu.VMEM((rows, part), jnp.float32),
            pltpu.SemaphoreType.DMA((2, 2)),
        ],
        compiler_params=pltpu.CompilerParams(vmem_limit_bytes=14 * 1024 * 1024),
        cost_estimate=pl.CostEstimate(flops=32 * rows * part * tokens,
                                      bytes_accessed=32 * tokens * (rows + part),
                                      transcendentals=0),
        name="gradient",
    )(position, *[in_hbm(x) for x in turned], *acts, *kept)


def assemble_kernel(y_ref, *refs):
    out_ref = refs[-1]
    part = refs[0].shape[1]
    for d in range(4):
        q = lax.rem(y_ref[1] + 4 - d, 4)
        out_ref[:, pl.ds(pl.multiple_of(q * part, part), part)] = refs[d][...]


def assemble(y, parts):
    rows, part = parts[0].shape
    whole = lambda i: (0, 0)
    return pl.pallas_call(
        assemble_kernel,
        grid=(1,),
        in_specs=[pl.BlockSpec(memory_space=pltpu.SMEM)] + [pl.BlockSpec((rows, part), whole)] * 4,
        out_specs=pl.BlockSpec((rows, 4 * part), whole),
        out_shape=jax.ShapeDtypeStruct((rows, 4 * part), parts[0].dtype),
        compiler_params=pltpu.CompilerParams(vmem_limit_bytes=14 * 1024 * 1024),
        name="assemble",
    )(y, *parts)


def by_y(x, d):
    return lax.ppermute(x, "dp", [(i, (i + 4 * d) % 16) for i in range(16)])


def by_z(x):
    return lax.ppermute(x, "dp", [(i, i ^ 2) for i in range(16)])


def by_core(x):
    return lax.ppermute(x, "dp", [(i, i ^ 1) for i in range(16)])


def tied(values, after):
    *values, after = lax.optimization_barrier((*values, after))
    return values, after


def local(section_inputs, weights, norm_gains, upstream, edge_list, time_steps):
    section = lax.axis_index("pipe")
    sections = lax.axis_size("pipe")
    replica = lax.axis_index("dp")
    micros = section_inputs.shape[1]
    nodes = section_inputs.shape[2]
    width = section_inputs.shape[3]
    hidden = section_inputs[0]
    gates = timestep_gate(time_steps[:, 0], width)
    edges_t = jnp.swapaxes(edge_list[:, 0], 1, 2)
    position = jnp.stack([section, replica // 4, (replica // 2) % 2, replica % 2]).astype(jnp.int32)
    own_own, own_far, far_own, far_far, slope, mixt, inv, wt, grads, act = recompute(
        position, hidden, edges_t, gates, norm_gains, weights[0])

    received = None
    ticks = sections + micros - 1
    for t in range(ticks):
        if t == ticks - 1:
            acts_last = last_act(position, received, slope, act)
            near_last = [acts_last[0]] + [by_y(acts_last[d], d) for d in range(1, 4)]
        sent, grads, act = tick(t, sections, position, received, upstream, slope, mixt, hidden, inv,
                                norm_gains, wt, grads, act)
        if t == 0:
            (own_far, far_own, far_far), sent = tied((own_far, far_own, far_far), sent)
            quad = [own_own, by_core(far_own), by_z(own_far), by_core(far_far)]
        if t == 1:
            (quad[1], quad[3]), sent = tied((quad[1], quad[3]), sent)
            quad[3] = by_z(quad[3])
            after = [by_y(quad[0], 1), by_y(quad[1], 1)]
            before = [by_y(quad[0], 3), by_y(quad[1], 3)]
        if t == 3:
            (quad[2], quad[3]), sent = tied((quad[2], quad[3]), sent)
            after += [by_y(quad[2], 1), by_y(quad[3], 1)]
            before += [by_y(quad[2], 3), by_y(quad[3], 3)]
        if t == 5:
            (after[0], after[1], before[2], before[3]), sent = tied(
                (after[0], after[1], before[2], before[3]), sent)
            opposite = [by_y(after[0], 1), by_y(after[1], 1), by_y(before[2], 3), by_y(before[3], 3)]
        if t == 7:
            opposite, sent = tied(opposite, sent)
        if t < ticks - 1:
            pairs = [(s, s - 1) for s in range(1, sections)
                     if 0 <= t - (sections - 1 - s) < micros]
            received = lax.ppermute(sent, "pipe", pairs)
        if t == ticks - 2:
            acts_head = head_acts(act)
            near_head = [acts_head[0]] + [by_y(acts_head[d], d) for d in range(1, 4)]

    def spread(near):
        across = [by_z(x) for x in near]
        return near + [by_core(x) for x in near] + across + [by_core(x) for x in across]

    turned = [x for n in range(4) for x in (quad[n], after[n], opposite[n], before[n])]
    total, = gradient(position, turned, spread(near_head), 0, None)
    near_last, sent = tied(near_last, sent)
    parts = gradient(position, turned, spread(near_last), (micros - 1) * nodes, total)
    parts = [parts[0]] + [by_y(parts[d], d) for d in range(1, 4)]
    rows = assemble(position, parts)
    return (grads[None], rows[None])


def solution(mesh):
    in_specs = (
        P("pipe", None, "dp", None),
        P("pipe", None, None),
        P("pipe", None),
        P(None, "dp", None),
        P(None, "dp", None, None),
        P(None, "dp"),
    )
    out_specs = (P("pipe", None, "dp", None), P("pipe", "dp", None))
    return jax.shard_map(local, mesh=mesh, in_specs=in_specs, out_specs=out_specs, check_vma=False)
```

```python
import functools
import math

import jax
import jax.numpy as jnp
from jax import lax
from jax.experimental import pallas as pl
from jax.experimental.pallas import tpu as pltpu
from jax.sharding import PartitionSpec as P

NT = (((1,), (1,)), ((), ()))
BLOCK = 512
IN_VMEM = pl.BlockSpec(memory_space=pltpu.VMEM)
ANYWHERE = pl.BlockSpec(memory_space=pl.ANY)


def timestep_gate(time_steps, width):
    frequency = jnp.exp(-math.log(10000.0) * jnp.arange(width).astype(jnp.float32) / width)
    return 1.0 + 0.5 * jnp.sin(time_steps.astype(jnp.float32)[..., None] * frequency)


def in_hbm(x):
    return pltpu.with_memory_space_constraint(x, pltpu.HBM)


def held(x):
    return pltpu.with_memory_space_constraint(x, pltpu.VMEM)


def prepare(k, hidden_ref, edge_ref, gain_ref, mixt_ref, inv_ref, turned_s, at):
    nodes, width = hidden_ref.shape[1:]
    rows16 = width // 16
    edges = edge_ref.shape[2]
    ids = lax.broadcasted_iota(jnp.int32, (nodes, edges), 0)
    rows = lax.broadcasted_iota(jnp.int32, (nodes, nodes), 0)
    cols = lax.broadcasted_iota(jnp.int32, (nodes, nodes), 1)
    eye = jnp.where(rows == cols, 1.0, 0.0)
    src = jnp.where(edge_ref[k, 0:1, :] == ids, 1.0, 0.0).astype(jnp.bfloat16)
    tgt = jnp.where(edge_ref[k, 1:2, :] == ids, 1.0, 0.0).astype(jnp.bfloat16)
    adj = lax.dot_general(src, tgt, NT, preferred_element_type=jnp.float32)
    adj = adj + lax.dot_general(tgt, src, NT, preferred_element_type=jnp.float32) + eye
    mix = adj / jnp.sum(adj, axis=-1, keepdims=True)
    mixt_ref[k] = mix.T.astype(jnp.bfloat16)
    wide = hidden_ref[k].astype(jnp.float32)
    inv = lax.rsqrt(jnp.mean(wide * wide, axis=-1, keepdims=True) + 1e-06)
    inv_ref[k] = jnp.broadcast_to(inv, (nodes, 128))
    normed = (wide * inv * gain_ref[...]).astype(jnp.bfloat16)
    mixed = jnp.dot(mix.astype(jnp.bfloat16), normed, preferred_element_type=jnp.float32)
    mixed = mixed.astype(jnp.bfloat16)
    turned = mixed.T
    for q in range(16):
        place = q // 4
        turned_s[q % 4, place * rows16:(place + 1) * rows16, at:at + nodes] = (
            turned[q * rows16:(q + 1) * rows16, :])
    return mixed


def gated_slope(u, gate):
    logistic = jax.nn.sigmoid(u)
    return (logistic * (1.0 + u * (1.0 - logistic)) * gate).astype(jnp.bfloat16)


def first_kernel(hidden_ref, edge_ref, gate_ref, gain_ref, w_ref,
                 p0, p1, p2, p3, slope_ref, mixt_ref, inv_ref, wt_ref, turned_ref, grads_ref, act_ref,
                 mixed_s, w_s, sems):
    del p0, p1, p2, p3, grads_ref, act_ref
    micros, nodes, width = hidden_ref.shape
    blocks = width // BLOCK

    def fetch(j, slot):
        at = pl.ds(pl.multiple_of(j * BLOCK, BLOCK), BLOCK)
        return pltpu.make_async_copy(w_ref.at[:, at], w_s.at[slot], sems.at[slot])

    for n in range(2):
        fetch(n, n).start()
    mixed_s[...] = prepare(0, hidden_ref, edge_ref, gain_ref, mixt_ref, inv_ref, turned_ref, 0)

    @pl.loop(0, blocks)
    def _(j):
        slot = lax.rem(j, 2)
        fetch(j, slot).wait()
        at = pl.ds(pl.multiple_of(j * BLOCK, BLOCK), BLOCK)
        u = jnp.dot(mixed_s[...], w_s[slot], preferred_element_type=jnp.float32)
        wt_ref[at, :] = w_s[slot].T
        slope_ref[0, :, at] = gated_slope(u, gate_ref[0:1, at])

        @pl.when(j + 2 < blocks)
        def _():
            fetch(j + 2, slot).start()


def first(hidden, edges_t, gates, gain, weight):
    micros, nodes, width = hidden.shape
    piece = pltpu.HBM((width // 4, micros * nodes), jnp.bfloat16)
    return pl.pallas_call(
        first_kernel,
        in_specs=[IN_VMEM] * 4 + [ANYWHERE],
        out_specs=[ANYWHERE] * 4 + [IN_VMEM] * 5 + [ANYWHERE] * 2,
        out_shape=[
            piece, piece, piece, piece,
            pltpu.VMEM((micros, nodes, width), jnp.bfloat16),
            pltpu.VMEM((micros, nodes, nodes), jnp.bfloat16),
            pltpu.VMEM((micros, nodes, 128), jnp.float32),
            pltpu.VMEM((width, width), jnp.bfloat16),
            pltpu.VMEM((4, width // 4, nodes), jnp.bfloat16),
            pltpu.HBM((micros, nodes, width), jnp.bfloat16),
            pltpu.HBM((micros, 4, nodes, width // 4), jnp.bfloat16),
        ],
        scratch_shapes=[
            pltpu.VMEM((nodes, width), jnp.bfloat16),
            pltpu.VMEM((2, width, BLOCK), jnp.bfloat16),
            pltpu.SemaphoreType.DMA((2,)),
        ],
        compiler_params=pltpu.CompilerParams(vmem_limit_bytes=16 * 1024 * 1024),
        cost_estimate=pl.CostEstimate(
            flops=2 * nodes * width * width,
            bytes_accessed=2 * width * width + 10 * micros * nodes * width,
            transcendentals=nodes * width),
        name="first",
    )(held(hidden), held(edges_t), held(gates), held(gain), in_hbm(weight))


def second_kernel(turn, pos_ref, hidden_ref, edge_ref, gate_ref, gain_ref, wt_ref, turned_ref,
                  p0, p1, p2, p3, s0, m0, i0,
                  own_own, own_far, far_own, far_far, slope_ref, mixt_ref, inv_ref,
                  mixed_s, turned_s, sems):
    del p0, p1, p2, p3, s0, m0, i0
    micros, nodes, width = hidden_ref.shape
    z, core = pos_ref[2], pos_ref[3]

    @pl.when(core == turn)
    def _():
        for k in range(1, micros):
            mixed_s[(k - 1) * nodes:k * nodes, :] = prepare(
                k, hidden_ref, edge_ref, gain_ref, mixt_ref, inv_ref, turned_s, k * nodes)
        turned_s[:, :, 0:nodes] = turned_ref[...]
        copies = []
        for n, ref in enumerate((own_own, own_far, far_own, far_far)):
            place = lax.rem(z + n % 2, 2) * 2 + lax.rem(core + n // 2, 2)
            copies.append(pltpu.make_async_copy(turned_s.at[place], ref, sems.at[n]))
            copies[n].start()

        @pl.loop(0, width // BLOCK)
        def _(j):
            at = pl.ds(pl.multiple_of(j * BLOCK, BLOCK), BLOCK)
            u = lax.dot_general(mixed_s[...], wt_ref[at, :], NT, preferred_element_type=jnp.float32)
            for k in range(1, micros):
                slope_ref[k, :, at] = gated_slope(
                    u[(k - 1) * nodes:k * nodes, :], gate_ref[k:k + 1, at])

        for copy in copies:
            copy.wait()


def second(turn, position, hidden, edges_t, gates, gain, wt, turned, pieces, slope, mixt, inv):
    micros, nodes, width = hidden.shape
    kept = [in_hbm(x) for x in pieces] + [held(slope), held(mixt), held(inv)]
    specs = [ANYWHERE] * 4 + [IN_VMEM] * 3
    return pl.pallas_call(
        functools.partial(second_kernel, turn),
        in_specs=[pl.BlockSpec(memory_space=pltpu.SMEM)] + [IN_VMEM] * 6 + specs,
        out_specs=specs,
        out_shape=[pltpu.HBM(x.shape, x.dtype) for x in pieces]
        + [pltpu.VMEM(x.shape, x.dtype) for x in (slope, mixt, inv)],
        scratch_shapes=[
            pltpu.VMEM(((micros - 1) * nodes, width), jnp.bfloat16),
            pltpu.VMEM((4, width // 4, micros * nodes), jnp.bfloat16),
            pltpu.SemaphoreType.DMA((4,)),
        ],
        input_output_aliases={7 + n: n for n in range(7)},
        compiler_params=pltpu.CompilerParams(vmem_limit_bytes=16 * 1024 * 1024),
        cost_estimate=pl.CostEstimate(
            flops=2 * (micros - 1) * nodes * width * width,
            bytes_accessed=10 * micros * nodes * width,
            transcendentals=(micros - 1) * nodes * width),
        name="second",
    )(position, held(hidden), held(edges_t), held(gates), held(gain), held(wt), held(turned), *kept)


def put_columns(ref, act, y):
    part = ref.shape[2]
    for q in range(4):
        ref[lax.rem(q + 4 - y, 4)] = act[:, q * part:(q + 1) * part]


def tick_kernel(t, sections, sec_ref, *refs):
    if t < 3:
        up_ref, *refs = refs
    if t > 0:
        recv_ref, *refs = refs
    (slope_ref, mixt_ref, hidden_ref, inv_ref, gain_ref, wt_ref, grads_in, act_in,
     out_ref, grads_ref, act_ref, g_s, a_s, z_s, inner_s, h_s, act_s, sems) = refs
    del grads_in, act_in
    micros, nodes, width = hidden_ref.shape
    section = sec_ref[0]
    slot = t - (sections - 1 - section)
    last = section == sections - 1

    @pl.when(jnp.logical_and(slot >= 0, slot < micros))
    def _():
        fetch = pltpu.make_async_copy(hidden_ref.at[slot], h_s, sems.at[0])
        fetch.start()
        if t < micros:
            @pl.when(last)
            def _():
                copy = pltpu.make_async_copy(up_ref.at[t], out_ref.at[0], sems.at[1])
                copy.start()
                copy.wait()
                g_s[...] = out_ref[0].astype(jnp.float32)

            if t > 0:
                @pl.when(jnp.logical_not(last))
                def _():
                    g_s[...] = recv_ref[0].astype(jnp.float32)
        else:
            g_s[...] = recv_ref[0].astype(jnp.float32)
        act = (g_s[...] * slope_ref[slot].astype(jnp.float32)).astype(jnp.bfloat16)
        put_columns(act_s, act, sec_ref[1])
        keep_act = pltpu.make_async_copy(act_s, act_ref.at[slot], sems.at[2])
        keep_act.start()
        a_s[...] = jnp.dot(mixt_ref[slot], act, preferred_element_type=jnp.float32).astype(jnp.bfloat16)
        inner_s[...] = jnp.zeros_like(inner_s)
        fetch.wait()

        @pl.loop(0, width // BLOCK)
        def _(j):
            at = pl.ds(pl.multiple_of(j * BLOCK, BLOCK), BLOCK)
            z = jnp.dot(a_s[...], wt_ref[:, at], preferred_element_type=jnp.float32)
            z = z * gain_ref[:, at]
            z_s[:, at] = z
            part = jnp.sum(z * h_s[:, at].astype(jnp.float32), axis=-1, keepdims=True)
            inner_s[...] += jnp.broadcast_to(part, inner_s.shape)

        inv = inv_ref[slot, :, 0:1]
        scale = inv * inv * inv * (inner_s[:, 0:1] * (1.0 / width))
        grad = g_s[...] + inv * z_s[...] - h_s[...].astype(jnp.float32) * scale
        out_ref[0] = grad.astype(jnp.bfloat16)
        keep_grad = pltpu.make_async_copy(out_ref.at[0], grads_ref.at[slot], sems.at[3])
        keep_grad.start()
        keep_act.wait()
        keep_grad.wait()


def tick(t, sections, section, received, upstream, slope, mixt, hidden, inv, gain, wt, grads, act):
    micros, nodes, width = hidden.shape
    extra = [in_hbm(upstream)] if t < 3 else []
    taken = [held(received)] if t > 0 else []
    base = 7 + len(extra) + len(taken)
    return pl.pallas_call(
        functools.partial(tick_kernel, t, sections),
        in_specs=[pl.BlockSpec(memory_space=pltpu.SMEM)] + [ANYWHERE] * len(extra)
        + [IN_VMEM] * (2 + len(taken)) + [ANYWHERE] + [IN_VMEM] * 3 + [ANYWHERE] * 2,
        out_specs=[IN_VMEM, ANYWHERE, ANYWHERE],
        scratch_shapes=[
            pltpu.VMEM((nodes, width), jnp.float32),
            pltpu.VMEM((nodes, width), jnp.bfloat16),
            pltpu.VMEM((nodes, width), jnp.float32),
            pltpu.VMEM((nodes, 128), jnp.float32),
            pltpu.VMEM((nodes, width), jnp.bfloat16),
            pltpu.VMEM(act.shape[1:], jnp.bfloat16),
            pltpu.SemaphoreType.DMA((4,)),
        ],
        out_shape=[
            pltpu.VMEM((1, nodes, width), jnp.bfloat16),
            pltpu.HBM(grads.shape, grads.dtype),
            pltpu.HBM(act.shape, act.dtype),
        ],
        input_output_aliases={base: 1, base + 1: 2},
        compiler_params=pltpu.CompilerParams(vmem_limit_bytes=14 * 1024 * 1024),
        cost_estimate=pl.CostEstimate(
            flops=2 * nodes * width * width,
            bytes_accessed=2 * width * width + 12 * nodes * width,
            transcendentals=0),
        name="tick",
    )(section, *extra, *taken, held(slope), held(mixt), in_hbm(hidden), held(inv),
      held(gain), held(wt), in_hbm(grads), in_hbm(act))


def last_act_kernel(pos_ref, recv_ref, slope_ref, act_ref, *refs):
    outs, (act_s, sems) = refs[:4], refs[4:]
    micros = act_ref.shape[0]

    @pl.when(pos_ref[0] == 0)
    def _():
        act = recv_ref[0].astype(jnp.float32) * slope_ref[micros - 1].astype(jnp.float32)
        put_columns(act_s, act.astype(jnp.bfloat16), pos_ref[1])

    @pl.when(pos_ref[0] != 0)
    def _():
        copy = pltpu.make_async_copy(act_ref.at[micros - 1], act_s, sems.at[0])
        copy.start()
        copy.wait()

    for d in range(4):
        outs[d][...] = act_s[d]


def last_act(position, received, slope, act):
    micros, nodes, width = slope.shape
    return pl.pallas_call(
        last_act_kernel,
        in_specs=[pl.BlockSpec(memory_space=pltpu.SMEM), IN_VMEM, IN_VMEM, ANYWHERE],
        out_specs=[IN_VMEM] * 4,
        out_shape=[pltpu.VMEM((nodes, width // 4), jnp.bfloat16)] * 4,
        scratch_shapes=[pltpu.VMEM(act.shape[1:], jnp.bfloat16), pltpu.SemaphoreType.DMA((1,))],
        compiler_params=pltpu.CompilerParams(vmem_limit_bytes=14 * 1024 * 1024),
        cost_estimate=pl.CostEstimate(flops=nodes * width, bytes_accessed=8 * nodes * width,
                                      transcendentals=0),
        name="last_act",
    )(position, held(received), held(slope), in_hbm(act))


def head_acts_kernel(act_ref, *refs):
    outs, (act_s, sems) = refs[:4], refs[4:]
    count, parts, nodes, part = act_s.shape
    copies = []
    for k in range(count):
        copies.append(pltpu.make_async_copy(act_ref.at[k], act_s.at[k], sems.at[k]))
        copies[k].start()
    for k in range(count):
        copies[k].wait()
        for d in range(4):
            outs[d][k * nodes:(k + 1) * nodes, :] = act_s[k, d]


def head_acts(act):
    micros, parts, nodes, part = act.shape
    return pl.pallas_call(
        head_acts_kernel,
        in_specs=[ANYWHERE],
        out_specs=[IN_VMEM] * 4,
        out_shape=[pltpu.VMEM(((micros - 1) * nodes, part), jnp.bfloat16)] * 4,
        scratch_shapes=[pltpu.VMEM((micros - 1,) + act.shape[1:], jnp.bfloat16),
                        pltpu.SemaphoreType.DMA((micros - 1,))],
        compiler_params=pltpu.CompilerParams(vmem_limit_bytes=14 * 1024 * 1024),
        cost_estimate=pl.CostEstimate(flops=0, bytes_accessed=16 * micros * nodes * part,
                                      transcendentals=0),
        name="head_acts",
    )(in_hbm(act))


def gradient_kernel(first_part, start, pos_ref, *refs):
    count = 16
    turned, acts, rest = refs[:count], refs[count:2 * count], refs[2 * count:]
    left_s, right_s, total_s, sems = rest[-4:]
    pairs, rows, depth = left_s.shape
    tokens = acts[0].shape[0]
    each = depth // tokens
    copies = []
    for p in range(count):
        place, at = p // each, (p % each) * tokens
        copies.append((
            pltpu.make_async_copy(turned[p].at[:, pl.ds(start, tokens)],
                                  left_s.at[place, :, pl.ds(at, tokens)], sems.at[0, p]),
            pltpu.make_async_copy(acts[p], right_s.at[place, pl.ds(at, tokens), :], sems.at[1, p])))
        for copy in copies[p]:
            copy.start()
    for n in range(pairs):
        for p in range(n * each, (n + 1) * each):
            for copy in copies[p]:
                copy.wait()
        product = jnp.dot(left_s[n], right_s[n], preferred_element_type=jnp.float32)
        if n > 0:
            total_s[...] += product
        elif first_part:
            total_s[...] = product
        else:
            total_s[...] = rest[0][...] + product
    if first_part:
        rest[0][...] = total_s[...]
    else:
        block = rest[1].shape[0]
        for d in range(4):
            q = lax.rem(pos_ref[1] + d, 4)
            part = total_s[pl.ds(pl.multiple_of(q * block, block), block), :]
            rest[1 + d][...] = part.astype(jnp.bfloat16)


def gradient(position, turned, acts, start, total):
    rows = turned[0].shape[0]
    tokens, part = acts[0].shape
    first_part = total is None
    depth = 256
    pairs = 16 * tokens // depth
    kept = [] if first_part else [held(total)]
    if first_part:
        out_shape = [pltpu.VMEM((rows, part), jnp.float32)]
    else:
        out_shape = [pltpu.VMEM((rows // 4, part), jnp.bfloat16)] * 4
    return pl.pallas_call(
        functools.partial(gradient_kernel, first_part, start),
        in_specs=[pl.BlockSpec(memory_space=pltpu.SMEM)] + [ANYWHERE] * 32 + [IN_VMEM] * len(kept),
        out_specs=[IN_VMEM] * len(out_shape),
        out_shape=out_shape,
        scratch_shapes=[
            pltpu.VMEM((pairs, rows, depth), jnp.bfloat16),
            pltpu.VMEM((pairs, depth, part), jnp.bfloat16),
            pltpu.VMEM((rows, part), jnp.float32),
            pltpu.SemaphoreType.DMA((2, 16)),
        ],
        compiler_params=pltpu.CompilerParams(vmem_limit_bytes=(28 if first_part else 18) * 1024 * 1024),
        cost_estimate=pl.CostEstimate(flops=32 * rows * part * tokens,
                                      bytes_accessed=32 * tokens * (rows + part),
                                      transcendentals=0),
        name="gradient",
    )(position, *[in_hbm(x) for x in turned], *acts, *kept)


def assemble_kernel(y_ref, *refs):
    out_ref = refs[-1]
    part = refs[0].shape[1]
    for d in range(4):
        q = lax.rem(y_ref[1] + 4 - d, 4)
        out_ref[:, pl.ds(pl.multiple_of(q * part, part), part)] = refs[d][...]


def assemble(y, parts):
    rows, part = parts[0].shape
    whole = lambda i: (0, 0)
    return pl.pallas_call(
        assemble_kernel,
        grid=(1,),
        in_specs=[pl.BlockSpec(memory_space=pltpu.SMEM)] + [pl.BlockSpec((rows, part), whole)] * 4,
        out_specs=pl.BlockSpec((rows, 4 * part), whole),
        out_shape=jax.ShapeDtypeStruct((rows, 4 * part), parts[0].dtype),
        compiler_params=pltpu.CompilerParams(vmem_limit_bytes=14 * 1024 * 1024),
        name="assemble",
    )(y, *parts)


def by_y(x, d):
    return lax.ppermute(x, "dp", [(i, (i + 4 * d) % 16) for i in range(16)])


def by_z(x):
    return lax.ppermute(x, "dp", [(i, i ^ 2) for i in range(16)])


def by_core(x):
    return lax.ppermute(x, "dp", [(i, i ^ 1) for i in range(16)])


def tied(values, after):
    *values, after = lax.optimization_barrier((*values, after))
    return values, after


def local(section_inputs, weights, norm_gains, upstream, edge_list, time_steps):
    section = lax.axis_index("pipe")
    sections = lax.axis_size("pipe")
    replica = lax.axis_index("dp")
    micros = section_inputs.shape[1]
    nodes = section_inputs.shape[2]
    width = section_inputs.shape[3]
    hidden = section_inputs[0]
    gates = timestep_gate(time_steps[:, 0], width)
    edges_t = jnp.swapaxes(edge_list[:, 0], 1, 2)
    position = jnp.stack([section, replica // 4, (replica // 2) % 2, replica % 2]).astype(jnp.int32)
    *state, wt, turned, grads, act = first(hidden, edges_t, gates, norm_gains, weights[0])

    def rest(turn, state):
        return second(turn, position, hidden, edges_t, gates, norm_gains, wt, turned,
                      state[:4], *state[4:])

    state = rest(1, state)
    slope, mixt, inv = state[4:]

    received = None
    ticks = sections + micros - 1
    for t in range(ticks):
        if t == ticks - 1:
            acts_last = last_act(position, received, slope, act)
            near_last = [acts_last[0]] + [by_y(acts_last[d], d) for d in range(1, 4)]
        sent, grads, act = tick(t, sections, position, received, upstream, slope, mixt, hidden, inv,
                                norm_gains, wt, grads, act)
        if t < ticks - 1:
            pairs = [(s, s - 1) for s in range(1, sections)
                     if 0 <= t - (sections - 1 - s) < micros]
            received = lax.ppermute(sent, "pipe", pairs)
        if t == 0:
            state = rest(0, state)
            own_own, own_far, far_own, far_far, slope, mixt, inv = state
            quad = [own_own, by_core(far_own), by_z(own_far), by_core(far_far)]
        if t == 1:
            (quad[1], quad[3]), received = tied((quad[1], quad[3]), received)
            quad[3] = by_z(quad[3])
            after = [by_y(quad[0], 1), by_y(quad[1], 1)]
            before = [by_y(quad[0], 3), by_y(quad[1], 3)]
        if t == 3:
            (quad[2], quad[3]), received = tied((quad[2], quad[3]), received)
            after += [by_y(quad[2], 1), by_y(quad[3], 1)]
            before += [by_y(quad[2], 3), by_y(quad[3], 3)]
        if t == 5:
            (after[0], after[1], before[2], before[3]), received = tied(
                (after[0], after[1], before[2], before[3]), received)
            opposite = [by_y(after[0], 1), by_y(after[1], 1), by_y(before[2], 3), by_y(before[3], 3)]
        if t == 7:
            opposite, received = tied(opposite, received)
        if t == ticks - 2:
            acts_head = head_acts(act)
            near_head = [acts_head[0]] + [by_y(acts_head[d], d) for d in range(1, 4)]

    def spread(near):
        across = [by_z(x) for x in near]
        return near + [by_core(x) for x in near] + across + [by_core(x) for x in across]

    lefts = [x for n in range(4) for x in (quad[n], after[n], opposite[n], before[n])]
    total, = gradient(position, lefts, spread(near_head), 0, None)
    near_last, sent = tied(near_last, sent)
    parts = gradient(position, lefts, spread(near_last), (micros - 1) * nodes, total)
    parts = [parts[0]] + [by_y(parts[d], d) for d in range(1, 4)]
    rows = assemble(position, parts)
    return (grads[None], rows[None])


def solution(mesh):
    in_specs = (
        P("pipe", None, "dp", None),
        P("pipe", None, None),
        P("pipe", None),
        P(None, "dp", None),
        P(None, "dp", None, None),
        P(None, "dp"),
    )
    out_specs = (P("pipe", None, "dp", None), P("pipe", "dp", None))
    return jax.shard_map(local, mesh=mesh, in_specs=in_specs, out_specs=out_specs, check_vma=False)
```

```python
import functools
import math

import jax
import jax.numpy as jnp
from jax import lax
from jax.experimental import pallas as pl
from jax.experimental.pallas import tpu as pltpu
from jax.sharding import PartitionSpec as P

NT = (((1,), (1,)), ((), ()))
BLOCK = 512
IN_VMEM = pl.BlockSpec(memory_space=pltpu.VMEM)
ANYWHERE = pl.BlockSpec(memory_space=pl.ANY)


def timestep_gate(time_steps, width):
    frequency = jnp.exp(-math.log(10000.0) * jnp.arange(width).astype(jnp.float32) / width)
    return 1.0 + 0.5 * jnp.sin(time_steps.astype(jnp.float32)[..., None] * frequency)


def in_hbm(x):
    return pltpu.with_memory_space_constraint(x, pltpu.HBM)


def held(x):
    return pltpu.with_memory_space_constraint(x, pltpu.VMEM)


def prepare(k, hidden_ref, edge_ref, gain_ref, mixt_ref, inv_ref, turned_s, at):
    nodes, width = hidden_ref.shape[1:]
    rows16 = width // 16
    edges = edge_ref.shape[2]
    ids = lax.broadcasted_iota(jnp.int32, (nodes, edges), 0)
    rows = lax.broadcasted_iota(jnp.int32, (nodes, nodes), 0)
    cols = lax.broadcasted_iota(jnp.int32, (nodes, nodes), 1)
    eye = jnp.where(rows == cols, 1.0, 0.0)
    src = jnp.where(edge_ref[k, 0:1, :] == ids, 1.0, 0.0).astype(jnp.bfloat16)
    tgt = jnp.where(edge_ref[k, 1:2, :] == ids, 1.0, 0.0).astype(jnp.bfloat16)
    adj = lax.dot_general(src, tgt, NT, preferred_element_type=jnp.float32)
    adj = adj + lax.dot_general(tgt, src, NT, preferred_element_type=jnp.float32) + eye
    mix = adj / jnp.sum(adj, axis=-1, keepdims=True)
    mixt_ref[k] = mix.T.astype(jnp.bfloat16)
    wide = hidden_ref[k].astype(jnp.float32)
    inv = lax.rsqrt(jnp.mean(wide * wide, axis=-1, keepdims=True) + 1e-06)
    inv_ref[k] = jnp.broadcast_to(inv, (nodes, 128))
    normed = (wide * inv * gain_ref[...]).astype(jnp.bfloat16)
    mixed = jnp.dot(mix.astype(jnp.bfloat16), normed, preferred_element_type=jnp.float32)
    mixed = mixed.astype(jnp.bfloat16)
    turned = mixed.T
    for q in range(16):
        place = q // 4
        turned_s[q % 4, place * rows16:(place + 1) * rows16, at:at + nodes] = (
            turned[q * rows16:(q + 1) * rows16, :])
    return mixed


def gated_slope(u, gate):
    logistic = jax.nn.sigmoid(u)
    return (logistic * (1.0 + u * (1.0 - logistic)) * gate).astype(jnp.bfloat16)


def first_kernel(hidden_ref, edge_ref, gate_ref, gain_ref, w_ref,
                 p0, p1, p2, p3, slope_ref, mixt_ref, inv_ref, wt_ref, turned_ref, grads_ref, act_ref,
                 mixed_s, w_s, sems):
    del p0, p1, p2, p3, grads_ref, act_ref
    micros, nodes, width = hidden_ref.shape
    blocks = width // BLOCK

    def fetch(j, slot):
        at = pl.ds(pl.multiple_of(j * BLOCK, BLOCK), BLOCK)
        return pltpu.make_async_copy(w_ref.at[:, at], w_s.at[slot], sems.at[slot])

    for n in range(2):
        fetch(n, n).start()
    mixed_s[...] = prepare(0, hidden_ref, edge_ref, gain_ref, mixt_ref, inv_ref, turned_ref, 0)

    @pl.loop(0, blocks)
    def _(j):
        slot = lax.rem(j, 2)
        fetch(j, slot).wait()
        at = pl.ds(pl.multiple_of(j * BLOCK, BLOCK), BLOCK)
        u = jnp.dot(mixed_s[...], w_s[slot], preferred_element_type=jnp.float32)
        wt_ref[at, :] = w_s[slot].T
        slope_ref[0, :, at] = gated_slope(u, gate_ref[0:1, at])

        @pl.when(j + 2 < blocks)
        def _():
            fetch(j + 2, slot).start()


def first(hidden, edges_t, gates, gain, weight):
    micros, nodes, width = hidden.shape
    piece = pltpu.HBM((width // 4, micros * nodes), jnp.bfloat16)
    return pl.pallas_call(
        first_kernel,
        in_specs=[IN_VMEM] * 4 + [ANYWHERE],
        out_specs=[ANYWHERE] * 4 + [IN_VMEM] * 5 + [ANYWHERE] * 2,
        out_shape=[
            piece, piece, piece, piece,
            pltpu.VMEM((micros, nodes, width), jnp.bfloat16),
            pltpu.VMEM((micros, nodes, nodes), jnp.bfloat16),
            pltpu.VMEM((micros, nodes, 128), jnp.float32),
            pltpu.VMEM((width, width), jnp.bfloat16),
            pltpu.VMEM((4, width // 4, nodes), jnp.bfloat16),
            pltpu.HBM((micros, nodes, width), jnp.bfloat16),
            pltpu.HBM((micros, 4, nodes, width // 4), jnp.bfloat16),
        ],
        scratch_shapes=[
            pltpu.VMEM((nodes, width), jnp.bfloat16),
            pltpu.VMEM((2, width, BLOCK), jnp.bfloat16),
            pltpu.SemaphoreType.DMA((2,)),
        ],
        compiler_params=pltpu.CompilerParams(vmem_limit_bytes=16 * 1024 * 1024),
        cost_estimate=pl.CostEstimate(
            flops=2 * nodes * width * width,
            bytes_accessed=2 * width * width + 10 * micros * nodes * width,
            transcendentals=nodes * width),
        name="first",
    )(held(hidden), held(edges_t), held(gates), held(gain), in_hbm(weight))


def second_kernel(turn, pos_ref, hidden_ref, edge_ref, gate_ref, gain_ref, wt_ref, turned_ref,
                  p0, p1, p2, p3, s0, m0, i0,
                  own_own, own_far, far_own, far_far, slope_ref, mixt_ref, inv_ref,
                  mixed_s, turned_s, sems):
    del p0, p1, p2, p3, s0, m0, i0
    micros, nodes, width = hidden_ref.shape
    z, core = pos_ref[2], pos_ref[3]

    @pl.when(core == turn)
    def _():
        for k in range(1, micros):
            mixed_s[(k - 1) * nodes:k * nodes, :] = prepare(
                k, hidden_ref, edge_ref, gain_ref, mixt_ref, inv_ref, turned_s, k * nodes)
        turned_s[:, :, 0:nodes] = turned_ref[...]
        copies = []
        for n, ref in enumerate((own_own, own_far, far_own, far_far)):
            place = lax.rem(z + n % 2, 2) * 2 + lax.rem(core + n // 2, 2)
            copies.append(pltpu.make_async_copy(turned_s.at[place], ref, sems.at[n]))
            copies[n].start()

        @pl.loop(0, width // BLOCK)
        def _(j):
            at = pl.ds(pl.multiple_of(j * BLOCK, BLOCK), BLOCK)
            u = lax.dot_general(mixed_s[...], wt_ref[at, :], NT, preferred_element_type=jnp.float32)
            for k in range(1, micros):
                slope_ref[k, :, at] = gated_slope(
                    u[(k - 1) * nodes:k * nodes, :], gate_ref[k:k + 1, at])

        for copy in copies:
            copy.wait()


def second(turn, position, hidden, edges_t, gates, gain, wt, turned, pieces, slope, mixt, inv):
    micros, nodes, width = hidden.shape
    kept = [in_hbm(x) for x in pieces] + [held(slope), held(mixt), held(inv)]
    specs = [ANYWHERE] * 4 + [IN_VMEM] * 3
    return pl.pallas_call(
        functools.partial(second_kernel, turn),
        in_specs=[pl.BlockSpec(memory_space=pltpu.SMEM)] + [IN_VMEM] * 6 + specs,
        out_specs=specs,
        out_shape=[pltpu.HBM(x.shape, x.dtype) for x in pieces]
        + [pltpu.VMEM(x.shape, x.dtype) for x in (slope, mixt, inv)],
        scratch_shapes=[
            pltpu.VMEM(((micros - 1) * nodes, width), jnp.bfloat16),
            pltpu.VMEM((4, width // 4, micros * nodes), jnp.bfloat16),
            pltpu.SemaphoreType.DMA((4,)),
        ],
        input_output_aliases={7 + n: n for n in range(7)},
        compiler_params=pltpu.CompilerParams(vmem_limit_bytes=16 * 1024 * 1024),
        cost_estimate=pl.CostEstimate(
            flops=2 * (micros - 1) * nodes * width * width,
            bytes_accessed=10 * micros * nodes * width,
            transcendentals=(micros - 1) * nodes * width),
        name="second",
    )(position, held(hidden), held(edges_t), held(gates), held(gain), held(wt), held(turned), *kept)


def put_columns(ref, act, y):
    part = ref.shape[2]
    for q in range(4):
        ref[lax.rem(q + 4 - y, 4)] = act[:, q * part:(q + 1) * part]


def tick_kernel(t, sections, sec_ref, *refs):
    if t < 3:
        up_ref, *refs = refs
    if t > 0:
        recv_ref, *refs = refs
    (slope_ref, mixt_ref, hidden_ref, inv_ref, gain_ref, wt_ref, grads_in, act_in,
     out_ref, grads_ref, act_ref, g_s, a_s, z_s, inner_s, h_s, act_s, sems) = refs
    del grads_in, act_in
    micros, nodes, width = hidden_ref.shape
    section = sec_ref[0]
    slot = t - (sections - 1 - section)
    last = section == sections - 1

    @pl.when(jnp.logical_and(slot >= 0, slot < micros))
    def _():
        fetch = pltpu.make_async_copy(hidden_ref.at[slot], h_s, sems.at[0])
        fetch.start()
        if t < micros:
            @pl.when(last)
            def _():
                copy = pltpu.make_async_copy(up_ref.at[t], out_ref.at[0], sems.at[1])
                copy.start()
                copy.wait()
                g_s[...] = out_ref[0].astype(jnp.float32)

            if t > 0:
                @pl.when(jnp.logical_not(last))
                def _():
                    g_s[...] = recv_ref[0].astype(jnp.float32)
        else:
            g_s[...] = recv_ref[0].astype(jnp.float32)
        act = (g_s[...] * slope_ref[slot].astype(jnp.float32)).astype(jnp.bfloat16)
        put_columns(act_s, act, sec_ref[1])
        keep_act = pltpu.make_async_copy(act_s, act_ref.at[slot], sems.at[2])
        keep_act.start()
        a_s[...] = jnp.dot(mixt_ref[slot], act, preferred_element_type=jnp.float32).astype(jnp.bfloat16)
        inner_s[...] = jnp.zeros_like(inner_s)
        fetch.wait()

        @pl.loop(0, width // BLOCK)
        def _(j):
            at = pl.ds(pl.multiple_of(j * BLOCK, BLOCK), BLOCK)
            z = jnp.dot(a_s[...], wt_ref[:, at], preferred_element_type=jnp.float32)
            z = z * gain_ref[:, at]
            z_s[:, at] = z
            part = jnp.sum(z * h_s[:, at].astype(jnp.float32), axis=-1, keepdims=True)
            inner_s[...] += jnp.broadcast_to(part, inner_s.shape)

        inv = inv_ref[slot, :, 0:1]
        scale = inv * inv * inv * (inner_s[:, 0:1] * (1.0 / width))
        grad = g_s[...] + inv * z_s[...] - h_s[...].astype(jnp.float32) * scale
        out_ref[0] = grad.astype(jnp.bfloat16)
        keep_grad = pltpu.make_async_copy(out_ref.at[0], grads_ref.at[slot], sems.at[3])
        keep_grad.start()
        keep_act.wait()
        keep_grad.wait()


def tick(t, sections, section, received, upstream, slope, mixt, hidden, inv, gain, wt, grads, act):
    micros, nodes, width = hidden.shape
    extra = [in_hbm(upstream)] if t < 3 else []
    taken = [held(received)] if t > 0 else []
    base = 7 + len(extra) + len(taken)
    return pl.pallas_call(
        functools.partial(tick_kernel, t, sections),
        in_specs=[pl.BlockSpec(memory_space=pltpu.SMEM)] + [ANYWHERE] * len(extra)
        + [IN_VMEM] * (2 + len(taken)) + [ANYWHERE] + [IN_VMEM] * 3 + [ANYWHERE] * 2,
        out_specs=[IN_VMEM, ANYWHERE, ANYWHERE],
        scratch_shapes=[
            pltpu.VMEM((nodes, width), jnp.float32),
            pltpu.VMEM((nodes, width), jnp.bfloat16),
            pltpu.VMEM((nodes, width), jnp.float32),
            pltpu.VMEM((nodes, 128), jnp.float32),
            pltpu.VMEM((nodes, width), jnp.bfloat16),
            pltpu.VMEM(act.shape[1:], jnp.bfloat16),
            pltpu.SemaphoreType.DMA((4,)),
        ],
        out_shape=[
            pltpu.VMEM((1, nodes, width), jnp.bfloat16),
            pltpu.HBM(grads.shape, grads.dtype),
            pltpu.HBM(act.shape, act.dtype),
        ],
        input_output_aliases={base: 1, base + 1: 2},
        compiler_params=pltpu.CompilerParams(vmem_limit_bytes=14 * 1024 * 1024),
        cost_estimate=pl.CostEstimate(
            flops=2 * nodes * width * width,
            bytes_accessed=2 * width * width + 12 * nodes * width,
            transcendentals=0),
        name="tick",
    )(section, *extra, *taken, held(slope), held(mixt), in_hbm(hidden), held(inv),
      held(gain), held(wt), in_hbm(grads), in_hbm(act))


def last_act_kernel(pos_ref, recv_ref, slope_ref, act_ref, *refs):
    outs, (act_s, sems) = refs[:4], refs[4:]
    micros = act_ref.shape[0]

    @pl.when(pos_ref[0] == 0)
    def _():
        act = recv_ref[0].astype(jnp.float32) * slope_ref[micros - 1].astype(jnp.float32)
        put_columns(act_s, act.astype(jnp.bfloat16), pos_ref[1])

    @pl.when(pos_ref[0] != 0)
    def _():
        copy = pltpu.make_async_copy(act_ref.at[micros - 1], act_s, sems.at[0])
        copy.start()
        copy.wait()

    for d in range(4):
        outs[d][...] = act_s[d]


def last_act(position, received, slope, act):
    micros, nodes, width = slope.shape
    return pl.pallas_call(
        last_act_kernel,
        in_specs=[pl.BlockSpec(memory_space=pltpu.SMEM), IN_VMEM, IN_VMEM, ANYWHERE],
        out_specs=[IN_VMEM] * 4,
        out_shape=[pltpu.VMEM((nodes, width // 4), jnp.bfloat16)] * 4,
        scratch_shapes=[pltpu.VMEM(act.shape[1:], jnp.bfloat16), pltpu.SemaphoreType.DMA((1,))],
        compiler_params=pltpu.CompilerParams(vmem_limit_bytes=14 * 1024 * 1024),
        cost_estimate=pl.CostEstimate(flops=nodes * width, bytes_accessed=8 * nodes * width,
                                      transcendentals=0),
        name="last_act",
    )(position, held(received), held(slope), in_hbm(act))


def pick_kernel(k, act_ref, *refs):
    outs, (act_s, sem) = refs[:4], refs[4:]
    copy = pltpu.make_async_copy(act_ref.at[k], act_s, sem)
    copy.start()
    copy.wait()
    for d in range(4):
        outs[d][...] = act_s[d]


def pick(k, act):
    micros, parts, nodes, part = act.shape
    return pl.pallas_call(
        functools.partial(pick_kernel, k),
        in_specs=[ANYWHERE],
        out_specs=[IN_VMEM] * 4,
        out_shape=[pltpu.VMEM((nodes, part), jnp.bfloat16)] * 4,
        scratch_shapes=[pltpu.VMEM(act.shape[1:], jnp.bfloat16), pltpu.SemaphoreType.DMA],
        compiler_params=pltpu.CompilerParams(vmem_limit_bytes=14 * 1024 * 1024),
        cost_estimate=pl.CostEstimate(flops=0, bytes_accessed=16 * nodes * part, transcendentals=0),
        name="pick",
    )(in_hbm(act))


def stack_kernel(*refs):
    out_ref = refs[-1]
    for d in range(4):
        out_ref[d] = refs[d][...]


def stack(parts):
    nodes, part = parts[0].shape
    return pl.pallas_call(
        stack_kernel,
        in_specs=[IN_VMEM] * 4,
        out_specs=IN_VMEM,
        out_shape=pltpu.VMEM((4, nodes, part), jnp.bfloat16),
        compiler_params=pltpu.CompilerParams(vmem_limit_bytes=14 * 1024 * 1024),
        cost_estimate=pl.CostEstimate(flops=0, bytes_accessed=16 * nodes * part, transcendentals=0),
        name="stack",
    )(*[held(x) for x in parts])


def gradient_kernel(groups, start, pos_ref, *refs):
    count = 16
    turned, acts, rest = refs[:count], refs[count:count + 4 * groups], refs[count + 4 * groups:]
    left_s, right_s, total_s, sems = rest[-4:]
    dots, rows, depth = left_s.shape
    nodes = acts[0].shape[1]
    tokens = nodes * groups
    each = depth // tokens
    copies = []
    for p in range(count):
        place, at = p // each, (p % each) * tokens
        batch = [pltpu.make_async_copy(turned[p].at[:, pl.ds(start, tokens)],
                                       left_s.at[place, :, pl.ds(at, tokens)], sems.at[0, p])]
        for g in range(groups):
            batch.append(pltpu.make_async_copy(
                acts[4 * g + p // 4].at[p % 4], right_s.at[place, pl.ds(at + g * nodes, nodes), :],
                sems.at[1 + g, p]))
        copies.append(batch)
        for copy in batch:
            copy.start()
    for n in range(dots):
        for p in range(n * each, (n + 1) * each):
            for copy in copies[p]:
                copy.wait()
        product = jnp.dot(left_s[n], right_s[n], preferred_element_type=jnp.float32)
        if n > 0:
            total_s[...] += product
        elif groups > 1:
            total_s[...] = product
        else:
            total_s[...] = rest[0][...] + product
    if groups > 1:
        rest[0][...] = total_s[...]
    else:
        block = rest[1].shape[0]
        for d in range(4):
            q = lax.rem(pos_ref[1] + d, 4)
            part = total_s[pl.ds(pl.multiple_of(q * block, block), block), :]
            rest[1 + d][...] = part.astype(jnp.bfloat16)


def gradient(position, turned, groups, start, total):
    rows = turned[0].shape[0]
    nodes, part = groups[0][0].shape[1:]
    tokens = nodes * len(groups)
    depth = 1024
    dots = 16 * tokens // depth
    if total is None:
        kept = []
        out_shape = [pltpu.VMEM((rows, part), jnp.float32)]
    else:
        kept = [held(total)]
        out_shape = [pltpu.VMEM((rows // 4, part), jnp.bfloat16)] * 4
    acts = [x for group in groups for x in group]
    return pl.pallas_call(
        functools.partial(gradient_kernel, len(groups), start),
        in_specs=[pl.BlockSpec(memory_space=pltpu.SMEM)] + [ANYWHERE] * (16 + len(acts))
        + [IN_VMEM] * len(kept),
        out_specs=[IN_VMEM] * len(out_shape),
        out_shape=out_shape,
        scratch_shapes=[
            pltpu.VMEM((dots, rows, depth), jnp.bfloat16),
            pltpu.VMEM((dots, depth, part), jnp.bfloat16),
            pltpu.VMEM((rows, part), jnp.float32),
            pltpu.SemaphoreType.DMA((3, 16)),
        ],
        compiler_params=pltpu.CompilerParams(
            vmem_limit_bytes=(18 if kept else 28) * 1024 * 1024),
        cost_estimate=pl.CostEstimate(flops=32 * rows * part * tokens,
                                      bytes_accessed=32 * tokens * (rows + part),
                                      transcendentals=0),
        name="gradient",
    )(position, *[in_hbm(x) for x in turned], *acts, *kept)


def assemble_kernel(y_ref, *refs):
    out_ref = refs[-1]
    part = refs[0].shape[1]
    for d in range(4):
        q = lax.rem(y_ref[1] + 4 - d, 4)
        out_ref[:, pl.ds(pl.multiple_of(q * part, part), part)] = refs[d][...]


def assemble(y, parts):
    rows, part = parts[0].shape
    whole = lambda i: (0, 0)
    return pl.pallas_call(
        assemble_kernel,
        grid=(1,),
        in_specs=[pl.BlockSpec(memory_space=pltpu.SMEM)] + [pl.BlockSpec((rows, part), whole)] * 4,
        out_specs=pl.BlockSpec((rows, 4 * part), whole),
        out_shape=jax.ShapeDtypeStruct((rows, 4 * part), parts[0].dtype),
        compiler_params=pltpu.CompilerParams(vmem_limit_bytes=14 * 1024 * 1024),
        name="assemble",
    )(y, *parts)


def by_y(x, d):
    return lax.ppermute(x, "dp", [(i, (i + 4 * d) % 16) for i in range(16)])


def by_z(x):
    return lax.ppermute(x, "dp", [(i, i ^ 2) for i in range(16)])


def by_core(x):
    return lax.ppermute(x, "dp", [(i, i ^ 1) for i in range(16)])


def tied(values, after):
    *values, after = lax.optimization_barrier((*values, after))
    return values, after


def local(section_inputs, weights, norm_gains, upstream, edge_list, time_steps):
    section = lax.axis_index("pipe")
    sections = lax.axis_size("pipe")
    replica = lax.axis_index("dp")
    micros = section_inputs.shape[1]
    nodes = section_inputs.shape[2]
    width = section_inputs.shape[3]
    hidden = section_inputs[0]
    gates = timestep_gate(time_steps[:, 0], width)
    edges_t = jnp.swapaxes(edge_list[:, 0], 1, 2)
    position = jnp.stack([section, replica // 4, (replica // 2) % 2, replica % 2]).astype(jnp.int32)
    *state, wt, turned, grads, act = first(hidden, edges_t, gates, norm_gains, weights[0])

    def rest(turn, state):
        return second(turn, position, hidden, edges_t, gates, norm_gains, wt, turned,
                      state[:4], *state[4:])

    state = rest(1, state)
    slope, mixt, inv = state[4:]

    def to_y(parts):
        return [parts[0]] + [by_y(parts[d], d) for d in range(1, 4)]

    received = None
    near = []
    after, before, opposite = [None] * 4, [None] * 4, [None] * 4
    ticks = sections + micros - 1
    for t in range(ticks):
        if t == ticks - 1:
            near.append(to_y(last_act(position, received, slope, act)))
        sent, grads, act = tick(t, sections, position, received, upstream, slope, mixt, hidden, inv,
                                norm_gains, wt, grads, act)
        if t == ticks - 1:
            break
        pairs = [(s, s - 1) for s in range(1, sections)
                 if 0 <= t - (sections - 1 - s) < micros]
        received = lax.ppermute(sent, "pipe", pairs)
        if t == 0:
            state = rest(0, state)
            own_own, own_far, far_own, far_far, slope, mixt, inv = state
            quad = [own_own, by_core(far_own), own_far, by_core(far_far)]
            after[0], before[0] = by_y(quad[0], 1), by_y(quad[0], 3)
            (quad[1], quad[3], after[0], before[0]), received = tied(
                (quad[1], quad[3], after[0], before[0]), received)
        if t == 1:
            after[1], before[1] = by_y(quad[1], 1), by_y(quad[1], 3)
            (after[1], before[1]), received = tied((after[1], before[1]), received)
        if t == 2:
            quad[2], opposite[0] = by_z(quad[2]), by_y(after[0], 1)
            (quad[2], opposite[0]), received = tied((quad[2], opposite[0]), received)
        if t == 3:
            quad[3], opposite[1] = by_z(quad[3]), by_y(after[1], 1)
            (quad[3], opposite[1]), received = tied((quad[3], opposite[1]), received)
        if t in (4, 5):
            n = t - 2
            after[n], before[n] = by_y(quad[n], 1), by_y(quad[n], 3)
            (after[n], before[n]), received = tied((after[n], before[n]), received)
        if t == 6:
            opposite[2], opposite[3] = by_y(after[2], 1), by_y(before[3], 3)
            (opposite[2], opposite[3]), received = tied((opposite[2], opposite[3]), received)
        if t in (7, 8):
            parts = to_y(pick(t - 7, act))
            parts, received = tied(parts, received)
            near.append(parts)

    groups = []
    for parts in near:
        mine = stack(parts)
        across = by_z(mine)
        groups.append([mine, by_core(mine), across, by_core(across)])
    lefts = [x for n in range(4) for x in (quad[n], after[n], opposite[n], before[n])]
    total, = gradient(position, lefts, groups[:2], 0, None)
    parts = gradient(position, lefts, groups[2:], (micros - 1) * nodes, total)
    rows = assemble(position, to_y(parts))
    return (grads[None], rows[None])


def solution(mesh):
    in_specs = (
        P("pipe", None, "dp", None),
        P("pipe", None, None),
        P("pipe", None),
        P(None, "dp", None),
        P(None, "dp", None, None),
        P(None, "dp"),
    )
    out_specs = (P("pipe", None, "dp", None), P("pipe", "dp", None))
    return jax.shard_map(local, mesh=mesh, in_specs=in_specs, out_specs=out_specs, check_vma=False)
```

```python
import functools
import math

import jax
import jax.numpy as jnp
from jax import lax
from jax.experimental import pallas as pl
from jax.experimental.pallas import tpu as pltpu
from jax.sharding import PartitionSpec as P

NT = (((1,), (1,)), ((), ()))
BLOCK = 512
IN_VMEM = pl.BlockSpec(memory_space=pltpu.VMEM)
ANYWHERE = pl.BlockSpec(memory_space=pl.ANY)
Y_GROUPS = [[4 * y + r for y in range(4)] for r in range(4)]


def timestep_gate(time_steps, width):
    frequency = jnp.exp(-math.log(10000.0) * jnp.arange(width).astype(jnp.float32) / width)
    return 1.0 + 0.5 * jnp.sin(time_steps.astype(jnp.float32)[..., None] * frequency)


def in_hbm(x):
    return pltpu.with_memory_space_constraint(x, pltpu.HBM)


def held(x):
    return pltpu.with_memory_space_constraint(x, pltpu.VMEM)


def prepare(k, hidden_ref, edge_ref, gain_ref, mixt_ref, inv_ref, turned_s):
    nodes, width = hidden_ref.shape[1:]
    rows16 = width // 16
    edges = edge_ref.shape[2]
    ids = lax.broadcasted_iota(jnp.int32, (nodes, edges), 0)
    rows = lax.broadcasted_iota(jnp.int32, (nodes, nodes), 0)
    cols = lax.broadcasted_iota(jnp.int32, (nodes, nodes), 1)
    eye = jnp.where(rows == cols, 1.0, 0.0)
    src = jnp.where(edge_ref[k, 0:1, :] == ids, 1.0, 0.0).astype(jnp.bfloat16)
    tgt = jnp.where(edge_ref[k, 1:2, :] == ids, 1.0, 0.0).astype(jnp.bfloat16)
    adj = lax.dot_general(src, tgt, NT, preferred_element_type=jnp.float32)
    adj = adj + lax.dot_general(tgt, src, NT, preferred_element_type=jnp.float32) + eye
    mix = adj / jnp.sum(adj, axis=-1, keepdims=True)
    mixt_ref[k] = mix.T.astype(jnp.bfloat16)
    wide = hidden_ref[k].astype(jnp.float32)
    inv = lax.rsqrt(jnp.mean(wide * wide, axis=-1, keepdims=True) + 1e-06)
    inv_ref[k] = jnp.broadcast_to(inv, (nodes, 128))
    normed = (wide * inv * gain_ref[...]).astype(jnp.bfloat16)
    mixed = jnp.dot(mix.astype(jnp.bfloat16), normed, preferred_element_type=jnp.float32)
    mixed = mixed.astype(jnp.bfloat16)
    turned = mixed.T
    for q in range(16):
        place = (q // 2) % 2 * 4 + q // 4
        turned_s[q % 2, k, place * rows16:(place + 1) * rows16, :] = (
            turned[q * rows16:(q + 1) * rows16, :])
    return mixed


def gated_slope(u, gate):
    logistic = jax.nn.sigmoid(u)
    return (logistic * (1.0 + u * (1.0 - logistic)) * gate).astype(jnp.bfloat16)


def first_kernel(hidden_ref, edge_ref, gate_ref, gain_ref, w_ref,
                 p0, p1, slope_ref, mixt_ref, inv_ref, wt_ref, turned_ref, grads_ref, act_ref,
                 mixed_s, w_s, sems):
    del p0, p1, grads_ref, act_ref
    micros, nodes, width = hidden_ref.shape
    blocks = width // BLOCK

    def fetch(j, slot):
        at = pl.ds(pl.multiple_of(j * BLOCK, BLOCK), BLOCK)
        return pltpu.make_async_copy(w_ref.at[:, at], w_s.at[slot], sems.at[slot])

    for n in range(2):
        fetch(n, n).start()
    mixed_s[...] = prepare(0, hidden_ref, edge_ref, gain_ref, mixt_ref, inv_ref, turned_ref)

    @pl.loop(0, blocks)
    def _(j):
        slot = lax.rem(j, 2)
        fetch(j, slot).wait()
        at = pl.ds(pl.multiple_of(j * BLOCK, BLOCK), BLOCK)
        u = jnp.dot(mixed_s[...], w_s[slot], preferred_element_type=jnp.float32)
        wt_ref[at, :] = w_s[slot].T
        slope_ref[0, :, at] = gated_slope(u, gate_ref[0:1, at])

        @pl.when(j + 2 < blocks)
        def _():
            fetch(j + 2, slot).start()


def first(hidden, edges_t, gates, gain, weight):
    micros, nodes, width = hidden.shape
    piece = pltpu.HBM((micros, width // 2, nodes), jnp.bfloat16)
    return pl.pallas_call(
        first_kernel,
        in_specs=[IN_VMEM] * 4 + [ANYWHERE],
        out_specs=[ANYWHERE] * 2 + [IN_VMEM] * 5 + [ANYWHERE] * 2,
        out_shape=[
            piece, piece,
            pltpu.VMEM((micros, nodes, width), jnp.bfloat16),
            pltpu.VMEM((micros, nodes, nodes), jnp.bfloat16),
            pltpu.VMEM((micros, nodes, 128), jnp.float32),
            pltpu.VMEM((width, width), jnp.bfloat16),
            pltpu.VMEM((2, 1, width // 2, nodes), jnp.bfloat16),
            pltpu.HBM((micros, nodes, width), jnp.bfloat16),
            pltpu.HBM((micros, 4, nodes, width // 4), jnp.bfloat16),
        ],
        scratch_shapes=[
            pltpu.VMEM((nodes, width), jnp.bfloat16),
            pltpu.VMEM((2, width, BLOCK), jnp.bfloat16),
            pltpu.SemaphoreType.DMA((2,)),
        ],
        compiler_params=pltpu.CompilerParams(vmem_limit_bytes=16 * 1024 * 1024),
        cost_estimate=pl.CostEstimate(
            flops=2 * nodes * width * width,
            bytes_accessed=2 * width * width + 10 * micros * nodes * width,
            transcendentals=nodes * width),
        name="first",
    )(held(hidden), held(edges_t), held(gates), held(gain), in_hbm(weight))


def second_kernel(turn, pos_ref, hidden_ref, edge_ref, gate_ref, gain_ref, wt_ref, turned_ref,
                  p0, p1, s0, m0, i0, own, far, slope_ref, mixt_ref, inv_ref,
                  mixed_s, turned_s, sems):
    del p0, p1, s0, m0, i0
    micros, nodes, width = hidden_ref.shape
    core = pos_ref[3]

    @pl.when(core == turn)
    def _():
        for k in range(1, micros):
            mixed_s[(k - 1) * nodes:k * nodes, :] = prepare(
                k, hidden_ref, edge_ref, gain_ref, mixt_ref, inv_ref, turned_s)
        turned_s[:, 0] = turned_ref[:, 0]
        copies = []
        for n, ref in enumerate((own, far)):
            copies.append(pltpu.make_async_copy(
                turned_s.at[lax.rem(core + n, 2)], ref, sems.at[n]))
            copies[n].start()

        @pl.loop(0, width // BLOCK)
        def _(j):
            at = pl.ds(pl.multiple_of(j * BLOCK, BLOCK), BLOCK)
            u = lax.dot_general(mixed_s[...], wt_ref[at, :], NT, preferred_element_type=jnp.float32)
            for k in range(1, micros):
                slope_ref[k, :, at] = gated_slope(
                    u[(k - 1) * nodes:k * nodes, :], gate_ref[k:k + 1, at])

        for copy in copies:
            copy.wait()


def second(turn, position, hidden, edges_t, gates, gain, wt, turned, pieces, slope, mixt, inv):
    micros, nodes, width = hidden.shape
    kept = [in_hbm(x) for x in pieces] + [held(slope), held(mixt), held(inv)]
    specs = [ANYWHERE] * 2 + [IN_VMEM] * 3
    return pl.pallas_call(
        functools.partial(second_kernel, turn),
        in_specs=[pl.BlockSpec(memory_space=pltpu.SMEM)] + [IN_VMEM] * 6 + specs,
        out_specs=specs,
        out_shape=[pltpu.HBM(x.shape, x.dtype) for x in pieces]
        + [pltpu.VMEM(x.shape, x.dtype) for x in (slope, mixt, inv)],
        scratch_shapes=[
            pltpu.VMEM(((micros - 1) * nodes, width), jnp.bfloat16),
            pltpu.VMEM((2, micros, width // 2, nodes), jnp.bfloat16),
            pltpu.SemaphoreType.DMA((2,)),
        ],
        input_output_aliases={7 + n: n for n in range(5)},
        compiler_params=pltpu.CompilerParams(vmem_limit_bytes=16 * 1024 * 1024),
        cost_estimate=pl.CostEstimate(
            flops=2 * (micros - 1) * nodes * width * width,
            bytes_accessed=10 * micros * nodes * width,
            transcendentals=(micros - 1) * nodes * width),
        name="second",
    )(position, held(hidden), held(edges_t), held(gates), held(gain), held(wt), held(turned), *kept)


def put_columns(ref, act, y):
    part = ref.shape[2]
    for q in range(4):
        ref[lax.rem(q + 4 - y, 4)] = act[:, q * part:(q + 1) * part]


def tick_kernel(t, sections, sec_ref, *refs):
    if t < 3:
        up_ref, *refs = refs
    if t > 0:
        recv_ref, *refs = refs
    if t == 1:
        refs = refs[:8] + refs[9:12] + refs[13:]
    (slope_ref, mixt_ref, hidden_ref, inv_ref, gain_ref, wt_ref, grads_in, act_in,
     out_ref, grads_ref, act_ref, g_s, a_s, z_s, inner_s, h_s, act_s, sems) = refs
    del grads_in, act_in
    micros, nodes, width = hidden_ref.shape
    section = sec_ref[0]
    slot = t - (sections - 1 - section)
    last = section == sections - 1

    @pl.when(jnp.logical_and(slot >= 0, slot < micros))
    def _():
        fetch = pltpu.make_async_copy(hidden_ref.at[slot], h_s, sems.at[0])
        fetch.start()
        if t < micros:
            @pl.when(last)
            def _():
                copy = pltpu.make_async_copy(up_ref.at[t], out_ref.at[0], sems.at[1])
                copy.start()
                copy.wait()
                g_s[...] = out_ref[0].astype(jnp.float32)

            if t > 0:
                @pl.when(jnp.logical_not(last))
                def _():
                    g_s[...] = recv_ref[0].astype(jnp.float32)
        else:
            g_s[...] = recv_ref[0].astype(jnp.float32)
        act = (g_s[...] * slope_ref[slot].astype(jnp.float32)).astype(jnp.bfloat16)
        put_columns(act_s, act, sec_ref[1])
        keep_act = pltpu.make_async_copy(act_s, act_ref.at[slot], sems.at[2])
        keep_act.start()
        a_s[...] = jnp.dot(mixt_ref[slot], act, preferred_element_type=jnp.float32).astype(jnp.bfloat16)
        inner_s[...] = jnp.zeros_like(inner_s)
        fetch.wait()

        @pl.loop(0, width // BLOCK)
        def _(j):
            at = pl.ds(pl.multiple_of(j * BLOCK, BLOCK), BLOCK)
            z = jnp.dot(a_s[...], wt_ref[:, at], preferred_element_type=jnp.float32)
            z = z * gain_ref[:, at]
            z_s[:, at] = z
            part = jnp.sum(z * h_s[:, at].astype(jnp.float32), axis=-1, keepdims=True)
            inner_s[...] += jnp.broadcast_to(part, inner_s.shape)

        inv = inv_ref[slot, :, 0:1]
        scale = inv * inv * inv * (inner_s[:, 0:1] * (1.0 / width))
        grad = g_s[...] + inv * z_s[...] - h_s[...].astype(jnp.float32) * scale
        out_ref[0] = grad.astype(jnp.bfloat16)
        keep_grad = pltpu.make_async_copy(out_ref.at[0], grads_ref.at[slot], sems.at[3])
        keep_grad.start()
        keep_act.wait()
        keep_grad.wait()


def tick(t, sections, section, received, upstream, slope, mixt, hidden, inv, gain, wt, grads, act,
         carried=()):
    micros, nodes, width = hidden.shape
    extra = [in_hbm(upstream)] if t < 3 else []
    taken = [held(received)] if t > 0 else []
    base = 7 + len(extra) + len(taken)
    return pl.pallas_call(
        functools.partial(tick_kernel, t, sections),
        in_specs=[pl.BlockSpec(memory_space=pltpu.SMEM)] + [ANYWHERE] * len(extra)
        + [IN_VMEM] * (2 + len(taken)) + [ANYWHERE] + [IN_VMEM] * 3 + [ANYWHERE] * (2 + len(carried)),
        out_specs=[IN_VMEM, ANYWHERE, ANYWHERE] + [ANYWHERE] * len(carried),
        scratch_shapes=[
            pltpu.VMEM((nodes, width), jnp.float32),
            pltpu.VMEM((nodes, width), jnp.bfloat16),
            pltpu.VMEM((nodes, width), jnp.float32),
            pltpu.VMEM((nodes, 128), jnp.float32),
            pltpu.VMEM((nodes, width), jnp.bfloat16),
            pltpu.VMEM(act.shape[1:], jnp.bfloat16),
            pltpu.SemaphoreType.DMA((4,)),
        ],
        out_shape=[
            pltpu.VMEM((1, nodes, width), jnp.bfloat16),
            pltpu.HBM(grads.shape, grads.dtype),
            pltpu.HBM(act.shape, act.dtype),
        ] + [pltpu.HBM(x.shape, x.dtype) for x in carried],
        input_output_aliases={base + n: 1 + n for n in range(2 + len(carried))},
        compiler_params=pltpu.CompilerParams(vmem_limit_bytes=14 * 1024 * 1024),
        cost_estimate=pl.CostEstimate(
            flops=2 * nodes * width * width,
            bytes_accessed=2 * width * width + 12 * nodes * width,
            transcendentals=0),
        name="tick",
    )(section, *extra, *taken, held(slope), held(mixt), in_hbm(hidden), held(inv),
      held(gain), held(wt), in_hbm(grads), in_hbm(act),
      *[in_hbm(x) for x in carried])


def last_act_kernel(pos_ref, recv_ref, slope_ref, act_ref, *refs):
    outs, (act_s, sems) = refs[:4], refs[4:]
    micros = act_ref.shape[0]

    @pl.when(pos_ref[0] == 0)
    def _():
        act = recv_ref[0].astype(jnp.float32) * slope_ref[micros - 1].astype(jnp.float32)
        put_columns(act_s, act.astype(jnp.bfloat16), pos_ref[1])

    @pl.when(pos_ref[0] != 0)
    def _():
        copy = pltpu.make_async_copy(act_ref.at[micros - 1], act_s, sems.at[0])
        copy.start()
        copy.wait()

    for d in range(4):
        outs[d][...] = act_s[d]


def last_act(position, received, slope, act):
    micros, nodes, width = slope.shape
    return pl.pallas_call(
        last_act_kernel,
        in_specs=[pl.BlockSpec(memory_space=pltpu.SMEM), IN_VMEM, IN_VMEM, ANYWHERE],
        out_specs=[IN_VMEM] * 4,
        out_shape=[pltpu.VMEM((nodes, width // 4), jnp.bfloat16)] * 4,
        scratch_shapes=[pltpu.VMEM(act.shape[1:], jnp.bfloat16), pltpu.SemaphoreType.DMA((1,))],
        compiler_params=pltpu.CompilerParams(vmem_limit_bytes=14 * 1024 * 1024),
        cost_estimate=pl.CostEstimate(flops=nodes * width, bytes_accessed=8 * nodes * width,
                                      transcendentals=0),
        name="last_act",
    )(position, held(received), held(slope), in_hbm(act))


def pick_kernel(k, act_ref, *refs):
    outs, (act_s, sem) = refs[:4], refs[4:]
    copy = pltpu.make_async_copy(act_ref.at[k], act_s, sem)
    copy.start()
    copy.wait()
    for d in range(4):
        outs[d][...] = act_s[d]


def pick(k, act):
    micros, parts, nodes, part = act.shape
    return pl.pallas_call(
        functools.partial(pick_kernel, k),
        in_specs=[ANYWHERE],
        out_specs=[IN_VMEM] * 4,
        out_shape=[pltpu.VMEM((nodes, part), jnp.bfloat16)] * 4,
        scratch_shapes=[pltpu.VMEM(act.shape[1:], jnp.bfloat16), pltpu.SemaphoreType.DMA],
        compiler_params=pltpu.CompilerParams(vmem_limit_bytes=14 * 1024 * 1024),
        cost_estimate=pl.CostEstimate(flops=0, bytes_accessed=16 * nodes * part, transcendentals=0),
        name="pick",
    )(in_hbm(act))


def stack_kernel(*refs):
    out_ref = refs[-1]
    for d in range(4):
        out_ref[d] = refs[d][...]


def stack(parts):
    nodes, part = parts[0].shape
    return pl.pallas_call(
        stack_kernel,
        in_specs=[IN_VMEM] * 4,
        out_specs=IN_VMEM,
        out_shape=pltpu.VMEM((4, nodes, part), jnp.bfloat16),
        compiler_params=pltpu.CompilerParams(vmem_limit_bytes=14 * 1024 * 1024),
        cost_estimate=pl.CostEstimate(flops=0, bytes_accessed=16 * nodes * part, transcendentals=0),
        name="stack",
    )(*[held(x) for x in parts])


def join_kernel(own_ref, in_ref, after_ref, out_ref, both_s, sems):
    del after_ref
    copies = [pltpu.make_async_copy(ref, both_s.at[n], sems.at[n])
              for n, ref in enumerate((own_ref, in_ref))]
    for copy in copies:
        copy.start()
    for copy in copies:
        copy.wait()
    copy = pltpu.make_async_copy(both_s, out_ref, sems.at[0])
    copy.start()
    copy.wait()


def join(own, received, after):
    shape = (2,) + own.shape
    return pl.pallas_call(
        join_kernel,
        in_specs=[ANYWHERE] * 2 + [IN_VMEM],
        out_specs=ANYWHERE,
        out_shape=pltpu.HBM(shape, own.dtype),
        scratch_shapes=[pltpu.VMEM(shape, own.dtype), pltpu.SemaphoreType.DMA((2,))],
        compiler_params=pltpu.CompilerParams(vmem_limit_bytes=14 * 1024 * 1024),
        cost_estimate=pl.CostEstimate(flops=0, bytes_accessed=8 * own.size, transcendentals=0),
        name="join",
    )(in_hbm(own), in_hbm(received), held(after))


def gradient_kernel(k, begin, end, pos_ref, left_ref, mine_ref, core_ref, *refs):
    if not begin:
        total_ref, *refs = refs
    *outs, left_s, total_s, sems = refs
    y, z = pos_ref[1], pos_ref[2]
    copies = []
    for p in range(8):
        source = lax.rem(y + 4 - p % 4, 4)
        copies.append(pltpu.make_async_copy(
            left_ref.at[source, p // 4, k], left_s.at[p], sems.at[p]))
        copies[p].start()
    for n, right_ref in enumerate((mine_ref, core_ref)):
        for p in range(4 * n, 4 * n + 4):
            copies[p].wait()
        left = jnp.concatenate([left_s[4 * n + d] for d in range(4)], axis=1)
        right = right_ref[...].reshape(left.shape[1], right_ref.shape[2])
        product = jnp.dot(left, right, preferred_element_type=jnp.float32)
        if n > 0:
            total_s[...] += product
        elif begin:
            total_s[...] = product
        else:
            total_s[...] = total_ref[...] + product
    if end:
        block = outs[0].shape[0]
        for half in range(2):
            for d in range(4):
                q = lax.rem(z + half, 2) * 4 + lax.rem(y + d, 4)
                part = total_s[pl.ds(pl.multiple_of(q * block, block), block), :]
                outs[half * 4 + d][...] = part.astype(jnp.bfloat16)
    else:
        outs[0][...] = total_s[...]


def gradient(k, position, lefts, mine, core, total, end):
    rows, nodes = lefts.shape[3:]
    part = mine.shape[2]
    kept = [] if total is None else [held(total)]
    if end:
        out_shape = [pltpu.VMEM((rows // 8, part), jnp.bfloat16)] * 8
    else:
        out_shape = [pltpu.VMEM((rows, part), jnp.float32)]
    return pl.pallas_call(
        functools.partial(gradient_kernel, k, total is None, end),
        in_specs=[pl.BlockSpec(memory_space=pltpu.SMEM), ANYWHERE] + [IN_VMEM] * (2 + len(kept)),
        out_specs=[IN_VMEM] * len(out_shape),
        out_shape=out_shape,
        scratch_shapes=[
            pltpu.VMEM((8, rows, nodes), jnp.bfloat16),
            pltpu.VMEM((rows, part), jnp.float32),
            pltpu.SemaphoreType.DMA((8,)),
        ],
        compiler_params=pltpu.CompilerParams(vmem_limit_bytes=20 * 1024 * 1024),
        cost_estimate=pl.CostEstimate(flops=16 * rows * part * nodes,
                                      bytes_accessed=16 * rows * nodes + 8 * rows * part,
                                      transcendentals=0),
        name="gradient",
    )(position, in_hbm(lefts), held(mine), held(core), *kept)


def assemble_kernel(pos_ref, *refs):
    out_ref = refs[-1]
    part = refs[0].shape[1]
    for d in range(4):
        q = lax.rem(pos_ref[1] + 4 - d, 4)
        both = refs[d][...].astype(jnp.float32) + refs[4 + d][...].astype(jnp.float32)
        out_ref[:, pl.ds(pl.multiple_of(q * part, part), part)] = both.astype(jnp.bfloat16)


def assemble(position, parts):
    rows, part = parts[0].shape
    return pl.pallas_call(
        assemble_kernel,
        in_specs=[pl.BlockSpec(memory_space=pltpu.SMEM)] + [IN_VMEM] * 8,
        out_specs=IN_VMEM,
        out_shape=jax.ShapeDtypeStruct((rows, 4 * part), parts[0].dtype),
        compiler_params=pltpu.CompilerParams(vmem_limit_bytes=14 * 1024 * 1024),
        name="assemble",
    )(position, *[held(x) for x in parts])


def by_y(x, d):
    return lax.ppermute(x, "dp", [(i, (i + 4 * d) % 16) for i in range(16)])


def by_y_and_z(x, d):
    return lax.ppermute(x, "dp", [(i, (i + 4 * d) % 16 ^ 2) for i in range(16)])


def by_core(x):
    return lax.ppermute(x, "dp", [(i, i ^ 1) for i in range(16)])


def tied(values, after):
    *values, after = lax.optimization_barrier((*values, after))
    return values, after


def local(section_inputs, weights, norm_gains, upstream, edge_list, time_steps):
    section = lax.axis_index("pipe")
    sections = lax.axis_size("pipe")
    replica = lax.axis_index("dp")
    micros = section_inputs.shape[1]
    nodes = section_inputs.shape[2]
    width = section_inputs.shape[3]
    hidden = section_inputs[0]
    gates = timestep_gate(time_steps[:, 0], width)
    edges_t = jnp.swapaxes(edge_list[:, 0], 1, 2)
    position = jnp.stack([section, replica // 4, (replica // 2) % 2, replica % 2]).astype(jnp.int32)
    *state, wt, turned, grads, act = first(hidden, edges_t, gates, norm_gains, weights[0])

    def rest(turn, state):
        return second(turn, position, hidden, edges_t, gates, norm_gains, wt, turned,
                      state[:2], *state[2:])

    state = rest(1, state)
    slope, mixt, inv = state[2:]

    def to_y(parts):
        return [parts[0]] + [by_y(parts[d], d) for d in range(1, 4)]

    received = None
    near = []
    ticks = sections + micros - 1
    for t in range(ticks):
        if t == ticks - 1:
            near.append(to_y(last_act(position, received, slope, act)))
        sent, grads, act, *carried = tick(
            t, sections, position, received, upstream, slope, mixt, hidden, inv, norm_gains, wt,
            grads, act, [far] if t == 1 else [])
        if t == ticks - 1:
            break
        pairs = [(s, s - 1) for s in range(1, sections)
                 if 0 <= t - (sections - 1 - s) < micros]
        received = lax.ppermute(sent, "pipe", pairs)
        if t == 0:
            state = rest(0, state)
            own, far, slope, mixt, inv = state
        if t == 1:
            far = by_core(carried[0])
        if t == 2:
            joined = join(own, far, sent)
            lefts = lax.all_gather(joined, "dp", axis_index_groups=Y_GROUPS)
        if t in (7, 8):
            parts = to_y(pick(t - 7, act))
            parts, received = tied(parts, received)
            near.append(parts)

    total = None
    for k in range(micros):
        mine = stack(near[k])
        total = gradient(k, position, lefts, mine, by_core(mine), total, k == micros - 1)
        if k < micros - 1:
            total, = total
    parts = to_y(total[:4]) + [by_y_and_z(total[4 + d], d) for d in range(4)]
    rows = assemble(position, parts)
    return (grads[None], rows[None])


def solution(mesh):
    in_specs = (
        P("pipe", None, "dp", None),
        P("pipe", None, None),
        P("pipe", None),
        P(None, "dp", None),
        P(None, "dp", None, None),
        P(None, "dp"),
    )
    out_specs = (P("pipe", None, "dp", None), P("pipe", "dp", None))
    return jax.shard_map(local, mesh=mesh, in_specs=in_specs, out_specs=out_specs, check_vma=False)
```

```python
import functools
import math

import jax
import jax.numpy as jnp
from jax import lax
from jax.experimental import pallas as pl
from jax.experimental.pallas import tpu as pltpu
from jax.sharding import PartitionSpec as P

NT = (((1,), (1,)), ((), ()))
BLOCK = 512
IN_VMEM = pl.BlockSpec(memory_space=pltpu.VMEM)
ANYWHERE = pl.BlockSpec(memory_space=pl.ANY)
Y_GROUPS = [[4 * y + r for y in range(4)] for r in range(4)]


def timestep_gate(time_steps, width):
    frequency = jnp.exp(-math.log(10000.0) * jnp.arange(width).astype(jnp.float32) / width)
    return 1.0 + 0.5 * jnp.sin(time_steps.astype(jnp.float32)[..., None] * frequency)


def in_hbm(x):
    return pltpu.with_memory_space_constraint(x, pltpu.HBM)


def held(x):
    return pltpu.with_memory_space_constraint(x, pltpu.VMEM)


def prepare(k, hidden_ref, edge_ref, gain_ref, mixt_ref, inv_ref, turned_s):
    nodes, width = hidden_ref.shape[1:]
    rows16 = width // 16
    edges = edge_ref.shape[2]
    ids = lax.broadcasted_iota(jnp.int32, (nodes, edges), 0)
    rows = lax.broadcasted_iota(jnp.int32, (nodes, nodes), 0)
    cols = lax.broadcasted_iota(jnp.int32, (nodes, nodes), 1)
    eye = jnp.where(rows == cols, 1.0, 0.0)
    src = jnp.where(edge_ref[k, 0:1, :] == ids, 1.0, 0.0).astype(jnp.bfloat16)
    tgt = jnp.where(edge_ref[k, 1:2, :] == ids, 1.0, 0.0).astype(jnp.bfloat16)
    adj = lax.dot_general(src, tgt, NT, preferred_element_type=jnp.float32)
    adj = adj + lax.dot_general(tgt, src, NT, preferred_element_type=jnp.float32) + eye
    mix = adj / jnp.sum(adj, axis=-1, keepdims=True)
    mixt_ref[k] = mix.T.astype(jnp.bfloat16)
    wide = hidden_ref[k].astype(jnp.float32)
    inv = lax.rsqrt(jnp.mean(wide * wide, axis=-1, keepdims=True) + 1e-06)
    inv_ref[k] = jnp.broadcast_to(inv, (nodes, 128))
    normed = (wide * inv * gain_ref[...]).astype(jnp.bfloat16)
    mixed = jnp.dot(mix.astype(jnp.bfloat16), normed, preferred_element_type=jnp.float32)
    mixed = mixed.astype(jnp.bfloat16)
    turned = mixed.T
    for q in range(16):
        place = (q // 2) % 2 * 4 + q // 4
        turned_s[q % 2, k, place * rows16:(place + 1) * rows16, :] = (
            turned[q * rows16:(q + 1) * rows16, :])
    return mixed


def gated_slope(u, gate):
    logistic = jax.nn.sigmoid(u)
    return (logistic * (1.0 + u * (1.0 - logistic)) * gate).astype(jnp.bfloat16)


def first_kernel(hidden_ref, edge_ref, gate_ref, gain_ref, w_ref,
                 p0, p1, p2, slope_ref, mixt_ref, inv_ref, wt_ref, turned_ref, grads_ref, act_ref,
                 mixed_s, w_s, sems):
    del p0, p1, p2, grads_ref, act_ref
    micros, nodes, width = hidden_ref.shape
    blocks = width // BLOCK

    def fetch(j, slot):
        at = pl.ds(pl.multiple_of(j * BLOCK, BLOCK), BLOCK)
        return pltpu.make_async_copy(w_ref.at[:, at], w_s.at[slot], sems.at[slot])

    for n in range(2):
        fetch(n, n).start()
    mixed_s[...] = prepare(0, hidden_ref, edge_ref, gain_ref, mixt_ref, inv_ref, turned_ref)

    @pl.loop(0, blocks)
    def _(j):
        slot = lax.rem(j, 2)
        fetch(j, slot).wait()
        at = pl.ds(pl.multiple_of(j * BLOCK, BLOCK), BLOCK)
        u = jnp.dot(mixed_s[...], w_s[slot], preferred_element_type=jnp.float32)
        wt_ref[at, :] = w_s[slot].T
        slope_ref[0, :, at] = gated_slope(u, gate_ref[0:1, at])

        @pl.when(j + 2 < blocks)
        def _():
            fetch(j + 2, slot).start()


def first(hidden, edges_t, gates, gain, weight):
    micros, nodes, width = hidden.shape
    piece = pltpu.HBM((micros, width // 2, nodes), jnp.bfloat16)
    return pl.pallas_call(
        first_kernel,
        in_specs=[IN_VMEM] * 4 + [ANYWHERE],
        out_specs=[ANYWHERE] * 3 + [IN_VMEM] * 5 + [ANYWHERE] * 2,
        out_shape=[
            piece, piece, pltpu.HBM((width, width), jnp.bfloat16),
            pltpu.VMEM((micros, nodes, width), jnp.bfloat16),
            pltpu.VMEM((micros, nodes, nodes), jnp.bfloat16),
            pltpu.VMEM((micros, nodes, 128), jnp.float32),
            pltpu.VMEM((width, width), jnp.bfloat16),
            pltpu.VMEM((2, 1, width // 2, nodes), jnp.bfloat16),
            pltpu.HBM((micros, nodes, width), jnp.bfloat16),
            pltpu.HBM((micros, 4, nodes, width // 4), jnp.bfloat16),
        ],
        scratch_shapes=[
            pltpu.VMEM((nodes, width), jnp.bfloat16),
            pltpu.VMEM((2, width, BLOCK), jnp.bfloat16),
            pltpu.SemaphoreType.DMA((2,)),
        ],
        compiler_params=pltpu.CompilerParams(vmem_limit_bytes=16 * 1024 * 1024),
        cost_estimate=pl.CostEstimate(
            flops=2 * nodes * width * width,
            bytes_accessed=2 * width * width + 10 * micros * nodes * width,
            transcendentals=nodes * width),
        name="first",
    )(held(hidden), held(edges_t), held(gates), held(gain), in_hbm(weight))


def second_kernel(turn, pos_ref, hidden_ref, edge_ref, gate_ref, gain_ref, wt_ref, turned_ref,
                  p0, p1, p2, s0, m0, i0, own, far, saved_ref, slope_ref, mixt_ref, inv_ref,
                  mixed_s, turned_s, sems):
    del p0, p1, p2, s0, m0, i0
    micros, nodes, width = hidden_ref.shape
    core = pos_ref[3]

    @pl.when(core == turn)
    def _():
        save = pltpu.make_async_copy(wt_ref, saved_ref, sems.at[2])
        save.start()
        for k in range(1, micros):
            mixed_s[(k - 1) * nodes:k * nodes, :] = prepare(
                k, hidden_ref, edge_ref, gain_ref, mixt_ref, inv_ref, turned_s)
        turned_s[:, 0] = turned_ref[:, 0]
        copies = []
        for n, ref in enumerate((own, far)):
            copies.append(pltpu.make_async_copy(
                turned_s.at[lax.rem(core + n, 2)], ref, sems.at[n]))
            copies[n].start()

        @pl.loop(0, width // BLOCK)
        def _(j):
            at = pl.ds(pl.multiple_of(j * BLOCK, BLOCK), BLOCK)
            u = lax.dot_general(mixed_s[...], wt_ref[at, :], NT, preferred_element_type=jnp.float32)
            for k in range(1, micros):
                slope_ref[k, :, at] = gated_slope(
                    u[(k - 1) * nodes:k * nodes, :], gate_ref[k:k + 1, at])

        for copy in copies:
            copy.wait()
        save.wait()


def second(turn, position, hidden, edges_t, gates, gain, wt, turned, pieces, slope, mixt, inv):
    micros, nodes, width = hidden.shape
    kept = [in_hbm(x) for x in pieces] + [held(slope), held(mixt), held(inv)]
    specs = [ANYWHERE] * 3 + [IN_VMEM] * 3
    return pl.pallas_call(
        functools.partial(second_kernel, turn),
        in_specs=[pl.BlockSpec(memory_space=pltpu.SMEM)] + [IN_VMEM] * 6 + specs,
        out_specs=specs,
        out_shape=[pltpu.HBM(x.shape, x.dtype) for x in pieces]
        + [pltpu.VMEM(x.shape, x.dtype) for x in (slope, mixt, inv)],
        scratch_shapes=[
            pltpu.VMEM(((micros - 1) * nodes, width), jnp.bfloat16),
            pltpu.VMEM((2, micros, width // 2, nodes), jnp.bfloat16),
            pltpu.SemaphoreType.DMA((3,)),
        ],
        input_output_aliases={7 + n: n for n in range(6)},
        compiler_params=pltpu.CompilerParams(vmem_limit_bytes=16 * 1024 * 1024),
        cost_estimate=pl.CostEstimate(
            flops=2 * (micros - 1) * nodes * width * width,
            bytes_accessed=10 * micros * nodes * width,
            transcendentals=(micros - 1) * nodes * width),
        name="second",
    )(position, held(hidden), held(edges_t), held(gates), held(gain), held(wt), held(turned), *kept)


def reload_kernel(saved_ref, after_ref, wt_ref, sems):
    del after_ref
    rows = wt_ref.shape[0] // 4
    copies = [pltpu.make_async_copy(saved_ref.at[pl.ds(n * rows, rows), :],
                                    wt_ref.at[pl.ds(n * rows, rows), :], sems.at[n])
              for n in range(4)]
    for copy in copies:
        copy.start()
    for copy in copies:
        copy.wait()


def reload(saved, after):
    return pl.pallas_call(
        reload_kernel,
        in_specs=[ANYWHERE] * 2,
        out_specs=IN_VMEM,
        out_shape=pltpu.VMEM(saved.shape, saved.dtype),
        scratch_shapes=[pltpu.SemaphoreType.DMA((4,))],
        compiler_params=pltpu.CompilerParams(vmem_limit_bytes=2 * 1024 * 1024),
        cost_estimate=pl.CostEstimate(flops=0, bytes_accessed=2 * saved.size, transcendentals=0),
        name="reload",
    )(in_hbm(saved), in_hbm(after))


def put_columns(ref, act, y):
    part = ref.shape[2]
    for q in range(4):
        ref[lax.rem(q + 4 - y, 4)] = act[:, q * part:(q + 1) * part]


def tick_kernel(t, sections, sec_ref, *refs):
    if t < 3:
        up_ref, *refs = refs
    if t > 0:
        recv_ref, *refs = refs
    if t == 1:
        refs = refs[:8] + refs[9:12] + refs[13:]
    (slope_ref, mixt_ref, hidden_ref, inv_ref, gain_ref, wt_ref, grads_in, act_in,
     out_ref, grads_ref, act_ref, g_s, a_s, z_s, inner_s, h_s, act_s, sems) = refs
    del grads_in, act_in
    micros, nodes, width = hidden_ref.shape
    section = sec_ref[0]
    slot = t - (sections - 1 - section)
    last = section == sections - 1

    @pl.when(jnp.logical_and(slot >= 0, slot < micros))
    def _():
        fetch = pltpu.make_async_copy(hidden_ref.at[slot], h_s, sems.at[0])
        fetch.start()
        if t < micros:
            @pl.when(last)
            def _():
                copy = pltpu.make_async_copy(up_ref.at[t], out_ref.at[0], sems.at[1])
                copy.start()
                copy.wait()
                g_s[...] = out_ref[0].astype(jnp.float32)

            if t > 0:
                @pl.when(jnp.logical_not(last))
                def _():
                    g_s[...] = recv_ref[0].astype(jnp.float32)
        else:
            g_s[...] = recv_ref[0].astype(jnp.float32)
        act = (g_s[...] * slope_ref[slot].astype(jnp.float32)).astype(jnp.bfloat16)
        put_columns(act_s, act, sec_ref[1])
        keep_act = pltpu.make_async_copy(act_s, act_ref.at[slot], sems.at[2])
        keep_act.start()
        a_s[...] = jnp.dot(mixt_ref[slot], act, preferred_element_type=jnp.float32).astype(jnp.bfloat16)
        inner_s[...] = jnp.zeros_like(inner_s)
        fetch.wait()

        @pl.loop(0, width // BLOCK)
        def _(j):
            at = pl.ds(pl.multiple_of(j * BLOCK, BLOCK), BLOCK)
            z = jnp.dot(a_s[...], wt_ref[:, at], preferred_element_type=jnp.float32)
            z = z * gain_ref[:, at]
            z_s[:, at] = z
            part = jnp.sum(z * h_s[:, at].astype(jnp.float32), axis=-1, keepdims=True)
            inner_s[...] += jnp.broadcast_to(part, inner_s.shape)

        inv = inv_ref[slot, :, 0:1]
        scale = inv * inv * inv * (inner_s[:, 0:1] * (1.0 / width))
        grad = g_s[...] + inv * z_s[...] - h_s[...].astype(jnp.float32) * scale
        out_ref[0] = grad.astype(jnp.bfloat16)
        keep_grad = pltpu.make_async_copy(out_ref.at[0], grads_ref.at[slot], sems.at[3])
        keep_grad.start()
        keep_act.wait()
        keep_grad.wait()


def tick(t, sections, section, received, upstream, slope, mixt, hidden, inv, gain, wt, grads, act,
         carried=()):
    micros, nodes, width = hidden.shape
    extra = [in_hbm(upstream)] if t < 3 else []
    taken = [held(received)] if t > 0 else []
    base = 7 + len(extra) + len(taken)
    return pl.pallas_call(
        functools.partial(tick_kernel, t, sections),
        in_specs=[pl.BlockSpec(memory_space=pltpu.SMEM)] + [ANYWHERE] * len(extra)
        + [IN_VMEM] * (2 + len(taken)) + [ANYWHERE] + [IN_VMEM] * 3 + [ANYWHERE] * (2 + len(carried)),
        out_specs=[IN_VMEM, ANYWHERE, ANYWHERE] + [ANYWHERE] * len(carried),
        scratch_shapes=[
            pltpu.VMEM((nodes, width), jnp.float32),
            pltpu.VMEM((nodes, width), jnp.bfloat16),
            pltpu.VMEM((nodes, width), jnp.float32),
            pltpu.VMEM((nodes, 128), jnp.float32),
            pltpu.VMEM((nodes, width), jnp.bfloat16),
            pltpu.VMEM(act.shape[1:], jnp.bfloat16),
            pltpu.SemaphoreType.DMA((4,)),
        ],
        out_shape=[
            pltpu.VMEM((1, nodes, width), jnp.bfloat16),
            pltpu.HBM(grads.shape, grads.dtype),
            pltpu.HBM(act.shape, act.dtype),
        ] + [pltpu.HBM(x.shape, x.dtype) for x in carried],
        input_output_aliases={base + n: 1 + n for n in range(2 + len(carried))},
        compiler_params=pltpu.CompilerParams(vmem_limit_bytes=14 * 1024 * 1024),
        cost_estimate=pl.CostEstimate(
            flops=2 * nodes * width * width,
            bytes_accessed=2 * width * width + 12 * nodes * width,
            transcendentals=0),
        name="tick",
    )(section, *extra, *taken, held(slope), held(mixt), in_hbm(hidden), held(inv),
      held(gain), held(wt), in_hbm(grads), in_hbm(act),
      *[in_hbm(x) for x in carried])


def last_act_kernel(pos_ref, recv_ref, slope_ref, act_ref, *refs):
    outs, (act_s, sems) = refs[:4], refs[4:]
    micros = act_ref.shape[0]

    @pl.when(pos_ref[0] == 0)
    def _():
        act = recv_ref[0].astype(jnp.float32) * slope_ref[micros - 1].astype(jnp.float32)
        put_columns(act_s, act.astype(jnp.bfloat16), pos_ref[1])

    @pl.when(pos_ref[0] != 0)
    def _():
        copy = pltpu.make_async_copy(act_ref.at[micros - 1], act_s, sems.at[0])
        copy.start()
        copy.wait()

    for d in range(4):
        outs[d][...] = act_s[d]


def last_act(position, received, slope, act):
    micros, nodes, width = slope.shape
    return pl.pallas_call(
        last_act_kernel,
        in_specs=[pl.BlockSpec(memory_space=pltpu.SMEM), IN_VMEM, IN_VMEM, ANYWHERE],
        out_specs=[IN_VMEM] * 4,
        out_shape=[pltpu.VMEM((nodes, width // 4), jnp.bfloat16)] * 4,
        scratch_shapes=[pltpu.VMEM(act.shape[1:], jnp.bfloat16), pltpu.SemaphoreType.DMA((1,))],
        compiler_params=pltpu.CompilerParams(vmem_limit_bytes=14 * 1024 * 1024),
        cost_estimate=pl.CostEstimate(flops=nodes * width, bytes_accessed=8 * nodes * width,
                                      transcendentals=0),
        name="last_act",
    )(position, held(received), held(slope), in_hbm(act))


def pick_kernel(k, act_ref, *refs):
    outs, (act_s, sem) = refs[:4], refs[4:]
    copy = pltpu.make_async_copy(act_ref.at[k], act_s, sem)
    copy.start()
    copy.wait()
    for d in range(4):
        outs[d][...] = act_s[d]


def pick(k, act):
    micros, parts, nodes, part = act.shape
    return pl.pallas_call(
        functools.partial(pick_kernel, k),
        in_specs=[ANYWHERE],
        out_specs=[IN_VMEM] * 4,
        out_shape=[pltpu.VMEM((nodes, part), jnp.bfloat16)] * 4,
        scratch_shapes=[pltpu.VMEM(act.shape[1:], jnp.bfloat16), pltpu.SemaphoreType.DMA],
        compiler_params=pltpu.CompilerParams(vmem_limit_bytes=14 * 1024 * 1024),
        cost_estimate=pl.CostEstimate(flops=0, bytes_accessed=16 * nodes * part, transcendentals=0),
        name="pick",
    )(in_hbm(act))


def stack_kernel(*refs):
    out_ref = refs[-1]
    for d in range(4):
        out_ref[d] = refs[d][...]


def stack(parts):
    nodes, part = parts[0].shape
    return pl.pallas_call(
        stack_kernel,
        in_specs=[IN_VMEM] * 4,
        out_specs=IN_VMEM,
        out_shape=pltpu.VMEM((4, nodes, part), jnp.bfloat16),
        compiler_params=pltpu.CompilerParams(vmem_limit_bytes=14 * 1024 * 1024),
        cost_estimate=pl.CostEstimate(flops=0, bytes_accessed=16 * nodes * part, transcendentals=0),
        name="stack",
    )(*[held(x) for x in parts])


def join_kernel(own_ref, in_ref, after_ref, out_ref, both_s, sems):
    del after_ref
    copies = [pltpu.make_async_copy(ref, both_s.at[n], sems.at[n])
              for n, ref in enumerate((own_ref, in_ref))]
    for copy in copies:
        copy.start()
    for copy in copies:
        copy.wait()
    copy = pltpu.make_async_copy(both_s, out_ref, sems.at[0])
    copy.start()
    copy.wait()


def join(own, received, after):
    shape = (2,) + own.shape
    return pl.pallas_call(
        join_kernel,
        in_specs=[ANYWHERE] * 2 + [IN_VMEM],
        out_specs=ANYWHERE,
        out_shape=pltpu.HBM(shape, own.dtype),
        scratch_shapes=[pltpu.VMEM(shape, own.dtype), pltpu.SemaphoreType.DMA((2,))],
        compiler_params=pltpu.CompilerParams(vmem_limit_bytes=14 * 1024 * 1024),
        cost_estimate=pl.CostEstimate(flops=0, bytes_accessed=8 * own.size, transcendentals=0),
        name="join",
    )(in_hbm(own), in_hbm(received), held(after))


def gradient_kernel(k, begin, half, pos_ref, left_ref, mine_ref, core_ref, *refs):
    if not begin:
        total_ref, *refs = refs
    *outs, left_s, total_s, sems = refs
    y, z = pos_ref[1], pos_ref[2]
    rows = left_s.shape[1]
    at = 0 if half is None else pl.multiple_of(lax.rem(z + half, 2) * rows, rows)
    copies = []
    for p in range(8):
        source = lax.rem(y + 4 - p % 4, 4)
        copies.append(pltpu.make_async_copy(
            left_ref.at[source, p // 4, k, pl.ds(at, rows), :], left_s.at[p], sems.at[p]))
        copies[p].start()
    for n, right_ref in enumerate((mine_ref, core_ref)):
        for p in range(4 * n, 4 * n + 4):
            copies[p].wait()
        left = jnp.concatenate([left_s[4 * n + d] for d in range(4)], axis=1)
        right = right_ref[...].reshape(left.shape[1], right_ref.shape[2])
        product = jnp.dot(left, right, preferred_element_type=jnp.float32)
        if n > 0:
            total_s[...] += product
        elif begin:
            total_s[...] = product
        else:
            total_s[...] = total_ref[pl.ds(at, rows), :] + product
    if half is None:
        outs[0][...] = total_s[...]
    else:
        block = outs[0].shape[0]
        for d in range(4):
            q = lax.rem(y + d, 4)
            part = total_s[pl.ds(pl.multiple_of(q * block, block), block), :]
            outs[d][...] = part.astype(jnp.bfloat16)


def gradient(k, position, lefts, mine, core, total, half=None):
    rows, nodes = lefts.shape[3:]
    part = mine.shape[2]
    kept = [] if total is None else [held(total)]
    if half is None:
        out_shape = [pltpu.VMEM((rows, part), jnp.float32)]
    else:
        out_shape = [pltpu.VMEM((rows // 8, part), jnp.bfloat16)] * 4
        rows = rows // 2
    return pl.pallas_call(
        functools.partial(gradient_kernel, k, total is None, half),
        in_specs=[pl.BlockSpec(memory_space=pltpu.SMEM), ANYWHERE] + [IN_VMEM] * (2 + len(kept)),
        out_specs=[IN_VMEM] * len(out_shape),
        out_shape=out_shape,
        scratch_shapes=[
            pltpu.VMEM((8, rows, nodes), jnp.bfloat16),
            pltpu.VMEM((rows, part), jnp.float32),
            pltpu.SemaphoreType.DMA((8,)),
        ],
        compiler_params=pltpu.CompilerParams(
            vmem_limit_bytes=(20 if half is None else 12) * 1024 * 1024),
        cost_estimate=pl.CostEstimate(flops=16 * rows * part * nodes,
                                      bytes_accessed=16 * rows * nodes + 8 * rows * part,
                                      transcendentals=0),
        name="gradient",
    )(position, in_hbm(lefts), held(mine), held(core), *kept)


def assemble_kernel(pos_ref, *refs):
    out_ref = refs[-1]
    part = refs[0].shape[1]
    for d in range(4):
        q = lax.rem(pos_ref[1] + 4 - d, 4)
        both = refs[d][...].astype(jnp.float32) + refs[4 + d][...].astype(jnp.float32)
        out_ref[:, pl.ds(pl.multiple_of(q * part, part), part)] = both.astype(jnp.bfloat16)


def assemble(position, parts):
    rows, part = parts[0].shape
    return pl.pallas_call(
        assemble_kernel,
        in_specs=[pl.BlockSpec(memory_space=pltpu.SMEM)] + [IN_VMEM] * 8,
        out_specs=IN_VMEM,
        out_shape=jax.ShapeDtypeStruct((rows, 4 * part), parts[0].dtype),
        compiler_params=pltpu.CompilerParams(vmem_limit_bytes=14 * 1024 * 1024),
        name="assemble",
    )(position, *[held(x) for x in parts])


def by_y(x, d):
    return lax.ppermute(x, "dp", [(i, (i + 4 * d) % 16) for i in range(16)])


def by_y_and_z(x, d):
    return lax.ppermute(x, "dp", [(i, (i + 4 * d) % 16 ^ 2) for i in range(16)])


def by_core(x):
    return lax.ppermute(x, "dp", [(i, i ^ 1) for i in range(16)])


def tied(values, after):
    *values, after = lax.optimization_barrier((*values, after))
    return values, after


def tied_list(values, others):
    both = lax.optimization_barrier((*values, *others))
    return both[:len(values)], list(both[len(values):])


def local(section_inputs, weights, norm_gains, upstream, edge_list, time_steps):
    section = lax.axis_index("pipe")
    sections = lax.axis_size("pipe")
    replica = lax.axis_index("dp")
    micros = section_inputs.shape[1]
    nodes = section_inputs.shape[2]
    width = section_inputs.shape[3]
    hidden = section_inputs[0]
    gates = timestep_gate(time_steps[:, 0], width)
    edges_t = jnp.swapaxes(edge_list[:, 0], 1, 2)
    position = jnp.stack([section, replica // 4, (replica // 2) % 2, replica % 2]).astype(jnp.int32)
    *state, wt, turned, grads, act = first(hidden, edges_t, gates, norm_gains, weights[0])

    def rest(turn, state):
        return second(turn, position, hidden, edges_t, gates, norm_gains, wt, turned,
                      state[:3], *state[3:])

    state = rest(1, state)
    slope, mixt, inv = state[3:]

    def to_y(parts):
        return [parts[0]] + [by_y(parts[d], d) for d in range(1, 4)]

    received = None
    near = []
    ticks = sections + micros - 1
    for t in range(ticks):
        if t == ticks - 1:
            near.append(to_y(last_act(position, received, slope, act)))
        sent, grads, act, *carried = tick(
            t, sections, position, received, upstream, slope, mixt, hidden, inv, norm_gains, wt,
            grads, act, [far] if t == 1 else [])
        if t == ticks - 1:
            break
        pairs = [(s, s - 1) for s in range(1, sections)
                 if 0 <= t - (sections - 1 - s) < micros]
        received = lax.ppermute(sent, "pipe", pairs)
        if t == 0:
            state = rest(0, state)
            own, far, saved, slope, mixt, inv = state
        if t == 1:
            far = by_core(carried[0])
        if t == 2:
            joined = join(own, far, sent)
            lefts = lax.all_gather(joined, "dp", axis_index_groups=Y_GROUPS)
            wt = reload(saved, joined)
        if t in (7, 8):
            mine = stack(to_y(pick(t - 7, act)))
            if t == 7:
                (mine,), received = tied((mine,), received)
            near.append(mine)
        if t == 8:
            total, = gradient(0, position, lefts, near[0], by_core(near[0]), None)
            (total, mine), received = tied((total, near[1]), received)
            near[1] = mine

    total, = gradient(1, position, lefts, near[1], by_core(near[1]), total)
    (total,), parts_last = tied_list((total,), near[2])
    mine = stack(parts_last)
    mine_core = by_core(mine)
    distant = gradient(micros - 1, position, lefts, mine, mine_core, total, 1)
    parts = [by_y_and_z(distant[d], d) for d in range(4)]
    local_parts = gradient(micros - 1, position, lefts, mine, mine_core, total, 0)
    rows = assemble(position, to_y(local_parts) + parts)
    return (grads[None], rows[None])


def solution(mesh):
    in_specs = (
        P("pipe", None, "dp", None),
        P("pipe", None, None),
        P("pipe", None),
        P(None, "dp", None),
        P(None, "dp", None, None),
        P(None, "dp"),
    )
    out_specs = (P("pipe", None, "dp", None), P("pipe", "dp", None))
    return jax.shard_map(local, mesh=mesh, in_specs=in_specs, out_specs=out_specs, check_vma=False)
```

```python
import functools
import math

import jax
import jax.numpy as jnp
from jax import lax
from jax.experimental import pallas as pl
from jax.experimental.pallas import tpu as pltpu
from jax.sharding import PartitionSpec as P

NT = (((1,), (1,)), ((), ()))
BLOCK = 512
IN_VMEM = pl.BlockSpec(memory_space=pltpu.VMEM)
ANYWHERE = pl.BlockSpec(memory_space=pl.ANY)
Y_GROUPS = [[4 * y + r for y in range(4)] for r in range(4)]


def timestep_gate(time_steps, width):
    frequency = jnp.exp(-math.log(10000.0) * jnp.arange(width).astype(jnp.float32) / width)
    return 1.0 + 0.5 * jnp.sin(time_steps.astype(jnp.float32)[..., None] * frequency)


def in_hbm(x):
    return pltpu.with_memory_space_constraint(x, pltpu.HBM)


def held(x):
    return pltpu.with_memory_space_constraint(x, pltpu.VMEM)


def prepare(k, hidden_ref, edge_ref, gain_ref, mixt_ref, inv_ref, turned_s):
    nodes, width = hidden_ref.shape[1:]
    rows16 = width // 16
    edges = edge_ref.shape[2]
    ids = lax.broadcasted_iota(jnp.int32, (nodes, edges), 0)
    rows = lax.broadcasted_iota(jnp.int32, (nodes, nodes), 0)
    cols = lax.broadcasted_iota(jnp.int32, (nodes, nodes), 1)
    eye = jnp.where(rows == cols, 1.0, 0.0)
    src = jnp.where(edge_ref[k, 0:1, :] == ids, 1.0, 0.0).astype(jnp.bfloat16)
    tgt = jnp.where(edge_ref[k, 1:2, :] == ids, 1.0, 0.0).astype(jnp.bfloat16)
    adj = lax.dot_general(src, tgt, NT, preferred_element_type=jnp.float32)
    adj = adj + lax.dot_general(tgt, src, NT, preferred_element_type=jnp.float32) + eye
    mix = adj / jnp.sum(adj, axis=-1, keepdims=True)
    mixt_ref[k] = mix.T.astype(jnp.bfloat16)
    wide = hidden_ref[k].astype(jnp.float32)
    inv = lax.rsqrt(jnp.mean(wide * wide, axis=-1, keepdims=True) + 1e-06)
    inv_ref[k] = jnp.broadcast_to(inv, (nodes, 128))
    normed = (wide * inv * gain_ref[...]).astype(jnp.bfloat16)
    mixed = jnp.dot(mix.astype(jnp.bfloat16), normed, preferred_element_type=jnp.float32)
    mixed = mixed.astype(jnp.bfloat16)
    turned = mixed.T
    for q in range(16):
        place = (q // 2) % 2 * 4 + q // 4
        turned_s[q % 2, k, place * rows16:(place + 1) * rows16, :] = (
            turned[q * rows16:(q + 1) * rows16, :])
    return mixed


def gated_slope(u, gate):
    logistic = jax.nn.sigmoid(u)
    return (logistic * (1.0 + u * (1.0 - logistic)) * gate).astype(jnp.bfloat16)


def first_kernel(hidden_ref, edge_ref, gate_ref, gain_ref, w_ref,
                 p0, p2, slope_ref, mixt_ref, inv_ref, wt_ref, turned_ref, grads_ref, act_ref,
                 mixed_s, w_s, sems):
    del p0, p2, grads_ref, act_ref
    micros, nodes, width = hidden_ref.shape
    blocks = width // BLOCK

    def fetch(j, slot):
        at = pl.ds(pl.multiple_of(j * BLOCK, BLOCK), BLOCK)
        return pltpu.make_async_copy(w_ref.at[:, at], w_s.at[slot], sems.at[slot])

    for n in range(2):
        fetch(n, n).start()
    mixed_s[...] = prepare(0, hidden_ref, edge_ref, gain_ref, mixt_ref, inv_ref, turned_ref)

    @pl.loop(0, blocks)
    def _(j):
        slot = lax.rem(j, 2)
        fetch(j, slot).wait()
        at = pl.ds(pl.multiple_of(j * BLOCK, BLOCK), BLOCK)
        u = jnp.dot(mixed_s[...], w_s[slot], preferred_element_type=jnp.float32)
        wt_ref[at, :] = w_s[slot].T
        slope_ref[0, :, at] = gated_slope(u, gate_ref[0:1, at])

        @pl.when(j + 2 < blocks)
        def _():
            fetch(j + 2, slot).start()


def first(hidden, edges_t, gates, gain, weight):
    micros, nodes, width = hidden.shape
    piece = pltpu.HBM((2, micros, width // 2, nodes), jnp.bfloat16)
    return pl.pallas_call(
        first_kernel,
        in_specs=[IN_VMEM] * 4 + [ANYWHERE],
        out_specs=[ANYWHERE] * 2 + [IN_VMEM] * 5 + [ANYWHERE] * 2,
        out_shape=[
            piece, pltpu.HBM((width, width), jnp.bfloat16),
            pltpu.VMEM((micros, nodes, width), jnp.bfloat16),
            pltpu.VMEM((micros, nodes, nodes), jnp.bfloat16),
            pltpu.VMEM((micros, nodes, 128), jnp.float32),
            pltpu.VMEM((width, width), jnp.bfloat16),
            pltpu.VMEM((2, 1, width // 2, nodes), jnp.bfloat16),
            pltpu.HBM((micros, nodes, width), jnp.bfloat16),
            pltpu.HBM((micros, 4, nodes, width // 4), jnp.bfloat16),
        ],
        scratch_shapes=[
            pltpu.VMEM((nodes, width), jnp.bfloat16),
            pltpu.VMEM((2, width, BLOCK), jnp.bfloat16),
            pltpu.SemaphoreType.DMA((2,)),
        ],
        compiler_params=pltpu.CompilerParams(vmem_limit_bytes=16 * 1024 * 1024),
        cost_estimate=pl.CostEstimate(
            flops=2 * nodes * width * width,
            bytes_accessed=2 * width * width + 10 * micros * nodes * width,
            transcendentals=nodes * width),
        name="first",
    )(held(hidden), held(edges_t), held(gates), held(gain), in_hbm(weight))


def second_kernel(turn, pos_ref, hidden_ref, edge_ref, gate_ref, gain_ref, wt_ref, turned_ref,
                  p0, p2, s0, m0, i0, whole_ref, saved_ref, slope_ref, mixt_ref, inv_ref,
                  mixed_s, turned_s, sems):
    del p0, p2, s0, m0, i0
    micros, nodes, width = hidden_ref.shape
    core = pos_ref[3]

    @pl.when(core == turn)
    def _():
        save = pltpu.make_async_copy(wt_ref, saved_ref, sems.at[2])
        save.start()
        for k in range(1, micros):
            mixed_s[(k - 1) * nodes:k * nodes, :] = prepare(
                k, hidden_ref, edge_ref, gain_ref, mixt_ref, inv_ref, turned_s)
        turned_s[:, 0] = turned_ref[:, 0]
        keep = pltpu.make_async_copy(turned_s, whole_ref, sems.at[0])
        keep.start()

        @pl.loop(0, width // BLOCK)
        def _(j):
            at = pl.ds(pl.multiple_of(j * BLOCK, BLOCK), BLOCK)
            u = lax.dot_general(mixed_s[...], wt_ref[at, :], NT, preferred_element_type=jnp.float32)
            for k in range(1, micros):
                slope_ref[k, :, at] = gated_slope(
                    u[(k - 1) * nodes:k * nodes, :], gate_ref[k:k + 1, at])

        keep.wait()
        save.wait()


def second(turn, position, hidden, edges_t, gates, gain, wt, turned, pieces, slope, mixt, inv):
    micros, nodes, width = hidden.shape
    kept = [in_hbm(x) for x in pieces] + [held(slope), held(mixt), held(inv)]
    specs = [ANYWHERE] * 2 + [IN_VMEM] * 3
    return pl.pallas_call(
        functools.partial(second_kernel, turn),
        in_specs=[pl.BlockSpec(memory_space=pltpu.SMEM)] + [IN_VMEM] * 6 + specs,
        out_specs=specs,
        out_shape=[pltpu.HBM(x.shape, x.dtype) for x in pieces]
        + [pltpu.VMEM(x.shape, x.dtype) for x in (slope, mixt, inv)],
        scratch_shapes=[
            pltpu.VMEM(((micros - 1) * nodes, width), jnp.bfloat16),
            pltpu.VMEM((2, micros, width // 2, nodes), jnp.bfloat16),
            pltpu.SemaphoreType.DMA((3,)),
        ],
        input_output_aliases={7 + n: n for n in range(5)},
        compiler_params=pltpu.CompilerParams(vmem_limit_bytes=16 * 1024 * 1024),
        cost_estimate=pl.CostEstimate(
            flops=2 * (micros - 1) * nodes * width * width,
            bytes_accessed=10 * micros * nodes * width,
            transcendentals=(micros - 1) * nodes * width),
        name="second",
    )(position, held(hidden), held(edges_t), held(gates), held(gain), held(wt), held(turned), *kept)


def reload_kernel(saved_ref, after_ref, wt_ref, sems):
    del after_ref
    rows = wt_ref.shape[0] // 4
    copies = [pltpu.make_async_copy(saved_ref.at[pl.ds(n * rows, rows), :],
                                    wt_ref.at[pl.ds(n * rows, rows), :], sems.at[n])
              for n in range(4)]
    for copy in copies:
        copy.start()
    for copy in copies:
        copy.wait()


def reload(saved, after):
    return pl.pallas_call(
        reload_kernel,
        in_specs=[ANYWHERE] * 2,
        out_specs=IN_VMEM,
        out_shape=pltpu.VMEM(saved.shape, saved.dtype),
        scratch_shapes=[pltpu.SemaphoreType.DMA((4,))],
        compiler_params=pltpu.CompilerParams(vmem_limit_bytes=2 * 1024 * 1024),
        cost_estimate=pl.CostEstimate(flops=0, bytes_accessed=2 * saved.size, transcendentals=0),
        name="reload",
    )(in_hbm(saved), in_hbm(after))


def put_columns(ref, act, y):
    part = ref.shape[2]
    for q in range(4):
        ref[lax.rem(q + 4 - y, 4)] = act[:, q * part:(q + 1) * part]


def tick_kernel(t, sections, sec_ref, *refs):
    if t < 3:
        up_ref, *refs = refs
    if t > 0:
        recv_ref, *refs = refs
    if t == 1:
        refs = refs[:8] + refs[9:12] + refs[13:]
    (slope_ref, mixt_ref, hidden_ref, inv_ref, gain_ref, wt_ref, grads_in, act_in,
     out_ref, grads_ref, act_ref, g_s, a_s, z_s, inner_s, h_s, act_s, sems) = refs
    del grads_in, act_in
    micros, nodes, width = hidden_ref.shape
    section = sec_ref[0]
    slot = t - (sections - 1 - section)
    last = section == sections - 1

    @pl.when(jnp.logical_and(slot >= 0, slot < micros))
    def _():
        fetch = pltpu.make_async_copy(hidden_ref.at[slot], h_s, sems.at[0])
        fetch.start()
        if t < micros:
            @pl.when(last)
            def _():
                copy = pltpu.make_async_copy(up_ref.at[t], out_ref.at[0], sems.at[1])
                copy.start()
                copy.wait()
                g_s[...] = out_ref[0].astype(jnp.float32)

            if t > 0:
                @pl.when(jnp.logical_not(last))
                def _():
                    g_s[...] = recv_ref[0].astype(jnp.float32)
        else:
            g_s[...] = recv_ref[0].astype(jnp.float32)
        act = (g_s[...] * slope_ref[slot].astype(jnp.float32)).astype(jnp.bfloat16)
        put_columns(act_s, act, sec_ref[1])
        keep_act = pltpu.make_async_copy(act_s, act_ref.at[slot], sems.at[2])
        keep_act.start()
        a_s[...] = jnp.dot(mixt_ref[slot], act, preferred_element_type=jnp.float32).astype(jnp.bfloat16)
        inner_s[...] = jnp.zeros_like(inner_s)
        fetch.wait()

        @pl.loop(0, width // BLOCK)
        def _(j):
            at = pl.ds(pl.multiple_of(j * BLOCK, BLOCK), BLOCK)
            z = jnp.dot(a_s[...], wt_ref[:, at], preferred_element_type=jnp.float32)
            z = z * gain_ref[:, at]
            z_s[:, at] = z
            part = jnp.sum(z * h_s[:, at].astype(jnp.float32), axis=-1, keepdims=True)
            inner_s[...] += jnp.broadcast_to(part, inner_s.shape)

        inv = inv_ref[slot, :, 0:1]
        scale = inv * inv * inv * (inner_s[:, 0:1] * (1.0 / width))
        grad = g_s[...] + inv * z_s[...] - h_s[...].astype(jnp.float32) * scale
        out_ref[0] = grad.astype(jnp.bfloat16)
        keep_grad = pltpu.make_async_copy(out_ref.at[0], grads_ref.at[slot], sems.at[3])
        keep_grad.start()
        keep_act.wait()
        keep_grad.wait()


def tick(t, sections, section, received, upstream, slope, mixt, hidden, inv, gain, wt, grads, act,
         carried=()):
    micros, nodes, width = hidden.shape
    extra = [in_hbm(upstream)] if t < 3 else []
    taken = [held(received)] if t > 0 else []
    base = 7 + len(extra) + len(taken)
    return pl.pallas_call(
        functools.partial(tick_kernel, t, sections),
        in_specs=[pl.BlockSpec(memory_space=pltpu.SMEM)] + [ANYWHERE] * len(extra)
        + [IN_VMEM] * (2 + len(taken)) + [ANYWHERE] + [IN_VMEM] * 3 + [ANYWHERE] * (2 + len(carried)),
        out_specs=[IN_VMEM, ANYWHERE, ANYWHERE] + [ANYWHERE] * len(carried),
        scratch_shapes=[
            pltpu.VMEM((nodes, width), jnp.float32),
            pltpu.VMEM((nodes, width), jnp.bfloat16),
            pltpu.VMEM((nodes, width), jnp.float32),
            pltpu.VMEM((nodes, 128), jnp.float32),
            pltpu.VMEM((nodes, width), jnp.bfloat16),
            pltpu.VMEM(act.shape[1:], jnp.bfloat16),
            pltpu.SemaphoreType.DMA((4,)),
        ],
        out_shape=[
            pltpu.VMEM((1, nodes, width), jnp.bfloat16),
            pltpu.HBM(grads.shape, grads.dtype),
            pltpu.HBM(act.shape, act.dtype),
        ] + [pltpu.HBM(x.shape, x.dtype) for x in carried],
        input_output_aliases={base + n: 1 + n for n in range(2 + len(carried))},
        compiler_params=pltpu.CompilerParams(vmem_limit_bytes=14 * 1024 * 1024),
        cost_estimate=pl.CostEstimate(
            flops=2 * nodes * width * width,
            bytes_accessed=2 * width * width + 12 * nodes * width,
            transcendentals=0),
        name="tick",
    )(section, *extra, *taken, held(slope), held(mixt), in_hbm(hidden), held(inv),
      held(gain), held(wt), in_hbm(grads), in_hbm(act),
      *[in_hbm(x) for x in carried])


def last_act_kernel(pos_ref, recv_ref, slope_ref, act_ref, *refs):
    outs, (act_s, sems) = refs[:4], refs[4:]
    micros = act_ref.shape[0]

    @pl.when(pos_ref[0] == 0)
    def _():
        act = recv_ref[0].astype(jnp.float32) * slope_ref[micros - 1].astype(jnp.float32)
        put_columns(act_s, act.astype(jnp.bfloat16), pos_ref[1])

    @pl.when(pos_ref[0] != 0)
    def _():
        copy = pltpu.make_async_copy(act_ref.at[micros - 1], act_s, sems.at[0])
        copy.start()
        copy.wait()

    for d in range(4):
        outs[d][...] = act_s[d]


def last_act(position, received, slope, act):
    micros, nodes, width = slope.shape
    return pl.pallas_call(
        last_act_kernel,
        in_specs=[pl.BlockSpec(memory_space=pltpu.SMEM), IN_VMEM, IN_VMEM, ANYWHERE],
        out_specs=[IN_VMEM] * 4,
        out_shape=[pltpu.VMEM((nodes, width // 4), jnp.bfloat16)] * 4,
        scratch_shapes=[pltpu.VMEM(act.shape[1:], jnp.bfloat16), pltpu.SemaphoreType.DMA((1,))],
        compiler_params=pltpu.CompilerParams(vmem_limit_bytes=14 * 1024 * 1024),
        cost_estimate=pl.CostEstimate(flops=nodes * width, bytes_accessed=8 * nodes * width,
                                      transcendentals=0),
        name="last_act",
    )(position, held(received), held(slope), in_hbm(act))


def pick_kernel(k, act_ref, *refs):
    outs, (act_s, sem) = refs[:4], refs[4:]
    copy = pltpu.make_async_copy(act_ref.at[k], act_s, sem)
    copy.start()
    copy.wait()
    for d in range(4):
        outs[d][...] = act_s[d]


def pick(k, act):
    micros, parts, nodes, part = act.shape
    return pl.pallas_call(
        functools.partial(pick_kernel, k),
        in_specs=[ANYWHERE],
        out_specs=[IN_VMEM] * 4,
        out_shape=[pltpu.VMEM((nodes, part), jnp.bfloat16)] * 4,
        scratch_shapes=[pltpu.VMEM(act.shape[1:], jnp.bfloat16), pltpu.SemaphoreType.DMA],
        compiler_params=pltpu.CompilerParams(vmem_limit_bytes=14 * 1024 * 1024),
        cost_estimate=pl.CostEstimate(flops=0, bytes_accessed=16 * nodes * part, transcendentals=0),
        name="pick",
    )(in_hbm(act))


def stack_kernel(*refs):
    out_ref = refs[-1]
    for d in range(4):
        out_ref[d] = refs[d][...]


def stack(parts):
    nodes, part = parts[0].shape
    return pl.pallas_call(
        stack_kernel,
        in_specs=[IN_VMEM] * 4,
        out_specs=IN_VMEM,
        out_shape=pltpu.VMEM((4, nodes, part), jnp.bfloat16),
        compiler_params=pltpu.CompilerParams(vmem_limit_bytes=14 * 1024 * 1024),
        cost_estimate=pl.CostEstimate(flops=0, bytes_accessed=16 * nodes * part, transcendentals=0),
        name="stack",
    )(*[held(x) for x in parts])


def gradient_kernel(k, begin, half, pos_ref, left_ref, mine_ref, *refs):
    if not begin:
        total_ref, *refs = refs
    out_ref, left_s, sems = refs
    y, core = pos_ref[1], pos_ref[3]
    halves = [0, 1] if half is None else [lax.rem(core + half, 2)]
    rows = left_s.shape[2]
    right = mine_ref[...].reshape(4 * mine_ref.shape[1], mine_ref.shape[2])
    copies = []
    for n, which in enumerate(halves):
        copies.append([])
        for d in range(4):
            source = lax.rem(y + 4 - d, 4)
            copies[n].append(pltpu.make_async_copy(
                left_ref.at[source, which, k], left_s.at[n, d], sems.at[n, d]))
            copies[n][d].start()
    for n, which in enumerate(halves):
        for copy in copies[n]:
            copy.wait()
        left = jnp.concatenate([left_s[n, d] for d in range(4)], axis=1)
        product = jnp.dot(left, right, preferred_element_type=jnp.float32)
        if not begin:
            product = product + total_ref[which]
        if half is None:
            out_ref[which] = product
        else:
            out_ref[...] = product.astype(out_ref.dtype)


def gradient(k, position, lefts, mine, total, half=None):
    rows, nodes = lefts.shape[3:]
    part = mine.shape[2]
    kept = [] if total is None else [held(total)]
    if half is None:
        count, out_shape = 2, pltpu.VMEM((2, rows, part), jnp.float32)
    else:
        count = 1
        out_shape = pltpu.VMEM((rows, part), jnp.bfloat16 if half else jnp.float32)
    return pl.pallas_call(
        functools.partial(gradient_kernel, k, total is None, half),
        in_specs=[pl.BlockSpec(memory_space=pltpu.SMEM), ANYWHERE] + [IN_VMEM] * (1 + len(kept)),
        out_specs=IN_VMEM,
        out_shape=out_shape,
        scratch_shapes=[
            pltpu.VMEM((count, 4, rows, nodes), jnp.bfloat16),
            pltpu.SemaphoreType.DMA((2, 4)),
        ],
        input_output_aliases={3: 0} if half is None and kept else {},
        compiler_params=pltpu.CompilerParams(vmem_limit_bytes=20 * 1024 * 1024),
        cost_estimate=pl.CostEstimate(flops=count * 8 * rows * part * nodes,
                                      bytes_accessed=count * (8 * rows * nodes + 8 * rows * part),
                                      transcendentals=0),
        name="gradient",
    )(position, in_hbm(lefts), held(mine), *kept)


def combine_kernel(pos_ref, own_ref, other_ref, *outs):
    y, z = pos_ref[1], pos_ref[2]
    block = outs[0].shape[0]
    for half in (1, 0):
        for d in range(4):
            q = lax.rem(z + half, 2) * 4 + lax.rem(y + d, 4)
            at = pl.ds(pl.multiple_of(q * block, block), block)
            both = own_ref[at, :] + other_ref[at, :].astype(jnp.float32)
            outs[half * 4 + d][...] = both.astype(jnp.bfloat16)


def combine(position, own, other):
    rows, part = own.shape
    return pl.pallas_call(
        combine_kernel,
        in_specs=[pl.BlockSpec(memory_space=pltpu.SMEM)] + [IN_VMEM] * 2,
        out_specs=[IN_VMEM] * 8,
        out_shape=[pltpu.VMEM((rows // 8, part), jnp.bfloat16)] * 8,
        compiler_params=pltpu.CompilerParams(vmem_limit_bytes=14 * 1024 * 1024),
        cost_estimate=pl.CostEstimate(flops=rows * part, bytes_accessed=8 * rows * part,
                                      transcendentals=0),
        name="combine",
    )(position, held(own), held(other))


def assemble_kernel(pos_ref, *refs):
    out_ref = refs[-1]
    part = refs[0].shape[1]
    for d in range(4):
        q = lax.rem(pos_ref[1] + 4 - d, 4)
        both = refs[d][...].astype(jnp.float32) + refs[4 + d][...].astype(jnp.float32)
        out_ref[:, pl.ds(pl.multiple_of(q * part, part), part)] = both.astype(jnp.bfloat16)


def assemble(position, parts):
    rows, part = parts[0].shape
    return pl.pallas_call(
        assemble_kernel,
        in_specs=[pl.BlockSpec(memory_space=pltpu.SMEM)] + [IN_VMEM] * 8,
        out_specs=IN_VMEM,
        out_shape=jax.ShapeDtypeStruct((rows, 4 * part), parts[0].dtype),
        compiler_params=pltpu.CompilerParams(vmem_limit_bytes=14 * 1024 * 1024),
        name="assemble",
    )(position, *[held(x) for x in parts])


def by_y(x, d):
    return lax.ppermute(x, "dp", [(i, (i + 4 * d) % 16) for i in range(16)])


def by_y_and_z(x, d):
    return lax.ppermute(x, "dp", [(i, (i + 4 * d) % 16 ^ 2) for i in range(16)])


def by_core(x):
    return lax.ppermute(x, "dp", [(i, i ^ 1) for i in range(16)])


def tied(values, after):
    *values, after = lax.optimization_barrier((*values, after))
    return values, after


def tied_list(values, others):
    both = lax.optimization_barrier((*values, *others))
    return both[:len(values)], list(both[len(values):])


def local(section_inputs, weights, norm_gains, upstream, edge_list, time_steps):
    section = lax.axis_index("pipe")
    sections = lax.axis_size("pipe")
    replica = lax.axis_index("dp")
    micros = section_inputs.shape[1]
    nodes = section_inputs.shape[2]
    width = section_inputs.shape[3]
    hidden = section_inputs[0]
    gates = timestep_gate(time_steps[:, 0], width)
    edges_t = jnp.swapaxes(edge_list[:, 0], 1, 2)
    position = jnp.stack([section, replica // 4, (replica // 2) % 2, replica % 2]).astype(jnp.int32)
    *state, wt, turned, grads, act = first(hidden, edges_t, gates, norm_gains, weights[0])

    def rest(turn, state):
        return second(turn, position, hidden, edges_t, gates, norm_gains, wt, turned,
                      state[:2], *state[2:])

    state = rest(1, state)
    slope, mixt, inv = state[2:]

    def to_y(parts):
        return [parts[0]] + [by_y(parts[d], d) for d in range(1, 4)]

    received = None
    near = []
    ticks = sections + micros - 1
    for t in range(ticks):
        if t == ticks - 1:
            near.append(to_y(last_act(position, received, slope, act)))
        sent, grads, act, *carried = tick(
            t, sections, position, received, upstream, slope, mixt, hidden, inv, norm_gains, wt,
            grads, act, [whole] if t == 1 else [])
        if t == ticks - 1:
            break
        pairs = [(s, s - 1) for s in range(1, sections)
                 if 0 <= t - (sections - 1 - s) < micros]
        received = lax.ppermute(sent, "pipe", pairs)
        if t == 0:
            state = rest(0, state)
            whole, saved, slope, mixt, inv = state
        if t == 1:
            lefts = lax.all_gather(carried[0], "dp", axis_index_groups=Y_GROUPS)
            wt = reload(saved, carried[0])
        if t in (7, 8):
            mine = stack(to_y(pick(t - 7, act)))
            if t == 7:
                (mine,), received = tied((mine,), received)
            near.append(mine)
        if t == 8:
            total = gradient(0, position, lefts, near[0], None)
            (total, mine), received = tied((total, near[1]), received)
            near[1] = mine

    total = gradient(1, position, lefts, near[1], total)
    (total,), parts_last = tied_list((total,), near[2])
    mine = stack(parts_last)
    other = by_core(gradient(micros - 1, position, lefts, mine, total, 1))
    own = gradient(micros - 1, position, lefts, mine, total, 0)
    pieces = combine(position, own, other)
    parts = to_y(pieces[:4]) + [by_y_and_z(pieces[4 + d], d) for d in range(4)]
    rows = assemble(position, parts)
    return (grads[None], rows[None])


def solution(mesh):
    in_specs = (
        P("pipe", None, "dp", None),
        P("pipe", None, None),
        P("pipe", None),
        P(None, "dp", None),
        P(None, "dp", None, None),
        P(None, "dp"),
    )
    out_specs = (P("pipe", None, "dp", None), P("pipe", "dp", None))
    return jax.shard_map(local, mesh=mesh, in_specs=in_specs, out_specs=out_specs, check_vma=False)
```

```python
import functools
import math

import jax
import jax.numpy as jnp
from jax import lax
from jax.experimental import pallas as pl
from jax.experimental.pallas import tpu as pltpu
from jax.sharding import PartitionSpec as P

NT = (((1,), (1,)), ((), ()))
BLOCK = 512
IN_VMEM = pl.BlockSpec(memory_space=pltpu.VMEM)
ANYWHERE = pl.BlockSpec(memory_space=pl.ANY)
Y_GROUPS = [[4 * y + r for y in range(4)] for r in range(4)]


def timestep_gate(time_steps, width):
    frequency = jnp.exp(-math.log(10000.0) * jnp.arange(width).astype(jnp.float32) / width)
    return 1.0 + 0.5 * jnp.sin(time_steps.astype(jnp.float32)[..., None] * frequency)


def in_hbm(x):
    return pltpu.with_memory_space_constraint(x, pltpu.HBM)


def held(x):
    return pltpu.with_memory_space_constraint(x, pltpu.VMEM)


def prepare(k, hidden_ref, edge_ref, gain_ref, mixt_ref, inv_ref, turned_s):
    nodes, width = hidden_ref.shape[1:]
    rows16 = width // 16
    edges = edge_ref.shape[2]
    ids = lax.broadcasted_iota(jnp.int32, (nodes, edges), 0)
    rows = lax.broadcasted_iota(jnp.int32, (nodes, nodes), 0)
    cols = lax.broadcasted_iota(jnp.int32, (nodes, nodes), 1)
    eye = jnp.where(rows == cols, 1.0, 0.0)
    src = jnp.where(edge_ref[k, 0:1, :] == ids, 1.0, 0.0).astype(jnp.bfloat16)
    tgt = jnp.where(edge_ref[k, 1:2, :] == ids, 1.0, 0.0).astype(jnp.bfloat16)
    adj = lax.dot_general(src, tgt, NT, preferred_element_type=jnp.float32)
    adj = adj + lax.dot_general(tgt, src, NT, preferred_element_type=jnp.float32) + eye
    mix = adj / jnp.sum(adj, axis=-1, keepdims=True)
    mixt_ref[k] = mix.T.astype(jnp.bfloat16)
    wide = hidden_ref[k].astype(jnp.float32)
    inv = lax.rsqrt(jnp.mean(wide * wide, axis=-1, keepdims=True) + 1e-06)
    inv_ref[k] = jnp.broadcast_to(inv, (nodes, 128))
    normed = (wide * inv * gain_ref[...]).astype(jnp.bfloat16)
    mixed = jnp.dot(mix.astype(jnp.bfloat16), normed, preferred_element_type=jnp.float32)
    mixed = mixed.astype(jnp.bfloat16)
    turned = mixed.T
    for q in range(16):
        place = (q // 2) % 2 * 4 + q // 4
        turned_s[q % 2, k, place * rows16:(place + 1) * rows16, :] = (
            turned[q * rows16:(q + 1) * rows16, :])
    return mixed


def gated_slope(u, gate):
    logistic = jax.nn.sigmoid(u)
    return (logistic * (1.0 + u * (1.0 - logistic)) * gate).astype(jnp.bfloat16)


def first_kernel(hidden_ref, edge_ref, gate_ref, gain_ref, w_ref,
                 p0, p2, slope_ref, mixt_ref, inv_ref, wt_ref, turned_ref, grads_ref, act_ref,
                 mixed_s, w_s, sems):
    del p0, p2, grads_ref, act_ref
    micros, nodes, width = hidden_ref.shape
    blocks = width // BLOCK

    def fetch(j, slot):
        at = pl.ds(pl.multiple_of(j * BLOCK, BLOCK), BLOCK)
        return pltpu.make_async_copy(w_ref.at[:, at], w_s.at[slot], sems.at[slot])

    for n in range(2):
        fetch(n, n).start()
    mixed_s[...] = prepare(0, hidden_ref, edge_ref, gain_ref, mixt_ref, inv_ref, turned_ref)

    @pl.loop(0, blocks)
    def _(j):
        slot = lax.rem(j, 2)
        fetch(j, slot).wait()
        at = pl.ds(pl.multiple_of(j * BLOCK, BLOCK), BLOCK)
        u = jnp.dot(mixed_s[...], w_s[slot], preferred_element_type=jnp.float32)
        wt_ref[at, :] = w_s[slot].T
        slope_ref[0, :, at] = gated_slope(u, gate_ref[0:1, at])

        @pl.when(j + 2 < blocks)
        def _():
            fetch(j + 2, slot).start()


def first(hidden, edges_t, gates, gain, weight):
    micros, nodes, width = hidden.shape
    piece = pltpu.HBM((2, micros, width // 2, nodes), jnp.bfloat16)
    return pl.pallas_call(
        first_kernel,
        in_specs=[IN_VMEM] * 4 + [ANYWHERE],
        out_specs=[ANYWHERE] * 2 + [IN_VMEM] * 5 + [ANYWHERE] * 2,
        out_shape=[
            piece, pltpu.HBM((width, width), jnp.bfloat16),
            pltpu.VMEM((micros, nodes, width), jnp.bfloat16),
            pltpu.VMEM((micros, nodes, nodes), jnp.bfloat16),
            pltpu.VMEM((micros, nodes, 128), jnp.float32),
            pltpu.VMEM((width, width), jnp.bfloat16),
            pltpu.VMEM((2, 1, width // 2, nodes), jnp.bfloat16),
            pltpu.HBM((micros, nodes, width), jnp.bfloat16),
            pltpu.HBM((micros, 4, nodes, width // 4), jnp.bfloat16),
        ],
        scratch_shapes=[
            pltpu.VMEM((nodes, width), jnp.bfloat16),
            pltpu.VMEM((2, width, BLOCK), jnp.bfloat16),
            pltpu.SemaphoreType.DMA((2,)),
        ],
        compiler_params=pltpu.CompilerParams(vmem_limit_bytes=16 * 1024 * 1024),
        cost_estimate=pl.CostEstimate(
            flops=2 * nodes * width * width,
            bytes_accessed=2 * width * width + 10 * micros * nodes * width,
            transcendentals=nodes * width),
        name="first",
    )(held(hidden), held(edges_t), held(gates), held(gain), in_hbm(weight))


def second_kernel(turn, pos_ref, hidden_ref, edge_ref, gate_ref, gain_ref, wt_ref, turned_ref,
                  p0, p2, s0, m0, i0, whole_ref, saved_ref, slope_ref, mixt_ref, inv_ref,
                  mixed_s, turned_s, sems):
    del p0, p2, s0, m0, i0
    micros, nodes, width = hidden_ref.shape
    core = pos_ref[3]

    @pl.when(core == turn)
    def _():
        split = width // 2
        parts = [pltpu.make_async_copy(wt_ref.at[pl.ds(n * split, split), :],
                                       saved_ref.at[pl.ds(n * split, split), :], sems.at[1 + n])
                 for n in range(2)]
        parts[0].start()
        if turn == 1:
            parts[0].wait()
        parts[1].start()
        for k in range(1, micros):
            mixed_s[(k - 1) * nodes:k * nodes, :] = prepare(
                k, hidden_ref, edge_ref, gain_ref, mixt_ref, inv_ref, turned_s)
        turned_s[:, 0] = turned_ref[:, 0]
        keep = pltpu.make_async_copy(turned_s, whole_ref, sems.at[0])
        keep.start()

        @pl.loop(0, width // BLOCK)
        def _(j):
            at = pl.ds(pl.multiple_of(j * BLOCK, BLOCK), BLOCK)
            u = lax.dot_general(mixed_s[...], wt_ref[at, :], NT, preferred_element_type=jnp.float32)
            for k in range(1, micros):
                slope_ref[k, :, at] = gated_slope(
                    u[(k - 1) * nodes:k * nodes, :], gate_ref[k:k + 1, at])

        keep.wait()
        if turn == 0:
            parts[0].wait()
        parts[1].wait()


def second(turn, position, hidden, edges_t, gates, gain, wt, turned, pieces, slope, mixt, inv):
    micros, nodes, width = hidden.shape
    kept = [in_hbm(x) for x in pieces] + [held(slope), held(mixt), held(inv)]
    specs = [ANYWHERE] * 2 + [IN_VMEM] * 3
    return pl.pallas_call(
        functools.partial(second_kernel, turn),
        in_specs=[pl.BlockSpec(memory_space=pltpu.SMEM)] + [IN_VMEM] * 6 + specs,
        out_specs=specs,
        out_shape=[pltpu.HBM(x.shape, x.dtype) for x in pieces]
        + [pltpu.VMEM(x.shape, x.dtype) for x in (slope, mixt, inv)],
        scratch_shapes=[
            pltpu.VMEM(((micros - 1) * nodes, width), jnp.bfloat16),
            pltpu.VMEM((2, micros, width // 2, nodes), jnp.bfloat16),
            pltpu.SemaphoreType.DMA((3,)),
        ],
        input_output_aliases={7 + n: n for n in range(5)},
        compiler_params=pltpu.CompilerParams(vmem_limit_bytes=16 * 1024 * 1024),
        cost_estimate=pl.CostEstimate(
            flops=2 * (micros - 1) * nodes * width * width,
            bytes_accessed=10 * micros * nodes * width,
            transcendentals=(micros - 1) * nodes * width),
        name="second",
    )(position, held(hidden), held(edges_t), held(gates), held(gain), held(wt), held(turned), *kept)


def reload_kernel(saved_ref, after_ref, wt_ref, sems):
    del after_ref
    rows = wt_ref.shape[0] // 4
    copies = [pltpu.make_async_copy(saved_ref.at[pl.ds(n * rows, rows), :],
                                    wt_ref.at[pl.ds(n * rows, rows), :], sems.at[n])
              for n in range(4)]
    for copy in copies:
        copy.start()
    for copy in copies:
        copy.wait()


def reload(saved, after):
    return pl.pallas_call(
        reload_kernel,
        in_specs=[ANYWHERE] * 2,
        out_specs=IN_VMEM,
        out_shape=pltpu.VMEM(saved.shape, saved.dtype),
        scratch_shapes=[pltpu.SemaphoreType.DMA((4,))],
        compiler_params=pltpu.CompilerParams(vmem_limit_bytes=2 * 1024 * 1024),
        cost_estimate=pl.CostEstimate(flops=0, bytes_accessed=2 * saved.size, transcendentals=0),
        name="reload",
    )(in_hbm(saved), in_hbm(after))


def put_columns(ref, act, y):
    part = ref.shape[2]
    for q in range(4):
        ref[lax.rem(q + 4 - y, 4)] = act[:, q * part:(q + 1) * part]


def tick_kernel(t, sections, sec_ref, *refs):
    if t < 3:
        up_ref, *refs = refs
    if t > 0:
        recv_ref, *refs = refs
    if t == 1:
        refs = refs[:8] + refs[9:12] + refs[13:]
    (slope_ref, mixt_ref, hidden_ref, inv_ref, gain_ref, wt_ref, grads_in, act_in,
     out_ref, grads_ref, act_ref, g_s, a_s, z_s, inner_s, h_s, act_s, sems) = refs
    del grads_in, act_in
    micros, nodes, width = hidden_ref.shape
    section = sec_ref[0]
    slot = t - (sections - 1 - section)
    last = section == sections - 1

    @pl.when(jnp.logical_and(slot >= 0, slot < micros))
    def _():
        fetch = pltpu.make_async_copy(hidden_ref.at[slot], h_s, sems.at[0])
        fetch.start()
        if t < micros:
            @pl.when(last)
            def _():
                copy = pltpu.make_async_copy(up_ref.at[t], out_ref.at[0], sems.at[1])
                copy.start()
                copy.wait()
                g_s[...] = out_ref[0].astype(jnp.float32)

            if t > 0:
                @pl.when(jnp.logical_not(last))
                def _():
                    g_s[...] = recv_ref[0].astype(jnp.float32)
        else:
            g_s[...] = recv_ref[0].astype(jnp.float32)
        act = (g_s[...] * slope_ref[slot].astype(jnp.float32)).astype(jnp.bfloat16)
        put_columns(act_s, act, sec_ref[1])
        keep_act = pltpu.make_async_copy(act_s, act_ref.at[slot], sems.at[2])
        keep_act.start()
        a_s[...] = jnp.dot(mixt_ref[slot], act, preferred_element_type=jnp.float32).astype(jnp.bfloat16)
        inner_s[...] = jnp.zeros_like(inner_s)
        fetch.wait()

        @pl.loop(0, width // BLOCK)
        def _(j):
            at = pl.ds(pl.multiple_of(j * BLOCK, BLOCK), BLOCK)
            z = jnp.dot(a_s[...], wt_ref[:, at], preferred_element_type=jnp.float32)
            z = z * gain_ref[:, at]
            z_s[:, at] = z
            part = jnp.sum(z * h_s[:, at].astype(jnp.float32), axis=-1, keepdims=True)
            inner_s[...] += jnp.broadcast_to(part, inner_s.shape)

        inv = inv_ref[slot, :, 0:1]
        scale = inv * inv * inv * (inner_s[:, 0:1] * (1.0 / width))
        grad = g_s[...] + inv * z_s[...] - h_s[...].astype(jnp.float32) * scale
        out_ref[0] = grad.astype(jnp.bfloat16)
        keep_grad = pltpu.make_async_copy(out_ref.at[0], grads_ref.at[slot], sems.at[3])
        keep_grad.start()
        keep_act.wait()
        keep_grad.wait()


def tick(t, sections, section, received, upstream, slope, mixt, hidden, inv, gain, wt, grads, act,
         carried=()):
    micros, nodes, width = hidden.shape
    extra = [in_hbm(upstream)] if t < 3 else []
    taken = [held(received)] if t > 0 else []
    base = 7 + len(extra) + len(taken)
    return pl.pallas_call(
        functools.partial(tick_kernel, t, sections),
        in_specs=[pl.BlockSpec(memory_space=pltpu.SMEM)] + [ANYWHERE] * len(extra)
        + [IN_VMEM] * (2 + len(taken)) + [ANYWHERE] + [IN_VMEM] * 3 + [ANYWHERE] * (2 + len(carried)),
        out_specs=[IN_VMEM, ANYWHERE, ANYWHERE] + [ANYWHERE] * len(carried),
        scratch_shapes=[
            pltpu.VMEM((nodes, width), jnp.float32),
            pltpu.VMEM((nodes, width), jnp.bfloat16),
            pltpu.VMEM((nodes, width), jnp.float32),
            pltpu.VMEM((nodes, 128), jnp.float32),
            pltpu.VMEM((nodes, width), jnp.bfloat16),
            pltpu.VMEM(act.shape[1:], jnp.bfloat16),
            pltpu.SemaphoreType.DMA((4,)),
        ],
        out_shape=[
            pltpu.VMEM((1, nodes, width), jnp.bfloat16),
            pltpu.HBM(grads.shape, grads.dtype),
            pltpu.HBM(act.shape, act.dtype),
        ] + [pltpu.HBM(x.shape, x.dtype) for x in carried],
        input_output_aliases={base + n: 1 + n for n in range(2 + len(carried))},
        compiler_params=pltpu.CompilerParams(vmem_limit_bytes=14 * 1024 * 1024),
        cost_estimate=pl.CostEstimate(
            flops=2 * nodes * width * width,
            bytes_accessed=2 * width * width + 12 * nodes * width,
            transcendentals=0),
        name="tick",
    )(section, *extra, *taken, held(slope), held(mixt), in_hbm(hidden), held(inv),
      held(gain), held(wt), in_hbm(grads), in_hbm(act),
      *[in_hbm(x) for x in carried])


def last_act_kernel(pos_ref, recv_ref, slope_ref, act_ref, *refs):
    outs, (act_s, sems) = refs[:4], refs[4:]
    micros = act_ref.shape[0]

    @pl.when(pos_ref[0] == 0)
    def _():
        act = recv_ref[0].astype(jnp.float32) * slope_ref[micros - 1].astype(jnp.float32)
        put_columns(act_s, act.astype(jnp.bfloat16), pos_ref[1])

    @pl.when(pos_ref[0] != 0)
    def _():
        copy = pltpu.make_async_copy(act_ref.at[micros - 1], act_s, sems.at[0])
        copy.start()
        copy.wait()

    for d in range(4):
        outs[d][...] = act_s[d]


def last_act(position, received, slope, act):
    micros, nodes, width = slope.shape
    return pl.pallas_call(
        last_act_kernel,
        in_specs=[pl.BlockSpec(memory_space=pltpu.SMEM), IN_VMEM, IN_VMEM, ANYWHERE],
        out_specs=[IN_VMEM] * 4,
        out_shape=[pltpu.VMEM((nodes, width // 4), jnp.bfloat16)] * 4,
        scratch_shapes=[pltpu.VMEM(act.shape[1:], jnp.bfloat16), pltpu.SemaphoreType.DMA((1,))],
        compiler_params=pltpu.CompilerParams(vmem_limit_bytes=14 * 1024 * 1024),
        cost_estimate=pl.CostEstimate(flops=nodes * width, bytes_accessed=8 * nodes * width,
                                      transcendentals=0),
        name="last_act",
    )(position, held(received), held(slope), in_hbm(act))


def pick_kernel(k, act_ref, *refs):
    outs, (act_s, sem) = refs[:4], refs[4:]
    copy = pltpu.make_async_copy(act_ref.at[k], act_s, sem)
    copy.start()
    copy.wait()
    for d in range(4):
        outs[d][...] = act_s[d]


def pick(k, act):
    micros, parts, nodes, part = act.shape
    return pl.pallas_call(
        functools.partial(pick_kernel, k),
        in_specs=[ANYWHERE],
        out_specs=[IN_VMEM] * 4,
        out_shape=[pltpu.VMEM((nodes, part), jnp.bfloat16)] * 4,
        scratch_shapes=[pltpu.VMEM(act.shape[1:], jnp.bfloat16), pltpu.SemaphoreType.DMA],
        compiler_params=pltpu.CompilerParams(vmem_limit_bytes=14 * 1024 * 1024),
        cost_estimate=pl.CostEstimate(flops=0, bytes_accessed=16 * nodes * part, transcendentals=0),
        name="pick",
    )(in_hbm(act))


def stack_kernel(*refs):
    out_ref = refs[-1]
    for d in range(4):
        out_ref[d] = refs[d][...]


def stack(parts):
    nodes, part = parts[0].shape
    return pl.pallas_call(
        stack_kernel,
        in_specs=[IN_VMEM] * 4,
        out_specs=IN_VMEM,
        out_shape=pltpu.VMEM((4, nodes, part), jnp.bfloat16),
        compiler_params=pltpu.CompilerParams(vmem_limit_bytes=14 * 1024 * 1024),
        cost_estimate=pl.CostEstimate(flops=0, bytes_accessed=16 * nodes * part, transcendentals=0),
        name="stack",
    )(*[held(x) for x in parts])


def gradient_kernel(k, begin, half, pos_ref, left_ref, mine_ref, *refs):
    if not begin:
        total_ref, *refs = refs
    out_ref, left_s, sems = refs
    y, core = pos_ref[1], pos_ref[3]
    halves = [0, 1] if half is None else [lax.rem(core + half, 2)]
    rows = left_s.shape[2]
    right = mine_ref[...].reshape(4 * mine_ref.shape[1], mine_ref.shape[2])
    copies = []
    for n, which in enumerate(halves):
        copies.append([])
        for d in range(4):
            source = lax.rem(y + 4 - d, 4)
            copies[n].append(pltpu.make_async_copy(
                left_ref.at[source, which, k], left_s.at[n, d], sems.at[n, d]))
            copies[n][d].start()
    for n, which in enumerate(halves):
        for copy in copies[n]:
            copy.wait()
        left = jnp.concatenate([left_s[n, d] for d in range(4)], axis=1)
        product = jnp.dot(left, right, preferred_element_type=jnp.float32)
        if not begin:
            product = product + total_ref[which]
        if half is None:
            out_ref[which] = product
        else:
            out_ref[...] = product.astype(out_ref.dtype)


def gradient(k, position, lefts, mine, total, half=None):
    rows, nodes = lefts.shape[3:]
    part = mine.shape[2]
    kept = [] if total is None else [held(total)]
    if half is None:
        count, out_shape = 2, pltpu.VMEM((2, rows, part), jnp.float32)
    else:
        count = 1
        out_shape = pltpu.VMEM((rows, part), jnp.bfloat16 if half else jnp.float32)
    return pl.pallas_call(
        functools.partial(gradient_kernel, k, total is None, half),
        in_specs=[pl.BlockSpec(memory_space=pltpu.SMEM), ANYWHERE] + [IN_VMEM] * (1 + len(kept)),
        out_specs=IN_VMEM,
        out_shape=out_shape,
        scratch_shapes=[
            pltpu.VMEM((count, 4, rows, nodes), jnp.bfloat16),
            pltpu.SemaphoreType.DMA((2, 4)),
        ],
        input_output_aliases={3: 0} if half is None and kept else {},
        compiler_params=pltpu.CompilerParams(
            vmem_limit_bytes=(14 if half is None else 11) * 1024 * 1024),
        cost_estimate=pl.CostEstimate(flops=count * 8 * rows * part * nodes,
                                      bytes_accessed=count * (8 * rows * nodes + 8 * rows * part),
                                      transcendentals=0),
        name="gradient",
    )(position, in_hbm(lefts), held(mine), *kept)


def combine_kernel(half, pos_ref, own_ref, other_ref, *refs):
    outs = refs[-4:]
    y, z = pos_ref[1], pos_ref[2]
    block = outs[0].shape[0]
    for d in range(4):
        q = lax.rem(z + half, 2) * 4 + lax.rem(y + d, 4)
        at = pl.ds(pl.multiple_of(q * block, block), block)
        both = own_ref[at, :] + other_ref[at, :].astype(jnp.float32)
        outs[d][...] = both.astype(jnp.bfloat16)


def combine(half, position, own, other, earlier=()):
    rows, part = own.shape
    return pl.pallas_call(
        functools.partial(combine_kernel, half),
        in_specs=[pl.BlockSpec(memory_space=pltpu.SMEM)] + [IN_VMEM] * 2 + [ANYWHERE] * len(earlier),
        out_specs=[IN_VMEM] * 4,
        out_shape=[pltpu.VMEM((rows // 8, part), jnp.bfloat16)] * 4,
        compiler_params=pltpu.CompilerParams(vmem_limit_bytes=11 * 1024 * 1024),
        cost_estimate=pl.CostEstimate(flops=rows * part, bytes_accessed=4 * rows * part,
                                      transcendentals=0),
        name="combine",
    )(position, held(own), held(other), *earlier)


def assemble_kernel(pos_ref, *refs):
    out_ref = refs[-1]
    part = refs[0].shape[1]
    for d in range(4):
        q = lax.rem(pos_ref[1] + 4 - d, 4)
        both = refs[d][...].astype(jnp.float32) + refs[4 + d][...].astype(jnp.float32)
        out_ref[:, pl.ds(pl.multiple_of(q * part, part), part)] = both.astype(jnp.bfloat16)


def assemble(position, parts):
    rows, part = parts[0].shape
    return pl.pallas_call(
        assemble_kernel,
        in_specs=[pl.BlockSpec(memory_space=pltpu.SMEM)] + [IN_VMEM] * 8,
        out_specs=IN_VMEM,
        out_shape=jax.ShapeDtypeStruct((rows, 4 * part), parts[0].dtype),
        compiler_params=pltpu.CompilerParams(vmem_limit_bytes=14 * 1024 * 1024),
        name="assemble",
    )(position, *[held(x) for x in parts])


def by_y(x, d):
    return lax.ppermute(x, "dp", [(i, (i + 4 * d) % 16) for i in range(16)])


def by_y_and_z(x, d):
    return lax.ppermute(x, "dp", [(i, (i + 4 * d) % 16 ^ 2) for i in range(16)])


def by_core(x):
    return lax.ppermute(x, "dp", [(i, i ^ 1) for i in range(16)])


def tied(values, after):
    *values, after = lax.optimization_barrier((*values, after))
    return values, after


def tied_list(values, others):
    both = lax.optimization_barrier((*values, *others))
    return both[:len(values)], list(both[len(values):])


def local(section_inputs, weights, norm_gains, upstream, edge_list, time_steps):
    section = lax.axis_index("pipe")
    sections = lax.axis_size("pipe")
    replica = lax.axis_index("dp")
    micros = section_inputs.shape[1]
    nodes = section_inputs.shape[2]
    width = section_inputs.shape[3]
    hidden = section_inputs[0]
    gates = timestep_gate(time_steps[:, 0], width)
    edges_t = jnp.swapaxes(edge_list[:, 0], 1, 2)
    position = jnp.stack([section, replica // 4, (replica // 2) % 2, replica % 2]).astype(jnp.int32)
    *state, wt, turned, grads, act = first(hidden, edges_t, gates, norm_gains, weights[0])

    def rest(turn, state):
        return second(turn, position, hidden, edges_t, gates, norm_gains, wt, turned,
                      state[:2], *state[2:])

    state = rest(1, state)
    slope, mixt, inv = state[2:]

    def to_y(parts):
        return [parts[0]] + [by_y(parts[d], d) for d in range(1, 4)]

    received = None
    near = []
    ticks = sections + micros - 1
    for t in range(ticks):
        if t == ticks - 1:
            near.append(to_y(last_act(position, received, slope, act)))
        sent, grads, act, *carried = tick(
            t, sections, position, received, upstream, slope, mixt, hidden, inv, norm_gains, wt,
            grads, act, [whole] if t == 1 else [])
        if t == ticks - 1:
            break
        pairs = [(s, s - 1) for s in range(1, sections)
                 if 0 <= t - (sections - 1 - s) < micros]
        received = lax.ppermute(sent, "pipe", pairs)
        if t == 0:
            state = rest(0, state)
            whole, saved, slope, mixt, inv = state
        if t == 1:
            lefts = lax.all_gather(carried[0], "dp", axis_index_groups=Y_GROUPS)
            wt = reload(saved, carried[0])
        if t in (7, 8):
            mine = stack(to_y(pick(t - 7, act)))
            if t == 7:
                (mine,), received = tied((mine,), received)
            near.append(mine)
        if t == 8:
            total = gradient(0, position, lefts, near[0], None)
            (total, mine), received = tied((total, near[1]), received)
            near[1] = mine

    total = gradient(1, position, lefts, near[1], total)
    (total,), parts_last = tied_list((total,), near[2])
    mine = stack(parts_last)
    other = by_core(gradient(micros - 1, position, lefts, mine, total, 1))
    own = gradient(micros - 1, position, lefts, mine, total, 0)
    distant = combine(1, position, own, other)
    parts = [by_y_and_z(distant[d], d) for d in range(4)]
    rows = assemble(position, to_y(combine(0, position, own, other, distant[3:])) + parts)
    return (grads[None], rows[None])


def solution(mesh):
    in_specs = (
        P("pipe", None, "dp", None),
        P("pipe", None, None),
        P("pipe", None),
        P(None, "dp", None),
        P(None, "dp", None, None),
        P(None, "dp"),
    )
    out_specs = (P("pipe", None, "dp", None), P("pipe", "dp", None))
    return jax.shard_map(local, mesh=mesh, in_specs=in_specs, out_specs=out_specs, check_vma=False)
```

```python
import functools
import math

import jax
import jax.numpy as jnp
from jax import lax
from jax.experimental import pallas as pl
from jax.experimental.pallas import tpu as pltpu
from jax.sharding import PartitionSpec as P

NT = (((1,), (1,)), ((), ()))
BLOCK = 512
IN_VMEM = pl.BlockSpec(memory_space=pltpu.VMEM)
ANYWHERE = pl.BlockSpec(memory_space=pl.ANY)
Y_GROUPS = [[4 * y + r for y in range(4)] for r in range(4)]


def timestep_gate(time_steps, width):
    frequency = jnp.exp(-math.log(10000.0) * jnp.arange(width).astype(jnp.float32) / width)
    return 1.0 + 0.5 * jnp.sin(time_steps.astype(jnp.float32)[..., None] * frequency)


def in_hbm(x):
    return pltpu.with_memory_space_constraint(x, pltpu.HBM)


def held(x):
    return pltpu.with_memory_space_constraint(x, pltpu.VMEM)


def prepare(k, hidden_ref, edge_ref, gain_ref, mixt_ref, inv_ref, turned_s):
    nodes, width = hidden_ref.shape[1:]
    rows16 = width // 16
    edges = edge_ref.shape[2]
    ids = lax.broadcasted_iota(jnp.int32, (nodes, edges), 0)
    rows = lax.broadcasted_iota(jnp.int32, (nodes, nodes), 0)
    cols = lax.broadcasted_iota(jnp.int32, (nodes, nodes), 1)
    eye = jnp.where(rows == cols, 1.0, 0.0)
    src = jnp.where(edge_ref[k, 0:1, :] == ids, 1.0, 0.0).astype(jnp.bfloat16)
    tgt = jnp.where(edge_ref[k, 1:2, :] == ids, 1.0, 0.0).astype(jnp.bfloat16)
    adj = lax.dot_general(src, tgt, NT, preferred_element_type=jnp.float32)
    adj = adj + lax.dot_general(tgt, src, NT, preferred_element_type=jnp.float32) + eye
    mix = adj / jnp.sum(adj, axis=-1, keepdims=True)
    mixt_ref[k] = mix.T.astype(jnp.bfloat16)
    wide = hidden_ref[k].astype(jnp.float32)
    inv = lax.rsqrt(jnp.mean(wide * wide, axis=-1, keepdims=True) + 1e-06)
    inv_ref[k] = jnp.broadcast_to(inv, (nodes, 128))
    normed = (wide * inv * gain_ref[...]).astype(jnp.bfloat16)
    mixed = jnp.dot(mix.astype(jnp.bfloat16), normed, preferred_element_type=jnp.float32)
    mixed = mixed.astype(jnp.bfloat16)
    turned = mixed.T
    for q in range(16):
        place = (q // 2) % 2 * 4 + q // 4
        turned_s[q % 2, k, place * rows16:(place + 1) * rows16, :] = (
            turned[q * rows16:(q + 1) * rows16, :])
    return mixed


def gated_slope(u, gate):
    logistic = jax.nn.sigmoid(u)
    return (logistic * (1.0 + u * (1.0 - logistic)) * gate).astype(jnp.bfloat16)


def first_kernel(hidden_ref, edge_ref, gate_ref, gain_ref, w_ref,
                 p0, p2, slope_ref, mixt_ref, inv_ref, wt_ref, turned_ref, grads_ref, act_ref,
                 mixed_s, w_s, sems):
    del p0, p2, grads_ref, act_ref
    micros, nodes, width = hidden_ref.shape
    blocks = width // BLOCK

    def fetch(j, slot):
        at = pl.ds(pl.multiple_of(j * BLOCK, BLOCK), BLOCK)
        return pltpu.make_async_copy(w_ref.at[:, at], w_s.at[slot], sems.at[slot])

    for n in range(2):
        fetch(n, n).start()
    mixed_s[...] = prepare(0, hidden_ref, edge_ref, gain_ref, mixt_ref, inv_ref, turned_ref)

    @pl.loop(0, blocks)
    def _(j):
        slot = lax.rem(j, 2)
        fetch(j, slot).wait()
        at = pl.ds(pl.multiple_of(j * BLOCK, BLOCK), BLOCK)
        u = jnp.dot(mixed_s[...], w_s[slot], preferred_element_type=jnp.float32)
        wt_ref[at, :] = w_s[slot].T
        slope_ref[0, :, at] = gated_slope(u, gate_ref[0:1, at])

        @pl.when(j + 2 < blocks)
        def _():
            fetch(j + 2, slot).start()


def first(hidden, edges_t, gates, gain, weight):
    micros, nodes, width = hidden.shape
    piece = pltpu.HBM((2, micros, width // 2, nodes), jnp.bfloat16)
    return pl.pallas_call(
        first_kernel,
        in_specs=[IN_VMEM] * 4 + [ANYWHERE],
        out_specs=[ANYWHERE] * 2 + [IN_VMEM] * 5 + [ANYWHERE] * 2,
        out_shape=[
            piece, pltpu.HBM((width, width), jnp.bfloat16),
            pltpu.VMEM((micros, nodes, width), jnp.bfloat16),
            pltpu.VMEM((micros, nodes, nodes), jnp.bfloat16),
            pltpu.VMEM((micros, nodes, 128), jnp.float32),
            pltpu.VMEM((width, width), jnp.bfloat16),
            pltpu.VMEM((2, 1, width // 2, nodes), jnp.bfloat16),
            pltpu.HBM((micros, nodes, width), jnp.bfloat16),
            pltpu.HBM((micros, 4, nodes, width // 4), jnp.bfloat16),
        ],
        scratch_shapes=[
            pltpu.VMEM((nodes, width), jnp.bfloat16),
            pltpu.VMEM((2, width, BLOCK), jnp.bfloat16),
            pltpu.SemaphoreType.DMA((2,)),
        ],
        compiler_params=pltpu.CompilerParams(vmem_limit_bytes=16 * 1024 * 1024),
        cost_estimate=pl.CostEstimate(
            flops=2 * nodes * width * width,
            bytes_accessed=2 * width * width + 10 * micros * nodes * width,
            transcendentals=nodes * width),
        name="first",
    )(held(hidden), held(edges_t), held(gates), held(gain), in_hbm(weight))


def second_kernel(turn, pos_ref, hidden_ref, edge_ref, gate_ref, gain_ref, wt_ref, turned_ref,
                  p0, p2, s0, m0, i0, whole_ref, saved_ref, slope_ref, mixt_ref, inv_ref,
                  mixed_s, turned_s, sems):
    del p0, p2, s0, m0, i0
    micros, nodes, width = hidden_ref.shape
    core = pos_ref[3]

    @pl.when(core == turn)
    def _():
        split = width // 2
        parts = [pltpu.make_async_copy(wt_ref.at[pl.ds(n * split, split), :],
                                       saved_ref.at[pl.ds(n * split, split), :], sems.at[1 + n])
                 for n in range(2)]
        parts[0].start()
        if turn == 1:
            parts[0].wait()
        parts[1].start()
        for k in range(1, micros):
            mixed_s[(k - 1) * nodes:k * nodes, :] = prepare(
                k, hidden_ref, edge_ref, gain_ref, mixt_ref, inv_ref, turned_s)
        turned_s[:, 0] = turned_ref[:, 0]
        keep = pltpu.make_async_copy(turned_s, whole_ref, sems.at[0])
        keep.start()

        @pl.loop(0, width // BLOCK)
        def _(j):
            at = pl.ds(pl.multiple_of(j * BLOCK, BLOCK), BLOCK)
            u = lax.dot_general(mixed_s[...], wt_ref[at, :], NT, preferred_element_type=jnp.float32)
            for k in range(1, micros):
                slope_ref[k, :, at] = gated_slope(
                    u[(k - 1) * nodes:k * nodes, :], gate_ref[k:k + 1, at])

        keep.wait()
        if turn == 0:
            parts[0].wait()
        parts[1].wait()


def second(turn, position, hidden, edges_t, gates, gain, wt, turned, pieces, slope, mixt, inv):
    micros, nodes, width = hidden.shape
    kept = [in_hbm(x) for x in pieces] + [held(slope), held(mixt), held(inv)]
    specs = [ANYWHERE] * 2 + [IN_VMEM] * 3
    return pl.pallas_call(
        functools.partial(second_kernel, turn),
        in_specs=[pl.BlockSpec(memory_space=pltpu.SMEM)] + [IN_VMEM] * 6 + specs,
        out_specs=specs,
        out_shape=[pltpu.HBM(x.shape, x.dtype) for x in pieces]
        + [pltpu.VMEM(x.shape, x.dtype) for x in (slope, mixt, inv)],
        scratch_shapes=[
            pltpu.VMEM(((micros - 1) * nodes, width), jnp.bfloat16),
            pltpu.VMEM((2, micros, width // 2, nodes), jnp.bfloat16),
            pltpu.SemaphoreType.DMA((3,)),
        ],
        input_output_aliases={7 + n: n for n in range(5)},
        compiler_params=pltpu.CompilerParams(vmem_limit_bytes=16 * 1024 * 1024),
        cost_estimate=pl.CostEstimate(
            flops=2 * (micros - 1) * nodes * width * width,
            bytes_accessed=10 * micros * nodes * width,
            transcendentals=(micros - 1) * nodes * width),
        name="second",
    )(position, held(hidden), held(edges_t), held(gates), held(gain), held(wt), held(turned), *kept)


def reload_kernel(saved_ref, after_ref, wt_ref, sems):
    del after_ref
    rows = wt_ref.shape[0] // 4
    copies = [pltpu.make_async_copy(saved_ref.at[pl.ds(n * rows, rows), :],
                                    wt_ref.at[pl.ds(n * rows, rows), :], sems.at[n])
              for n in range(4)]
    for copy in copies:
        copy.start()
    for copy in copies:
        copy.wait()


def reload(saved, after):
    return pl.pallas_call(
        reload_kernel,
        in_specs=[ANYWHERE] * 2,
        out_specs=IN_VMEM,
        out_shape=pltpu.VMEM(saved.shape, saved.dtype),
        scratch_shapes=[pltpu.SemaphoreType.DMA((4,))],
        compiler_params=pltpu.CompilerParams(vmem_limit_bytes=2 * 1024 * 1024),
        cost_estimate=pl.CostEstimate(flops=0, bytes_accessed=2 * saved.size, transcendentals=0),
        name="reload",
    )(in_hbm(saved), in_hbm(after))


def put_columns(ref, act, y):
    part = ref.shape[2]
    for q in range(4):
        ref[lax.rem(q + 4 - y, 4)] = act[:, q * part:(q + 1) * part]


def tick_kernel(t, sections, sec_ref, *refs):
    if t < 3:
        up_ref, *refs = refs
    if t > 0:
        recv_ref, *refs = refs
    if t == 1:
        refs = refs[:8] + refs[9:12] + refs[13:]
    (slope_ref, mixt_ref, hidden_ref, inv_ref, gain_ref, wt_ref, grads_in, act_in,
     out_ref, grads_ref, act_ref, g_s, a_s, z_s, inner_s, h_s, act_s, sems) = refs
    del grads_in, act_in
    micros, nodes, width = hidden_ref.shape
    section = sec_ref[0]
    slot = t - (sections - 1 - section)
    last = section == sections - 1

    @pl.when(jnp.logical_and(slot >= 0, slot < micros))
    def _():
        fetch = pltpu.make_async_copy(hidden_ref.at[slot], h_s, sems.at[0])
        fetch.start()
        if t < micros:
            @pl.when(last)
            def _():
                copy = pltpu.make_async_copy(up_ref.at[t], out_ref.at[0], sems.at[1])
                copy.start()
                copy.wait()
                g_s[...] = out_ref[0].astype(jnp.float32)

            if t > 0:
                @pl.when(jnp.logical_not(last))
                def _():
                    g_s[...] = recv_ref[0].astype(jnp.float32)
        else:
            g_s[...] = recv_ref[0].astype(jnp.float32)
        act = (g_s[...] * slope_ref[slot].astype(jnp.float32)).astype(jnp.bfloat16)
        put_columns(act_s, act, sec_ref[1])
        keep_act = pltpu.make_async_copy(act_s, act_ref.at[slot], sems.at[2])
        keep_act.start()
        a_s[...] = jnp.dot(mixt_ref[slot], act, preferred_element_type=jnp.float32).astype(jnp.bfloat16)
        fetch.wait()
        inner = jnp.zeros((nodes, 128), jnp.float32)
        for j in range(width // BLOCK):
            at = slice(j * BLOCK, (j + 1) * BLOCK)
            z = jnp.dot(a_s[...], wt_ref[:, at], preferred_element_type=jnp.float32)
            z = z * gain_ref[:, at]
            z_s[:, at] = z
            part = z * h_s[:, at].astype(jnp.float32)
            for n in range(BLOCK // 128):
                inner = inner + part[:, n * 128:(n + 1) * 128]
        inner_s[...] = jnp.broadcast_to(jnp.sum(inner, axis=-1, keepdims=True), inner_s.shape)

        inv = inv_ref[slot, :, 0:1]
        scale = inv * inv * inv * (inner_s[:, 0:1] * (1.0 / width))
        grad = g_s[...] + inv * z_s[...] - h_s[...].astype(jnp.float32) * scale
        out_ref[0] = grad.astype(jnp.bfloat16)
        keep_grad = pltpu.make_async_copy(out_ref.at[0], grads_ref.at[slot], sems.at[3])
        keep_grad.start()
        keep_act.wait()
        keep_grad.wait()


def tick(t, sections, section, received, upstream, slope, mixt, hidden, inv, gain, wt, grads, act,
         carried=()):
    micros, nodes, width = hidden.shape
    extra = [in_hbm(upstream)] if t < 3 else []
    taken = [held(received)] if t > 0 else []
    base = 7 + len(extra) + len(taken)
    return pl.pallas_call(
        functools.partial(tick_kernel, t, sections),
        in_specs=[pl.BlockSpec(memory_space=pltpu.SMEM)] + [ANYWHERE] * len(extra)
        + [IN_VMEM] * (2 + len(taken)) + [ANYWHERE] + [IN_VMEM] * 3 + [ANYWHERE] * (2 + len(carried)),
        out_specs=[IN_VMEM, ANYWHERE, ANYWHERE] + [ANYWHERE] * len(carried),
        scratch_shapes=[
            pltpu.VMEM((nodes, width), jnp.float32),
            pltpu.VMEM((nodes, width), jnp.bfloat16),
            pltpu.VMEM((nodes, width), jnp.float32),
            pltpu.VMEM((nodes, 128), jnp.float32),
            pltpu.VMEM((nodes, width), jnp.bfloat16),
            pltpu.VMEM(act.shape[1:], jnp.bfloat16),
            pltpu.SemaphoreType.DMA((4,)),
        ],
        out_shape=[
            pltpu.VMEM((1, nodes, width), jnp.bfloat16),
            pltpu.HBM(grads.shape, grads.dtype),
            pltpu.HBM(act.shape, act.dtype),
        ] + [pltpu.HBM(x.shape, x.dtype) for x in carried],
        input_output_aliases={base + n: 1 + n for n in range(2 + len(carried))},
        compiler_params=pltpu.CompilerParams(vmem_limit_bytes=14 * 1024 * 1024),
        cost_estimate=pl.CostEstimate(
            flops=2 * nodes * width * width,
            bytes_accessed=2 * width * width + 12 * nodes * width,
            transcendentals=0),
        name="tick",
    )(section, *extra, *taken, held(slope), held(mixt), in_hbm(hidden), held(inv),
      held(gain), held(wt), in_hbm(grads), in_hbm(act),
      *[in_hbm(x) for x in carried])


def last_act_kernel(pos_ref, recv_ref, slope_ref, act_ref, *refs):
    outs, (act_s, sems) = refs[:4], refs[4:]
    micros = act_ref.shape[0]

    @pl.when(pos_ref[0] == 0)
    def _():
        act = recv_ref[0].astype(jnp.float32) * slope_ref[micros - 1].astype(jnp.float32)
        put_columns(act_s, act.astype(jnp.bfloat16), pos_ref[1])

    @pl.when(pos_ref[0] != 0)
    def _():
        copy = pltpu.make_async_copy(act_ref.at[micros - 1], act_s, sems.at[0])
        copy.start()
        copy.wait()

    for d in range(4):
        outs[d][...] = act_s[d]


def last_act(position, received, slope, act):
    micros, nodes, width = slope.shape
    return pl.pallas_call(
        last_act_kernel,
        in_specs=[pl.BlockSpec(memory_space=pltpu.SMEM), IN_VMEM, IN_VMEM, ANYWHERE],
        out_specs=[IN_VMEM] * 4,
        out_shape=[pltpu.VMEM((nodes, width // 4), jnp.bfloat16)] * 4,
        scratch_shapes=[pltpu.VMEM(act.shape[1:], jnp.bfloat16), pltpu.SemaphoreType.DMA((1,))],
        compiler_params=pltpu.CompilerParams(vmem_limit_bytes=14 * 1024 * 1024),
        cost_estimate=pl.CostEstimate(flops=nodes * width, bytes_accessed=8 * nodes * width,
                                      transcendentals=0),
        name="last_act",
    )(position, held(received), held(slope), in_hbm(act))


def pick_kernel(k, act_ref, *refs):
    outs, (act_s, sem) = refs[:4], refs[4:]
    copy = pltpu.make_async_copy(act_ref.at[k], act_s, sem)
    copy.start()
    copy.wait()
    for d in range(4):
        outs[d][...] = act_s[d]


def pick(k, act):
    micros, parts, nodes, part = act.shape
    return pl.pallas_call(
        functools.partial(pick_kernel, k),
        in_specs=[ANYWHERE],
        out_specs=[IN_VMEM] * 4,
        out_shape=[pltpu.VMEM((nodes, part), jnp.bfloat16)] * 4,
        scratch_shapes=[pltpu.VMEM(act.shape[1:], jnp.bfloat16), pltpu.SemaphoreType.DMA],
        compiler_params=pltpu.CompilerParams(vmem_limit_bytes=14 * 1024 * 1024),
        cost_estimate=pl.CostEstimate(flops=0, bytes_accessed=16 * nodes * part, transcendentals=0),
        name="pick",
    )(in_hbm(act))


def stack_kernel(*refs):
    out_ref = refs[-1]
    for d in range(4):
        out_ref[d] = refs[d][...]


def stack(parts):
    nodes, part = parts[0].shape
    return pl.pallas_call(
        stack_kernel,
        in_specs=[IN_VMEM] * 4,
        out_specs=IN_VMEM,
        out_shape=pltpu.VMEM((4, nodes, part), jnp.bfloat16),
        compiler_params=pltpu.CompilerParams(vmem_limit_bytes=14 * 1024 * 1024),
        cost_estimate=pl.CostEstimate(flops=0, bytes_accessed=16 * nodes * part, transcendentals=0),
        name="stack",
    )(*[held(x) for x in parts])


def gradient_kernel(k, begin, half, pos_ref, left_ref, mine_ref, *refs):
    if not begin:
        total_ref, *refs = refs
    out_ref, left_s, sems = refs
    y, core = pos_ref[1], pos_ref[3]
    halves = [0, 1] if half is None else [lax.rem(core + half, 2)]
    rows = left_s.shape[2]
    right = mine_ref[...].reshape(4 * mine_ref.shape[1], mine_ref.shape[2])
    copies = []
    for n, which in enumerate(halves):
        copies.append([])
        for d in range(4):
            source = lax.rem(y + 4 - d, 4)
            copies[n].append(pltpu.make_async_copy(
                left_ref.at[source, which, k], left_s.at[n, d], sems.at[n, d]))
            copies[n][d].start()
    for n, which in enumerate(halves):
        for copy in copies[n]:
            copy.wait()
        left = jnp.concatenate([left_s[n, d] for d in range(4)], axis=1)
        product = jnp.dot(left, right, preferred_element_type=jnp.float32)
        if not begin:
            product = product + total_ref[which]
        if half is None:
            out_ref[which] = product
        else:
            out_ref[...] = product.astype(out_ref.dtype)


def gradient(k, position, lefts, mine, total, half=None):
    rows, nodes = lefts.shape[3:]
    part = mine.shape[2]
    kept = [] if total is None else [held(total)]
    if half is None:
        count, out_shape = 2, pltpu.VMEM((2, rows, part), jnp.float32)
    else:
        count = 1
        out_shape = pltpu.VMEM((rows, part), jnp.bfloat16 if half else jnp.float32)
    return pl.pallas_call(
        functools.partial(gradient_kernel, k, total is None, half),
        in_specs=[pl.BlockSpec(memory_space=pltpu.SMEM), ANYWHERE] + [IN_VMEM] * (1 + len(kept)),
        out_specs=IN_VMEM,
        out_shape=out_shape,
        scratch_shapes=[
            pltpu.VMEM((count, 4, rows, nodes), jnp.bfloat16),
            pltpu.SemaphoreType.DMA((2, 4)),
        ],
        input_output_aliases={3: 0} if half is None and kept else {},
        compiler_params=pltpu.CompilerParams(
            vmem_limit_bytes=(14 if half is None else 11) * 1024 * 1024),
        cost_estimate=pl.CostEstimate(flops=count * 8 * rows * part * nodes,
                                      bytes_accessed=count * (8 * rows * nodes + 8 * rows * part),
                                      transcendentals=0),
        name="gradient",
    )(position, in_hbm(lefts), held(mine), *kept)


def combine_kernel(half, pos_ref, own_ref, other_ref, *refs):
    outs = refs[-4:]
    y, z = pos_ref[1], pos_ref[2]
    block = outs[0].shape[0]
    for d in range(4):
        q = lax.rem(z + half, 2) * 4 + lax.rem(y + d, 4)
        at = pl.ds(pl.multiple_of(q * block, block), block)
        both = own_ref[at, :] + other_ref[at, :].astype(jnp.float32)
        outs[d][...] = both.astype(jnp.bfloat16)


def combine(half, position, own, other, earlier=()):
    rows, part = own.shape
    return pl.pallas_call(
        functools.partial(combine_kernel, half),
        in_specs=[pl.BlockSpec(memory_space=pltpu.SMEM)] + [IN_VMEM] * 2 + [ANYWHERE] * len(earlier),
        out_specs=[IN_VMEM] * 4,
        out_shape=[pltpu.VMEM((rows // 8, part), jnp.bfloat16)] * 4,
        compiler_params=pltpu.CompilerParams(vmem_limit_bytes=11 * 1024 * 1024),
        cost_estimate=pl.CostEstimate(flops=rows * part, bytes_accessed=4 * rows * part,
                                      transcendentals=0),
        name="combine",
    )(position, held(own), held(other), *earlier)


def assemble_kernel(pos_ref, *refs):
    out_ref = refs[-1]
    part = refs[0].shape[1]
    for d in range(4):
        q = lax.rem(pos_ref[1] + 4 - d, 4)
        both = refs[d][...].astype(jnp.float32) + refs[4 + d][...].astype(jnp.float32)
        out_ref[:, pl.ds(pl.multiple_of(q * part, part), part)] = both.astype(jnp.bfloat16)


def assemble(position, parts):
    rows, part = parts[0].shape
    return pl.pallas_call(
        assemble_kernel,
        in_specs=[pl.BlockSpec(memory_space=pltpu.SMEM)] + [IN_VMEM] * 8,
        out_specs=IN_VMEM,
        out_shape=jax.ShapeDtypeStruct((rows, 4 * part), parts[0].dtype),
        compiler_params=pltpu.CompilerParams(vmem_limit_bytes=14 * 1024 * 1024),
        name="assemble",
    )(position, *[held(x) for x in parts])


def by_y(x, d):
    return lax.ppermute(x, "dp", [(i, (i + 4 * d) % 16) for i in range(16)])


def by_y_and_z(x, d):
    return lax.ppermute(x, "dp", [(i, (i + 4 * d) % 16 ^ 2) for i in range(16)])


def by_core(x):
    return lax.ppermute(x, "dp", [(i, i ^ 1) for i in range(16)])


def tied(values, after):
    *values, after = lax.optimization_barrier((*values, after))
    return values, after


def tied_list(values, others):
    both = lax.optimization_barrier((*values, *others))
    return both[:len(values)], list(both[len(values):])


def local(section_inputs, weights, norm_gains, upstream, edge_list, time_steps):
    section = lax.axis_index("pipe")
    sections = lax.axis_size("pipe")
    replica = lax.axis_index("dp")
    micros = section_inputs.shape[1]
    nodes = section_inputs.shape[2]
    width = section_inputs.shape[3]
    hidden = section_inputs[0]
    gates = timestep_gate(time_steps[:, 0], width)
    edges_t = jnp.swapaxes(edge_list[:, 0], 1, 2)
    position = jnp.stack([section, replica // 4, (replica // 2) % 2, replica % 2]).astype(jnp.int32)
    *state, wt, turned, grads, act = first(hidden, edges_t, gates, norm_gains, weights[0])

    def rest(turn, state):
        return second(turn, position, hidden, edges_t, gates, norm_gains, wt, turned,
                      state[:2], *state[2:])

    state = rest(1, state)
    slope, mixt, inv = state[2:]

    def to_y(parts):
        return [parts[0]] + [by_y(parts[d], d) for d in range(1, 4)]

    received = None
    near = []
    ticks = sections + micros - 1
    for t in range(ticks):
        if t == ticks - 1:
            near.append(to_y(last_act(position, received, slope, act)))
        sent, grads, act, *carried = tick(
            t, sections, position, received, upstream, slope, mixt, hidden, inv, norm_gains, wt,
            grads, act, [whole] if t == 1 else [])
        if t == ticks - 1:
            break
        pairs = [(s, s - 1) for s in range(1, sections)
                 if 0 <= t - (sections - 1 - s) < micros]
        received = lax.ppermute(sent, "pipe", pairs)
        if t == 0:
            state = rest(0, state)
            whole, saved, slope, mixt, inv = state
        if t == 1:
            lefts = lax.all_gather(carried[0], "dp", axis_index_groups=Y_GROUPS)
            wt = reload(saved, carried[0])
        if t in (7, 8):
            mine = stack(to_y(pick(t - 7, act)))
            if t == 7:
                (mine,), received = tied((mine,), received)
            near.append(mine)
        if t == 8:
            total = gradient(0, position, lefts, near[0], None)
            (total, mine), received = tied((total, near[1]), received)
            near[1] = mine

    total = gradient(1, position, lefts, near[1], total)
    (total,), parts_last = tied_list((total,), near[2])
    mine = stack(parts_last)
    other = by_core(gradient(micros - 1, position, lefts, mine, total, 1))
    own = gradient(micros - 1, position, lefts, mine, total, 0)
    distant = combine(1, position, own, other)
    parts = [by_y_and_z(distant[d], d) for d in range(4)]
    rows = assemble(position, to_y(combine(0, position, own, other, parts[:1])) + parts)
    return (grads[None], rows[None])


def solution(mesh):
    in_specs = (
        P("pipe", None, "dp", None),
        P("pipe", None, None),
        P("pipe", None),
        P(None, "dp", None),
        P(None, "dp", None, None),
        P(None, "dp"),
    )
    out_specs = (P("pipe", None, "dp", None), P("pipe", "dp", None))
    return jax.shard_map(local, mesh=mesh, in_specs=in_specs, out_specs=out_specs, check_vma=False)
```

```python
import functools
import math

import jax
import jax.numpy as jnp
from jax import lax
from jax.experimental import pallas as pl
from jax.experimental.pallas import tpu as pltpu
from jax.sharding import PartitionSpec as P

NT = (((1,), (1,)), ((), ()))
BLOCK = 512
IN_VMEM = pl.BlockSpec(memory_space=pltpu.VMEM)
ANYWHERE = pl.BlockSpec(memory_space=pl.ANY)
Y_GROUPS = [[4 * y + r for y in range(4)] for r in range(4)]


def timestep_gate(time_steps, width):
    frequency = jnp.exp(-math.log(10000.0) * jnp.arange(width).astype(jnp.float32) / width)
    return 1.0 + 0.5 * jnp.sin(time_steps.astype(jnp.float32)[..., None] * frequency)


def in_hbm(x):
    return pltpu.with_memory_space_constraint(x, pltpu.HBM)


def held(x):
    return pltpu.with_memory_space_constraint(x, pltpu.VMEM)


def prepare(k, hidden_ref, edge_ref, gain_ref, mixt_ref, inv_ref, turned_s):
    nodes, width = hidden_ref.shape[1:]
    rows16 = width // 16
    edges = edge_ref.shape[2]
    ids = lax.broadcasted_iota(jnp.int32, (nodes, edges), 0)
    rows = lax.broadcasted_iota(jnp.int32, (nodes, nodes), 0)
    cols = lax.broadcasted_iota(jnp.int32, (nodes, nodes), 1)
    eye = jnp.where(rows == cols, 1.0, 0.0)
    src = jnp.where(edge_ref[k, 0:1, :] == ids, 1.0, 0.0).astype(jnp.bfloat16)
    tgt = jnp.where(edge_ref[k, 1:2, :] == ids, 1.0, 0.0).astype(jnp.bfloat16)
    adj = lax.dot_general(src, tgt, NT, preferred_element_type=jnp.float32)
    adj = adj + lax.dot_general(tgt, src, NT, preferred_element_type=jnp.float32) + eye
    mix = adj / jnp.sum(adj, axis=-1, keepdims=True)
    mixt_ref[k] = mix.T.astype(jnp.bfloat16)
    wide = hidden_ref[k].astype(jnp.float32)
    inv = lax.rsqrt(jnp.mean(wide * wide, axis=-1, keepdims=True) + 1e-06)
    inv_ref[k] = jnp.broadcast_to(inv, (nodes, 128))
    normed = (wide * inv * gain_ref[...]).astype(jnp.bfloat16)
    mixed = jnp.dot(mix.astype(jnp.bfloat16), normed, preferred_element_type=jnp.float32)
    mixed = mixed.astype(jnp.bfloat16)
    turned = mixed.T
    for q in range(16):
        place = (q // 2) % 2 * 4 + q // 4
        turned_s[q % 2, k, place * rows16:(place + 1) * rows16, :] = (
            turned[q * rows16:(q + 1) * rows16, :])
    return mixed


def gated_slope(u, gate):
    logistic = jax.nn.sigmoid(u)
    return (logistic * (1.0 + u * (1.0 - logistic)) * gate).astype(jnp.bfloat16)


def first_kernel(hidden_ref, edge_ref, gate_ref, gain_ref, w_ref,
                 p0, p2, slope_ref, mixt_ref, inv_ref, wt_ref, turned_ref, grads_ref, act_ref,
                 mixed_s, w_s, sems):
    del p0, p2, grads_ref, act_ref
    micros, nodes, width = hidden_ref.shape
    blocks = width // BLOCK

    def fetch(j, slot):
        at = pl.ds(pl.multiple_of(j * BLOCK, BLOCK), BLOCK)
        return pltpu.make_async_copy(w_ref.at[:, at], w_s.at[slot], sems.at[slot])

    for n in range(2):
        fetch(n, n).start()
    mixed_s[...] = prepare(0, hidden_ref, edge_ref, gain_ref, mixt_ref, inv_ref, turned_ref)

    @pl.loop(0, blocks)
    def _(j):
        slot = lax.rem(j, 2)
        fetch(j, slot).wait()
        at = pl.ds(pl.multiple_of(j * BLOCK, BLOCK), BLOCK)
        u = jnp.dot(mixed_s[...], w_s[slot], preferred_element_type=jnp.float32)
        wt_ref[at, :] = w_s[slot].T
        slope_ref[0, :, at] = gated_slope(u, gate_ref[0:1, at])

        @pl.when(j + 2 < blocks)
        def _():
            fetch(j + 2, slot).start()


def first(hidden, edges_t, gates, gain, weight):
    micros, nodes, width = hidden.shape
    piece = pltpu.HBM((2, micros, width // 2, nodes), jnp.bfloat16)
    return pl.pallas_call(
        first_kernel,
        in_specs=[IN_VMEM] * 4 + [ANYWHERE],
        out_specs=[ANYWHERE] * 2 + [IN_VMEM] * 5 + [ANYWHERE] * 2,
        out_shape=[
            piece, pltpu.HBM((width, width), jnp.bfloat16),
            pltpu.VMEM((micros, nodes, width), jnp.bfloat16),
            pltpu.VMEM((micros, nodes, nodes), jnp.bfloat16),
            pltpu.VMEM((micros, nodes, 128), jnp.float32),
            pltpu.VMEM((width, width), jnp.bfloat16),
            pltpu.VMEM((2, 1, width // 2, nodes), jnp.bfloat16),
            pltpu.HBM((micros, nodes, width), jnp.bfloat16),
            pltpu.HBM((micros, 4, nodes, width // 4), jnp.bfloat16),
        ],
        scratch_shapes=[
            pltpu.VMEM((nodes, width), jnp.bfloat16),
            pltpu.VMEM((2, width, BLOCK), jnp.bfloat16),
            pltpu.SemaphoreType.DMA((2,)),
        ],
        compiler_params=pltpu.CompilerParams(vmem_limit_bytes=16 * 1024 * 1024),
        cost_estimate=pl.CostEstimate(
            flops=2 * nodes * width * width,
            bytes_accessed=2 * width * width + 10 * micros * nodes * width,
            transcendentals=nodes * width),
        name="first",
    )(held(hidden), held(edges_t), held(gates), held(gain), in_hbm(weight))


def second_kernel(turn, pos_ref, hidden_ref, edge_ref, gate_ref, gain_ref, wt_ref, turned_ref,
                  p0, p2, s0, m0, i0, whole_ref, saved_ref, slope_ref, mixt_ref, inv_ref,
                  mixed_s, turned_s, sems):
    del p0, p2, s0, m0, i0
    micros, nodes, width = hidden_ref.shape
    core = pos_ref[3]

    @pl.when(core == turn)
    def _():
        split = width // 2
        parts = [pltpu.make_async_copy(wt_ref.at[pl.ds(n * split, split), :],
                                       saved_ref.at[pl.ds(n * split, split), :], sems.at[1 + n])
                 for n in range(2)]
        parts[0].start()
        if turn == 1:
            parts[0].wait()
        parts[1].start()
        for k in range(1, micros):
            mixed_s[(k - 1) * nodes:k * nodes, :] = prepare(
                k, hidden_ref, edge_ref, gain_ref, mixt_ref, inv_ref, turned_s)
        turned_s[:, 0] = turned_ref[:, 0]
        keep = pltpu.make_async_copy(turned_s, whole_ref, sems.at[0])
        keep.start()

        @pl.loop(0, width // BLOCK)
        def _(j):
            at = pl.ds(pl.multiple_of(j * BLOCK, BLOCK), BLOCK)
            u = lax.dot_general(mixed_s[...], wt_ref[at, :], NT, preferred_element_type=jnp.float32)
            for k in range(1, micros):
                slope_ref[k, :, at] = gated_slope(
                    u[(k - 1) * nodes:k * nodes, :], gate_ref[k:k + 1, at])

        keep.wait()
        if turn == 0:
            parts[0].wait()
        parts[1].wait()


def second(turn, position, hidden, edges_t, gates, gain, wt, turned, pieces, slope, mixt, inv):
    micros, nodes, width = hidden.shape
    kept = [in_hbm(x) for x in pieces] + [held(slope), held(mixt), held(inv)]
    specs = [ANYWHERE] * 2 + [IN_VMEM] * 3
    return pl.pallas_call(
        functools.partial(second_kernel, turn),
        in_specs=[pl.BlockSpec(memory_space=pltpu.SMEM)] + [IN_VMEM] * 6 + specs,
        out_specs=specs,
        out_shape=[pltpu.HBM(x.shape, x.dtype) for x in pieces]
        + [pltpu.VMEM(x.shape, x.dtype) for x in (slope, mixt, inv)],
        scratch_shapes=[
            pltpu.VMEM(((micros - 1) * nodes, width), jnp.bfloat16),
            pltpu.VMEM((2, micros, width // 2, nodes), jnp.bfloat16),
            pltpu.SemaphoreType.DMA((3,)),
        ],
        input_output_aliases={7 + n: n for n in range(5)},
        compiler_params=pltpu.CompilerParams(vmem_limit_bytes=16 * 1024 * 1024),
        cost_estimate=pl.CostEstimate(
            flops=2 * (micros - 1) * nodes * width * width,
            bytes_accessed=10 * micros * nodes * width,
            transcendentals=(micros - 1) * nodes * width),
        name="second",
    )(position, held(hidden), held(edges_t), held(gates), held(gain), held(wt), held(turned), *kept)


def reload_kernel(saved_ref, after_ref, wt_ref, sems):
    del after_ref
    rows = wt_ref.shape[0] // 4
    copies = [pltpu.make_async_copy(saved_ref.at[pl.ds(n * rows, rows), :],
                                    wt_ref.at[pl.ds(n * rows, rows), :], sems.at[n])
              for n in range(4)]
    for copy in copies:
        copy.start()
    for copy in copies:
        copy.wait()


def reload(saved, after):
    return pl.pallas_call(
        reload_kernel,
        in_specs=[ANYWHERE] * 2,
        out_specs=IN_VMEM,
        out_shape=pltpu.VMEM(saved.shape, saved.dtype),
        scratch_shapes=[pltpu.SemaphoreType.DMA((4,))],
        compiler_params=pltpu.CompilerParams(vmem_limit_bytes=2 * 1024 * 1024),
        cost_estimate=pl.CostEstimate(flops=0, bytes_accessed=2 * saved.size, transcendentals=0),
        name="reload",
    )(in_hbm(saved), in_hbm(after))


def put_columns(ref, act, y):
    part = ref.shape[2]
    for q in range(4):
        ref[lax.rem(q + 4 - y, 4)] = act[:, q * part:(q + 1) * part]


def tick_kernel(t, sections, sec_ref, *refs):
    if t < 3:
        up_ref, *refs = refs
    if t > 0:
        recv_ref, *refs = refs
    if t == 1:
        refs = refs[:8] + refs[9:12] + refs[13:]
    (slope_ref, mixt_ref, hidden_ref, inv_ref, gain_ref, wt_ref, grads_in, act_in,
     out_ref, grads_ref, act_ref, g_s, a_s, z_s, inner_s, h_s, act_s, sems) = refs
    del grads_in, act_in
    micros, nodes, width = hidden_ref.shape
    section = sec_ref[0]
    slot = t - (sections - 1 - section)
    last = section == sections - 1

    @pl.when(jnp.logical_and(slot >= 0, slot < micros))
    def _():
        fetch = pltpu.make_async_copy(hidden_ref.at[slot], h_s, sems.at[0])
        fetch.start()
        if t < micros:
            @pl.when(last)
            def _():
                copy = pltpu.make_async_copy(up_ref.at[t], out_ref.at[0], sems.at[1])
                copy.start()
                copy.wait()
                g_s[...] = out_ref[0].astype(jnp.float32)

            if t > 0:
                @pl.when(jnp.logical_not(last))
                def _():
                    g_s[...] = recv_ref[0].astype(jnp.float32)
        else:
            g_s[...] = recv_ref[0].astype(jnp.float32)
        act = (g_s[...] * slope_ref[slot].astype(jnp.float32)).astype(jnp.bfloat16)
        put_columns(act_s, act, sec_ref[1])
        keep_act = pltpu.make_async_copy(act_s, act_ref.at[slot], sems.at[2])
        keep_act.start()
        a_s[...] = jnp.dot(mixt_ref[slot], act, preferred_element_type=jnp.float32).astype(jnp.bfloat16)
        fetch.wait()
        inner = jnp.zeros((nodes, 128), jnp.float32)
        for j in range(width // BLOCK):
            at = slice(j * BLOCK, (j + 1) * BLOCK)
            z = jnp.dot(a_s[...], wt_ref[:, at], preferred_element_type=jnp.float32)
            z = z * gain_ref[:, at]
            z_s[:, at] = z
            part = z * h_s[:, at].astype(jnp.float32)
            for n in range(BLOCK // 128):
                inner = inner + part[:, n * 128:(n + 1) * 128]
        inner_s[...] = jnp.broadcast_to(jnp.sum(inner, axis=-1, keepdims=True), inner_s.shape)

        inv = inv_ref[slot, :, 0:1]
        scale = inv * inv * inv * (inner_s[:, 0:1] * (1.0 / width))
        grad = g_s[...] + inv * z_s[...] - h_s[...].astype(jnp.float32) * scale
        out_ref[0] = grad.astype(jnp.bfloat16)
        keep_grad = pltpu.make_async_copy(out_ref.at[0], grads_ref.at[slot], sems.at[3])
        keep_grad.start()
        keep_act.wait()
        keep_grad.wait()


def tick(t, sections, section, received, upstream, slope, mixt, hidden, inv, gain, wt, grads, act,
         carried=()):
    micros, nodes, width = hidden.shape
    extra = [in_hbm(upstream)] if t < 3 else []
    taken = [held(received)] if t > 0 else []
    base = 7 + len(extra) + len(taken)
    return pl.pallas_call(
        functools.partial(tick_kernel, t, sections),
        in_specs=[pl.BlockSpec(memory_space=pltpu.SMEM)] + [ANYWHERE] * len(extra)
        + [IN_VMEM] * (2 + len(taken)) + [ANYWHERE] + [IN_VMEM] * 3 + [ANYWHERE] * (2 + len(carried)),
        out_specs=[IN_VMEM, ANYWHERE, ANYWHERE] + [ANYWHERE] * len(carried),
        scratch_shapes=[
            pltpu.VMEM((nodes, width), jnp.float32),
            pltpu.VMEM((nodes, width), jnp.bfloat16),
            pltpu.VMEM((nodes, width), jnp.float32),
            pltpu.VMEM((nodes, 128), jnp.float32),
            pltpu.VMEM((nodes, width), jnp.bfloat16),
            pltpu.VMEM(act.shape[1:], jnp.bfloat16),
            pltpu.SemaphoreType.DMA((4,)),
        ],
        out_shape=[
            pltpu.VMEM((1, nodes, width), jnp.bfloat16),
            pltpu.HBM(grads.shape, grads.dtype),
            pltpu.HBM(act.shape, act.dtype),
        ] + [pltpu.HBM(x.shape, x.dtype) for x in carried],
        input_output_aliases={base + n: 1 + n for n in range(2 + len(carried))},
        compiler_params=pltpu.CompilerParams(vmem_limit_bytes=14 * 1024 * 1024),
        cost_estimate=pl.CostEstimate(
            flops=2 * nodes * width * width,
            bytes_accessed=2 * width * width + 12 * nodes * width,
            transcendentals=0),
        name="tick",
    )(section, *extra, *taken, held(slope), held(mixt), in_hbm(hidden), held(inv),
      held(gain), held(wt), in_hbm(grads), in_hbm(act),
      *[in_hbm(x) for x in carried])


def last_act_kernel(pos_ref, recv_ref, slope_ref, act_ref, *refs):
    outs, (act_s, sems) = refs[:4], refs[4:]
    micros = act_ref.shape[0]

    @pl.when(pos_ref[0] == 0)
    def _():
        act = recv_ref[0].astype(jnp.float32) * slope_ref[micros - 1].astype(jnp.float32)
        put_columns(act_s, act.astype(jnp.bfloat16), pos_ref[1])

    @pl.when(pos_ref[0] != 0)
    def _():
        copy = pltpu.make_async_copy(act_ref.at[micros - 1], act_s, sems.at[0])
        copy.start()
        copy.wait()

    for d in range(4):
        outs[d][...] = act_s[d]


def last_act(position, received, slope, act):
    micros, nodes, width = slope.shape
    return pl.pallas_call(
        last_act_kernel,
        in_specs=[pl.BlockSpec(memory_space=pltpu.SMEM), IN_VMEM, IN_VMEM, ANYWHERE],
        out_specs=[IN_VMEM] * 4,
        out_shape=[pltpu.VMEM((nodes, width // 4), jnp.bfloat16)] * 4,
        scratch_shapes=[pltpu.VMEM(act.shape[1:], jnp.bfloat16), pltpu.SemaphoreType.DMA((1,))],
        compiler_params=pltpu.CompilerParams(vmem_limit_bytes=14 * 1024 * 1024),
        cost_estimate=pl.CostEstimate(flops=nodes * width, bytes_accessed=8 * nodes * width,
                                      transcendentals=0),
        name="last_act",
    )(position, held(received), held(slope), in_hbm(act))


def pick_kernel(k, act_ref, *refs):
    outs, (act_s, sem) = refs[:4], refs[4:]
    copy = pltpu.make_async_copy(act_ref.at[k], act_s, sem)
    copy.start()
    copy.wait()
    for d in range(4):
        outs[d][...] = act_s[d]


def pick(k, act):
    micros, parts, nodes, part = act.shape
    return pl.pallas_call(
        functools.partial(pick_kernel, k),
        in_specs=[ANYWHERE],
        out_specs=[IN_VMEM] * 4,
        out_shape=[pltpu.VMEM((nodes, part), jnp.bfloat16)] * 4,
        scratch_shapes=[pltpu.VMEM(act.shape[1:], jnp.bfloat16), pltpu.SemaphoreType.DMA],
        compiler_params=pltpu.CompilerParams(vmem_limit_bytes=14 * 1024 * 1024),
        cost_estimate=pl.CostEstimate(flops=0, bytes_accessed=16 * nodes * part, transcendentals=0),
        name="pick",
    )(in_hbm(act))


def stack_kernel(*refs):
    out_ref = refs[-1]
    for d in range(4):
        out_ref[d] = refs[d][...]


def stack(parts):
    nodes, part = parts[0].shape
    return pl.pallas_call(
        stack_kernel,
        in_specs=[IN_VMEM] * 4,
        out_specs=IN_VMEM,
        out_shape=pltpu.VMEM((4, nodes, part), jnp.bfloat16),
        compiler_params=pltpu.CompilerParams(vmem_limit_bytes=14 * 1024 * 1024),
        cost_estimate=pl.CostEstimate(flops=0, bytes_accessed=16 * nodes * part, transcendentals=0),
        name="stack",
    )(*[held(x) for x in parts])


def gradient_kernel(k, begin, half, pos_ref, left_ref, mine_ref, *refs):
    if not begin:
        total_ref, *refs = refs
    out_ref, left_s, sems = refs
    y, core = pos_ref[1], pos_ref[3]
    halves = [0, 1] if half is None else [lax.rem(core + half, 2)]
    rows = left_s.shape[2]
    right = mine_ref[...].reshape(4 * mine_ref.shape[1], mine_ref.shape[2])
    copies = []
    for n, which in enumerate(halves):
        copies.append([])
        for d in range(4):
            source = lax.rem(y + 4 - d, 4)
            copies[n].append(pltpu.make_async_copy(
                left_ref.at[source, which, k], left_s.at[n, d], sems.at[n, d]))
            copies[n][d].start()
    for n, which in enumerate(halves):
        for copy in copies[n]:
            copy.wait()
        left = jnp.concatenate([left_s[n, d] for d in range(4)], axis=1)
        product = jnp.dot(left, right, preferred_element_type=jnp.float32)
        if not begin:
            product = product + total_ref[which]
        if half is None:
            out_ref[which] = product
        else:
            out_ref[...] = product.astype(out_ref.dtype)


def gradient(k, position, lefts, mine, total, half=None):
    rows, nodes = lefts.shape[3:]
    part = mine.shape[2]
    kept = [] if total is None else [held(total)]
    if half is None:
        count, out_shape = 2, pltpu.VMEM((2, rows, part), jnp.float32)
    else:
        count = 1
        out_shape = pltpu.VMEM((rows, part), jnp.bfloat16 if half else jnp.float32)
    return pl.pallas_call(
        functools.partial(gradient_kernel, k, total is None, half),
        in_specs=[pl.BlockSpec(memory_space=pltpu.SMEM), ANYWHERE] + [IN_VMEM] * (1 + len(kept)),
        out_specs=IN_VMEM,
        out_shape=out_shape,
        scratch_shapes=[
            pltpu.VMEM((count, 4, rows, nodes), jnp.bfloat16),
            pltpu.SemaphoreType.DMA((2, 4)),
        ],
        input_output_aliases={3: 0} if half is None and kept else {},
        compiler_params=pltpu.CompilerParams(
            vmem_limit_bytes=(14 if half is None else 11) * 1024 * 1024),
        cost_estimate=pl.CostEstimate(flops=count * 8 * rows * part * nodes,
                                      bytes_accessed=count * (8 * rows * nodes + 8 * rows * part),
                                      transcendentals=0),
        name="gradient",
    )(position, in_hbm(lefts), held(mine), *kept)


def combine_kernel(half, pos_ref, own_ref, other_ref, *refs):
    outs = refs[-4:]
    y, z = pos_ref[1], pos_ref[2]
    block = outs[0].shape[0]
    for d in range(4):
        q = lax.rem(z + half, 2) * 4 + lax.rem(y + d, 4)
        at = pl.ds(pl.multiple_of(q * block, block), block)
        both = own_ref[at, :] + other_ref[at, :].astype(jnp.float32)
        outs[d][...] = both.astype(jnp.bfloat16)


def combine(half, position, own, other, earlier=()):
    rows, part = own.shape
    return pl.pallas_call(
        functools.partial(combine_kernel, half),
        in_specs=[pl.BlockSpec(memory_space=pltpu.SMEM)] + [IN_VMEM] * 2 + [ANYWHERE] * len(earlier),
        out_specs=[IN_VMEM] * 4,
        out_shape=[pltpu.VMEM((rows // 8, part), jnp.bfloat16)] * 4,
        compiler_params=pltpu.CompilerParams(vmem_limit_bytes=11 * 1024 * 1024),
        cost_estimate=pl.CostEstimate(flops=rows * part, bytes_accessed=4 * rows * part,
                                      transcendentals=0),
        name="combine",
    )(position, held(own), held(other), *earlier)


def assemble_kernel(pos_ref, *refs):
    out_ref = refs[-1]
    part = refs[0].shape[1]
    for d in range(4):
        q = lax.rem(pos_ref[1] + 4 - d, 4)
        both = refs[d][...].astype(jnp.float32) + refs[4 + d][...].astype(jnp.float32)
        out_ref[:, pl.ds(pl.multiple_of(q * part, part), part)] = both.astype(jnp.bfloat16)


def assemble(position, parts):
    rows, part = parts[0].shape
    return pl.pallas_call(
        assemble_kernel,
        in_specs=[pl.BlockSpec(memory_space=pltpu.SMEM)] + [IN_VMEM] * 8,
        out_specs=IN_VMEM,
        out_shape=jax.ShapeDtypeStruct((rows, 4 * part), parts[0].dtype),
        compiler_params=pltpu.CompilerParams(vmem_limit_bytes=14 * 1024 * 1024),
        name="assemble",
    )(position, *[held(x) for x in parts])


def by_y(x, d):
    return lax.ppermute(x, "dp", [(i, (i + 4 * d) % 16) for i in range(16)])


def by_y_and_z(x, d):
    return lax.ppermute(x, "dp", [(i, (i + 4 * d) % 16 ^ 2) for i in range(16)])


def by_core(x):
    return lax.ppermute(x, "dp", [(i, i ^ 1) for i in range(16)])


def tied(values, after):
    *values, after = lax.optimization_barrier((*values, after))
    return values, after


def tied_list(values, others):
    both = lax.optimization_barrier((*values, *others))
    return both[:len(values)], list(both[len(values):])


def local(section_inputs, weights, norm_gains, upstream, edge_list, time_steps):
    section = lax.axis_index("pipe")
    sections = lax.axis_size("pipe")
    replica = lax.axis_index("dp")
    micros = section_inputs.shape[1]
    nodes = section_inputs.shape[2]
    width = section_inputs.shape[3]
    hidden = section_inputs[0]
    gates = timestep_gate(time_steps[:, 0], width)
    edges_t = jnp.swapaxes(edge_list[:, 0], 1, 2)
    position = jnp.stack([section, replica // 4, (replica // 2) % 2, replica % 2]).astype(jnp.int32)
    *state, wt, turned, grads, act = first(hidden, edges_t, gates, norm_gains, weights[0])

    def rest(turn, state):
        return second(turn, position, hidden, edges_t, gates, norm_gains, wt, turned,
                      state[:2], *state[2:])

    state = rest(1, state)
    slope, mixt, inv = state[2:]

    def to_y(parts):
        return [parts[0]] + [by_y(parts[d], d) for d in range(1, 4)]

    received = None
    near = []
    ticks = sections + micros - 1
    for t in range(ticks):
        if t == ticks - 1:
            near.append(to_y(last_act(position, received, slope, act)))
        sent, grads, act, *carried = tick(
            t, sections, position, received, upstream, slope, mixt, hidden, inv, norm_gains, wt,
            grads, act, [whole] if t == 1 else [])
        if t == ticks - 1:
            break
        pairs = [(s, s - 1) for s in range(1, sections)
                 if 0 <= t - (sections - 1 - s) < micros]
        received = lax.ppermute(sent, "pipe", pairs)
        if t == 0:
            state = rest(0, state)
            whole, saved, slope, mixt, inv = state
        if t == 1:
            lefts = lax.all_gather(carried[0], "dp", axis_index_groups=Y_GROUPS)
            wt = reload(saved, carried[0])
        if t in (7, 8):
            mine = stack(to_y(pick(t - 7, act)))
            if t == 7:
                (mine,), received = tied((mine,), received)
            near.append(mine)
        if t == 8:
            total = gradient(0, position, lefts, near[0], None)
            (total, mine), received = tied((total, near[1]), received)
            near[1] = mine

    total = gradient(1, position, lefts, near[1], total)
    (total,), parts_last = tied_list((total,), near[2])
    mine = stack(parts_last)
    other = by_core(gradient(micros - 1, position, lefts, mine, total, 1))
    own = gradient(micros - 1, position, lefts, mine, total, 0)
    distant = combine(1, position, own, other)
    parts = [by_y_and_z(distant[d], d) for d in range(4)]
    rows = assemble(position, to_y(combine(0, position, own, other, distant[3:])) + parts)
    return (grads[None], rows[None])


def solution(mesh):
    in_specs = (
        P("pipe", None, "dp", None),
        P("pipe", None, None),
        P("pipe", None),
        P(None, "dp", None),
        P(None, "dp", None, None),
        P(None, "dp"),
    )
    out_specs = (P("pipe", None, "dp", None), P("pipe", "dp", None))
    return jax.shard_map(local, mesh=mesh, in_specs=in_specs, out_specs=out_specs, check_vma=False)
```
